512 devices in a mesh: lat: 64 (over z, y), batch: 8 (over x, core).
Axes of the slice: x: 4, y: 8, z: 8, core: 2. Of those that a mesh axis runs over, the one named last changes fastest.
Arguments:
- fields: bfloat16 [8, 192, 384, 384], P('batch', 'lat'), may hold values from -6 to 6
- cotangent: bfloat16 [8, 192, 384, 384], P('batch', 'lat'), may hold values from -6 to 6
- weights: bfloat16 [128, 2, 384, 384], P('lat'), may hold values from -0.21875 to 0.21875
- degree_of: int32 [128], replicated, may hold values from 0 to 127, each once
Outputs:
- grad_fields: bfloat16 [8, 192, 384, 384], P('batch', 'lat')
- grad_weights: bfloat16 [128, 2, 384, 384], P('lat')
The draws below stay inside these ranges and needn't reach their ends.
Inputs may be any that keep to these rules, and one draw needn't show every extreme that they name: `degree_of`: each degree 0 to 127 is held by exactly one slot.
All inputs are finite; a program needn't handle non-finite values.
Results may differ from the reference program's by a relative error of at most 0.018.
Values may be sent and summed in bfloat16 or wider, within the bound.
No kernel may reach another device: no remote copies, remote signals or barrier semaphores. Data moves between devices by JAX's collectives and lax.ppermute only.
A program may use at most 64 MiB of HBM per device.

```python
import jax
import jax.numpy as jnp
from jax import lax

LATS = 192
LONS = 384
ORDERS = 128
DEGREES = 128
CHANNELS = 384
BATCH = 8


def shard_levels(key, extent, split, least, largest):
    loudness = 1.0
    for axis_at, blocks in split:
        draws = jax.random.uniform(jax.random.fold_in(jax.random.fold_in(key, 6), axis_at), (blocks,), jnp.float32, least / len(split), largest / len(split))
        loudness = loudness * jnp.repeat(jnp.exp(draws), extent[axis_at] // blocks).reshape((-1,) + (1,) * (len(extent) - 1 - axis_at))
    return loudness


def normal_values(own_key, dims, spread, limit, split=(), held_as=jnp.bfloat16):
    values = spread * jax.random.normal(own_key, dims, jnp.float32)
    if split:
        values = values * shard_levels(own_key, dims, split, -0.22, 0.18)
    return jnp.clip(values, -limit, limit).astype(held_as)


def setup_inputs(seed: int = 0) -> dict:
    keys = jax.random.split(jax.random.key(seed), 5)
    return {
        "fields": normal_values(keys[0], (BATCH, LATS, LONS, CHANNELS), 1.0, 6.0, ((0, 8), (1, 64))),
        "cotangent": normal_values(keys[1], (BATCH, LATS, LONS, CHANNELS), 1.0, 6.0, ((0, 8), (1, 64))),
        "weights": normal_values(keys[2], (DEGREES, 2, CHANNELS, CHANNELS), (2 * CHANNELS) ** -0.5, 0.21875, ((0, 64),)),
        "degree_of": jax.random.permutation(keys[3], DEGREES).astype(jnp.int32),
    }


def legendre_table(order_ids, lat_count, degree_count):
    colatitude = jnp.pi * (jnp.arange(lat_count, dtype=jnp.float32) + 0.5) / lat_count
    cosine = jnp.cos(colatitude)[None, :]
    log_sine = jnp.log(jnp.sin(colatitude))[None, :]
    order_col = order_ids.astype(jnp.int32)[:, None]
    order_real = order_col.astype(jnp.float32)
    steps_up = jnp.arange(1, degree_count + 1, dtype=jnp.float32)[None, :]
    factor = jnp.where(steps_up <= order_real, 0.5 * jnp.log((2.0 * steps_up + 1.0) / (2.0 * steps_up)), 0.0)
    log_start = 0.5 * jnp.log(1.0 / (4.0 * jnp.pi)) + lax.optimization_barrier(jnp.sum(factor, axis=1, keepdims=True))
    diagonal = jnp.exp(log_start + order_real * log_sine)
    squared = order_real * order_real

    def advance(carry, degree):
        previous, older = carry
        degree_real = degree.astype(jnp.float32)
        lead = jnp.sqrt(jnp.maximum(4.0 * degree_real * degree_real - 1.0, 0.0) / jnp.maximum(degree_real * degree_real - squared, 1.0))
        lower = degree_real - 1.0
        back = jnp.sqrt(jnp.maximum(lower * lower - squared, 0.0) / jnp.maximum(4.0 * lower * lower - 1.0, 1.0))
        general = lead * (cosine * previous - back * older)
        first = jnp.sqrt(2.0 * order_real + 3.0) * cosine * previous
        value = jnp.where(degree == order_col, diagonal, jnp.where(degree == order_col + 1, first, jnp.where(degree > order_col + 1, general, 0.0)))
        return ((value, previous), value)
    zeros = jnp.zeros((order_ids.shape[0], lat_count), jnp.float32)
    final_state, table = lax.scan(advance, (zeros, zeros), jnp.arange(degree_count, dtype=jnp.int32))
    return jnp.transpose(table, (1, 0, 2))

def spectral_tables(order_ids, degree_of, lat_count, degree_count):
    table = legendre_table(order_ids, lat_count, degree_count)
    chosen = jnp.take(table, degree_of.astype(jnp.int32), axis=1)
    colatitude = jnp.pi * (jnp.arange(lat_count, dtype=jnp.float32) + 0.5) / lat_count
    quadrature = 2.0 * jnp.pi * jnp.pi / lat_count * jnp.sin(colatitude)
    return ((chosen * quadrature[None, None, :]).astype(jnp.bfloat16), chosen.astype(jnp.bfloat16))

def fourier_tables(lon_count, order_count):
    lon_ids = jnp.arange(lon_count, dtype=jnp.int32)[:, None]
    order_ids = jnp.arange(order_count, dtype=jnp.int32)[None, :]
    phase = 2.0 * jnp.pi * (lon_ids * order_ids % lon_count).astype(jnp.float32) / lon_count
    forward = jnp.stack([jnp.cos(phase), -jnp.sin(phase)], axis=2).reshape(lon_count, 2 * order_count) / lon_count
    doubled = jnp.where(order_ids == 0, 1.0, 2.0)
    inverse = jnp.stack([doubled * jnp.cos(phase), -doubled * jnp.sin(phase)], axis=2).reshape(lon_count, 2 * order_count)
    return (forward.astype(jnp.bfloat16), jnp.transpose(inverse).astype(jnp.bfloat16))

def as_real(values):
    return values.astype(jnp.float32)

def sample_pass(field, cotangent, weights, forward, inverse, qslot, pslot):
    w_real = as_real(weights[:, 0])
    w_imag = as_real(weights[:, 1])
    spectra = jnp.einsum('ikc,kf->ifc', as_real(field), as_real(forward)).astype(jnp.bfloat16)
    spectra = spectra.reshape(LATS, ORDERS, 2, CHANNELS)
    coeffs = jnp.einsum('mji,imrc->jmrc', as_real(qslot), as_real(spectra)).astype(jnp.bfloat16)
    c_real = as_real(coeffs[:, :, 0])
    c_imag = as_real(coeffs[:, :, 1])
    f_real = jnp.einsum('jmc,jcd->jmd', c_real, w_real) - jnp.einsum('jmc,jcd->jmd', c_imag, w_imag)
    f_imag = jnp.einsum('jmc,jcd->jmd', c_real, w_imag) + jnp.einsum('jmc,jcd->jmd', c_imag, w_real)
    filtered = jnp.stack([f_real, f_imag], axis=2).astype(jnp.bfloat16)
    synth = jnp.einsum('mji,jmrc->imrc', as_real(pslot), as_real(filtered)).astype(jnp.bfloat16)
    response = jnp.einsum('ifc,fk->ikc', as_real(synth.reshape(LATS, 2 * ORDERS, CHANNELS)), as_real(inverse))
    activated, pullback = jax.vjp(jax.nn.gelu, response)
    upstream = pullback(as_real(cotangent))[0].astype(jnp.bfloat16)
    grad_synth = jnp.einsum('ikc,fk->ifc', as_real(upstream), as_real(inverse)).astype(jnp.bfloat16)
    grad_synth = grad_synth.reshape(LATS, ORDERS, 2, CHANNELS)
    grad_filtered = jnp.einsum('mji,imrc->jmrc', as_real(pslot), as_real(grad_synth)).astype(jnp.bfloat16)
    g_real = as_real(grad_filtered[:, :, 0])
    g_imag = as_real(grad_filtered[:, :, 1])
    dw_real = jnp.einsum('jmc,jmd->jcd', c_real, g_real) + jnp.einsum('jmc,jmd->jcd', c_imag, g_imag)
    dw_imag = jnp.einsum('jmc,jmd->jcd', c_real, g_imag) - jnp.einsum('jmc,jmd->jcd', c_imag, g_real)
    a_real = jnp.einsum('jmd,jcd->jmc', g_real, w_real) + jnp.einsum('jmd,jcd->jmc', g_imag, w_imag)
    a_imag = jnp.einsum('jmd,jcd->jmc', g_imag, w_real) - jnp.einsum('jmd,jcd->jmc', g_real, w_imag)
    grad_coeffs = jnp.stack([a_real, a_imag], axis=2).astype(jnp.bfloat16)
    grad_spectra = jnp.einsum('mji,jmrc->imrc', as_real(qslot), as_real(grad_coeffs)).astype(jnp.bfloat16)
    delta = jnp.einsum('ifc,kf->ikc', as_real(grad_spectra.reshape(LATS, 2 * ORDERS, CHANNELS)), as_real(forward))
    grad_field = (as_real(cotangent) + delta).astype(jnp.bfloat16)
    return (grad_field, jnp.stack([dw_real, dw_imag], axis=1))

def reference(fields, cotangent, weights, degree_of):
    forward, inverse = fourier_tables(LONS, ORDERS)
    qslot, pslot = spectral_tables(jnp.arange(ORDERS, dtype=jnp.int32), degree_of, LATS, DEGREES)

    def one_sample(total, pair):
        grad_field, weight_part = sample_pass(pair[0], pair[1], weights, forward, inverse, qslot, pslot)
        return (total + weight_part, grad_field)
    start = jnp.zeros((DEGREES, 2, CHANNELS, CHANNELS), jnp.float32)
    total, grad_fields = lax.scan(one_sample, start, (fields, cotangent))
    return (grad_fields, total.astype(jnp.bfloat16))
```

```python
import jax
import jax.numpy as jnp
import numpy as np
from jax import lax
from jax.sharding import PartitionSpec as P

LATS = 192
LONS = 384
ORDERS = 128
DEGREES = 128
CHANNELS = 384


def in_one_piece(arrays, axis, dim, along):
    widths = [a.shape[along] for a in arrays]
    both = jnp.concatenate(arrays, axis=along)
    out = lax.all_gather(both, axis, axis=dim, tiled=True)
    return tuple(jnp.split(out, [sum(widths[:k]) for k in range(1, len(widths))], axis=along))


def legendre_table():
    colatitude = np.pi * (np.arange(LATS) + 0.5) / LATS
    cosine, sine = np.cos(colatitude), np.sin(colatitude)
    order = np.arange(ORDERS, dtype=np.float64)[:, None]
    steps = np.arange(1, ORDERS)
    growth = np.concatenate([[0.0], np.cumsum(0.5 * np.log((2.0 * steps + 1.0) / (2.0 * steps)))])
    diagonal = np.exp(0.5 * np.log(1.0 / (4.0 * np.pi)) + growth[:, None] + order * np.log(sine))
    table = np.zeros((ORDERS, DEGREES, LATS))
    for degree in range(DEGREES):
        table[degree, degree] = diagonal[degree]
        if degree >= 1:
            m = degree - 1
            table[m, degree] = np.sqrt(2.0 * m + 3.0) * cosine * table[m, m]
        if degree >= 2:
            m = order[: degree - 1]
            lead = np.sqrt((4.0 * degree**2 - 1.0) / (degree**2 - m**2))
            back = np.sqrt(((degree - 1.0) ** 2 - m**2) / (4.0 * (degree - 1.0) ** 2 - 1.0))
            table[: degree - 1, degree] = lead * (
                cosine * table[: degree - 1, degree - 1] - back * table[: degree - 1, degree - 2]
            )
    return table, 2.0 * np.pi * np.pi / LATS * sine


def spectral_tables(start, ord_dev, degree_of):
    table, quadrature = legendre_table()
    both = jnp.asarray(np.stack([table * quadrature, table], axis=1).astype(jnp.bfloat16))
    mine = lax.dynamic_slice_in_dim(both, start, ord_dev, 0)
    selector = (degree_of[:, None] == jnp.arange(DEGREES, dtype=jnp.int32)[None, :]).astype(
        jnp.bfloat16
    )
    chosen = jnp.einsum(
        "mpli,jl->pmji", mine, selector, preferred_element_type=jnp.float32
    ).astype(jnp.bfloat16)
    return (chosen[0], chosen[1])


def fourier_tables(lon_count, order_count):
    lon_ids = jnp.arange(lon_count, dtype=jnp.int32)[:, None]
    order_ids = jnp.arange(order_count, dtype=jnp.int32)[None, :]
    phase = 2.0 * jnp.pi * (lon_ids * order_ids % lon_count).astype(jnp.float32) / lon_count
    forward = (
        jnp.stack([jnp.cos(phase), -jnp.sin(phase)], axis=2).reshape(lon_count, 2 * order_count)
        / lon_count
    )
    doubled = jnp.where(order_ids == 0, 1.0, 2.0)
    inverse = jnp.stack([doubled * jnp.cos(phase), -doubled * jnp.sin(phase)], axis=2).reshape(
        lon_count, 2 * order_count
    )
    return (forward.astype(jnp.bfloat16), jnp.transpose(inverse).astype(jnp.bfloat16))


def to_orders(values):
    return lax.all_to_all(values, "lat", split_axis=1, concat_axis=0, tiled=True)


def to_degrees(values):
    return lax.all_to_all(values, "lat", split_axis=0, concat_axis=1, tiled=True)


def back_to_orders(values):
    return lax.all_to_all(values, "lat", split_axis=1, concat_axis=0, tiled=True)


def to_bands(values):
    return lax.all_to_all(values, "lat", split_axis=0, concat_axis=1, tiled=True)


def product(spec, left, right):
    return jnp.einsum(spec, left, right, preferred_element_type=jnp.float32)


def apply_filter(coeffs, weights):
    c_real = coeffs[:, :, 0]
    c_imag = coeffs[:, :, 1]
    w_real = weights[:, 0]
    w_imag = weights[:, 1]
    f_real = product("jmsc,jcd->jmsd", c_real, w_real) - product("jmsc,jcd->jmsd", c_imag, w_imag)
    f_imag = product("jmsc,jcd->jmsd", c_real, w_imag) + product("jmsc,jcd->jmsd", c_imag, w_real)
    return jnp.stack([f_real, f_imag], axis=2).astype(jnp.bfloat16)


def adjoint_filter(grads, weights):
    g_real = grads[:, :, 0]
    g_imag = grads[:, :, 1]
    w_real = weights[:, 0]
    w_imag = weights[:, 1]
    a_real = product("jmsd,jcd->jmsc", g_real, w_real) + product("jmsd,jcd->jmsc", g_imag, w_imag)
    a_imag = product("jmsd,jcd->jmsc", g_imag, w_real) - product("jmsd,jcd->jmsc", g_real, w_imag)
    return jnp.stack([a_real, a_imag], axis=2).astype(jnp.bfloat16)


def filter_grad(coeffs, grads):
    c_real = coeffs[:, :, 0]
    c_imag = coeffs[:, :, 1]
    g_real = grads[:, :, 0]
    g_imag = grads[:, :, 1]
    dw_real = product("jmsc,jmsd->jcd", c_real, g_real) + product("jmsc,jmsd->jcd", c_imag, g_imag)
    dw_imag = product("jmsc,jmsd->jcd", c_real, g_imag) - product("jmsc,jmsd->jcd", c_imag, g_real)
    return jnp.stack([dw_real, dw_imag], axis=1)


def local(fields, cotangent, weights, degree_of):
    samples = fields.shape[0]
    band_rows = fields.shape[1]
    ord_dev = ORDERS // lax.axis_size("lat")
    forward, inverse = fourier_tables(LONS, ORDERS)
    qslot, pslot = spectral_tables(lax.axis_index("lat") * ord_dev, ord_dev, degree_of)
    spectra = product("sikc,kf->ifsc", fields, forward).astype(jnp.bfloat16)
    spectra = spectra.reshape(band_rows, ORDERS, 2, samples, CHANNELS)
    gathered = to_orders(spectra)
    coeffs_local = product("mji,imrsc->jmrsc", qslot, gathered).astype(jnp.bfloat16)
    coeffs = to_degrees(coeffs_local)
    filtered = apply_filter(coeffs, weights)
    returned = back_to_orders(filtered)
    synth_local = product("mji,jmrsc->imrsc", pslot, returned).astype(jnp.bfloat16)
    synth = to_bands(synth_local)
    response = product(
        "ifsc,fk->sikc", synth.reshape(band_rows, 2 * ORDERS, samples, CHANNELS), inverse
    )
    activated, pullback = jax.vjp(jax.nn.gelu, response)
    upstream = pullback(cotangent.astype(jnp.float32))[0].astype(jnp.bfloat16)
    grad_synth = product("sikc,fk->ifsc", upstream, inverse).astype(jnp.bfloat16)
    grad_synth = grad_synth.reshape(band_rows, ORDERS, 2, samples, CHANNELS)
    grad_gathered = to_orders(grad_synth)
    grad_local = product("mji,imrsc->jmrsc", pslot, grad_gathered).astype(jnp.bfloat16)
    grad_filtered = to_degrees(grad_local)
    all_coeffs, all_grads = in_one_piece((coeffs, grad_filtered), "batch", 3, 0)
    weight_total = filter_grad(all_coeffs, all_grads)
    grad_coeffs = adjoint_filter(grad_filtered, weights)
    grad_back = back_to_orders(grad_coeffs)
    grad_local_spec = product("mji,jmrsc->imrsc", qslot, grad_back).astype(jnp.bfloat16)
    grad_bands = to_bands(grad_local_spec)
    delta = product(
        "ifsc,kf->sikc", grad_bands.reshape(band_rows, 2 * ORDERS, samples, CHANNELS), forward
    )
    grad_fields = (cotangent.astype(jnp.float32) + delta).astype(jnp.bfloat16)
    return (grad_fields, weight_total.astype(jnp.bfloat16))


def solution(mesh):
    return jax.shard_map(
        local,
        mesh=mesh,
        in_specs=(
            P("batch", "lat", None, None),
            P("batch", "lat", None, None),
            P("lat", None, None, None),
            P(),
        ),
        out_specs=(P("batch", "lat", None, None), P("lat", None, None, None)),
        check_vma=False,
    )
```

```python
import functools

import jax
import jax.numpy as jnp
import numpy as np
from jax import lax
from jax.experimental import pallas as pl
from jax.experimental.pallas import tpu as pltpu
from jax.sharding import PartitionSpec as P

LATS = 192
LONS = 384
ORDERS = 128
DEGREES = 128
CHANNELS = 384

GROUPS = 64
BAND = LATS // GROUPS
PARTS = CHANNELS // GROUPS
SLOTS = DEGREES // GROUPS
COEFS = 2 * ORDERS
BLOCKS = ORDERS // 16
SPEC_ROWS = BAND * PARTS * 2
FIRST_ROWS = 96
SLOT_ROWS = SLOTS * PARTS * 2
LAST_ROWS = 40
REACH = [DEGREES - 16 * t for t in range(BLOCKS)]
STARTS = [16 * sum(REACH[:t]) for t in range(BLOCKS + 1)]
PAIR_ROWS = 8 * LATS

f32 = jnp.float32
bf16 = jnp.bfloat16
TN = (((0,), (0,)), ((), ()))
NN = (((1,), (0,)), ((), ()))
NT = (((1,), (1,)), ((), ()))


def legendre_table():
    colatitude = np.pi * (np.arange(LATS) + 0.5) / LATS
    cosine, sine = np.cos(colatitude), np.sin(colatitude)
    order = np.arange(ORDERS, dtype=np.float64)[:, None]
    steps = np.arange(1, ORDERS)
    growth = np.concatenate([[0.0], np.cumsum(0.5 * np.log((2.0 * steps + 1.0) / (2.0 * steps)))])
    diagonal = np.exp(0.5 * np.log(1.0 / (4.0 * np.pi)) + growth[:, None] + order * np.log(sine))
    table = np.zeros((ORDERS, DEGREES, LATS))
    for degree in range(DEGREES):
        table[degree, degree] = diagonal[degree]
        if degree >= 1:
            m = degree - 1
            table[m, degree] = np.sqrt(2.0 * m + 3.0) * cosine * table[m, m]
        if degree >= 2:
            m = order[: degree - 1]
            lead = np.sqrt((4.0 * degree**2 - 1.0) / (degree**2 - m**2))
            back = np.sqrt(((degree - 1.0) ** 2 - m**2) / (4.0 * (degree - 1.0) ** 2 - 1.0))
            table[: degree - 1, degree] = lead * (
                cosine * table[: degree - 1, degree - 1] - back * table[: degree - 1, degree - 2]
            )
    return table, 2.0 * np.pi * np.pi / LATS * sine


def fourier_tables():
    lon = np.arange(LONS)[:, None]
    order = np.arange(ORDERS)[None, :]
    phase = 2.0 * np.pi * (lon * order % LONS) / LONS
    forward = np.stack([np.cos(phase), -np.sin(phase)], axis=2).reshape(LONS, COEFS) / LONS
    doubled = np.where(order == 0, 1.0, 2.0)
    inverse = np.stack([doubled * np.cos(phase), -doubled * np.sin(phase)], axis=2)
    return forward.astype(bf16), inverse.reshape(LONS, COEFS).astype(bf16)


@functools.cache
def constants():
    table, quadrature = legendre_table()
    where = np.arange(LATS).reshape(GROUPS, BAND).T.reshape(-1)
    table = table[:, :, where].astype(bf16)
    analysis = np.concatenate(
        [table[16 * t + k, 16 * t :] for t in range(BLOCKS) for k in range(16)], axis=0
    )
    synthesis = np.concatenate(
        [
            np.concatenate([table[16 * t + k].T, table[16 * t + k + 8].T], axis=1)
            for t in range(BLOCKS)
            for k in range(8)
        ],
        axis=0,
    )
    forward, inverse = fourier_tables()
    turn = np.zeros((COEFS, COEFS), np.float32)
    even = np.arange(0, COEFS, 2)
    turn[even + 1, even] = -1.0
    turn[even, even + 1] = 1.0
    return dict(
        analysis=analysis,
        synthesis=synthesis,
        forward=forward,
        inverse=inverse,
        inverse_t=np.ascontiguousarray(inverse.T),
        turn=turn.astype(bf16),
        weight=quadrature.astype(np.float32),
        weight_rows=quadrature[where].astype(np.float32)[:, None],
    )


def dot(left, right, dims=NN):
    return lax.dot_general(left, right, dims, preferred_element_type=f32)


def lane_of(shape):
    return lax.broadcasted_iota(jnp.int32, shape, 1)


def join(pieces, lanes):
    rolled = [pltpu.roll(x, s % 128, 1) if s % 128 else x for x, s in pieces]
    left = jnp.where(lanes < 32, rolled[0], rolled[1])
    right = jnp.where(lanes < 96, rolled[2], rolled[3])
    return jnp.where(lanes < 64, left, right)


def join_two(first, shift_first, second, shift_second, lanes):
    a = pltpu.roll(first, shift_first % 128, 1) if shift_first % 128 else first
    b = pltpu.roll(second, shift_second % 128, 1) if shift_second % 128 else second
    return jnp.where(lanes < 64, a, b)


def to_tiles(parts):
    lanes = lane_of(parts[0][0].shape)
    tiles = []
    for pair in range(BLOCKS // 2):
        h, at = pair // 2, 64 * (pair % 2)
        x = [parts[q][h] for q in range(PARTS)]
        a = join([(x[s], 32 * s - at) for s in range(4)], lanes)
        c = join([(x[s], 32 * s - at - 32) for s in range(4)], lanes)
        b = join_two(x[4], -at, x[5], 64 - at, lanes)
        tiles.append((a, b, c))
    return tiles


def from_tiles(tiles):
    lanes = lane_of(tiles[0][0].shape)
    parts = []
    for q in range(4):
        halves = []
        for h in range(2):
            pieces = []
            for k in range(4):
                a, _, c = tiles[2 * h + k // 2]
                pieces.append((c if k % 2 else a, 32 * (k - q)))
            halves.append(join(pieces, lanes))
        parts.append(halves)
    parts.append([join_two(tiles[2 * h][1], 0, tiles[2 * h + 1][1], 64, lanes) for h in range(2)])
    parts.append([join_two(tiles[2 * h][1], 64, tiles[2 * h + 1][1], 0, lanes) for h in range(2)])
    return parts


def as_bf16(tiles):
    return [tuple(x.astype(bf16) for x in tile) for tile in tiles]


def block_operand(tiles, t):
    a, b, c = tiles[t // 2]
    return jnp.concatenate([c if t % 2 else a, b], axis=1)


def merge_blocks(sums):
    tiles = []
    for pair in range(BLOCKS // 2):
        one, two = sums[2 * pair], sums[2 * pair + 1]
        lanes = lane_of((one.shape[0], 128))
        b = jnp.where((lanes // 32) % 2 == 0, one[:, 128:], two[:, 128:])
        tiles.append((one[:, :128], b, two[:, :128]))
    return tiles


def analyse(tiles, table, ready, rows_each=4):
    sums = []
    for t in range(BLOCKS):
        ready(t)
        operand = block_operand(tiles, t)
        reach = REACH[t]
        order = (lane_of((reach, 256)) % 32) // 2
        total = jnp.zeros((reach, 256), f32)
        for k in range(0, 16, rows_each):
            part = dot(table[pl.ds(STARTS[t] + k * reach, rows_each * reach), :], operand)
            for n in range(rows_each):
                total = jnp.where(order == k + n, part[n * reach : (n + 1) * reach], total)
        if t:
            total = jnp.concatenate([jnp.zeros((16 * t, 256), f32), total], axis=0)
        sums.append(total)
    return merge_blocks(sums)


def synthesise(tiles, table, ready, rows_each=2):
    sums = []
    for t in range(BLOCKS):
        ready(t)
        operand = block_operand(tiles, t)
        low = (lane_of((DEGREES, 256)) % 32) < 16
        none = jnp.zeros_like(operand)
        stacked = jnp.concatenate(
            [jnp.where(low, operand, none), jnp.where(low, none, operand)], axis=0
        )
        order = (lane_of((LATS, 256)) % 16) // 2
        total = jnp.zeros((LATS, 256), f32)
        for k in range(0, 8, rows_each):
            part = dot(table[pl.ds(t * PAIR_ROWS + k * LATS, rows_each * LATS), :], stacked)
            for n in range(rows_each):
                total = jnp.where(order == k + n, part[n * LATS : (n + 1) * LATS], total)
        sums.append(total)
    return merge_blocks(sums)


def permute_rows(matrix, tiles):
    out = []
    for tile in tiles:
        moved = dot(matrix, jnp.concatenate(tile, axis=1))
        out.append(tuple(moved[:, 128 * n : 128 * (n + 1)] for n in range(3)))
    return out


def slot_rows_out(tiles, degree_col, stage, out):
    pick = (degree_col[...] == lane_of((DEGREES, DEGREES))).astype(f32).astype(bf16)
    parts = from_tiles(permute_rows(pick, as_bf16(tiles)))
    for j in range(SLOTS):
        for q in range(PARTS):
            for h in range(2):
                stage[pl.ds((j * PARTS + q) * 2 + h, GROUPS, stride=SLOT_ROWS), :] = parts[q][h][
                    j * GROUPS : (j + 1) * GROUPS
                ]
    out[...] = stage[...].astype(bf16)


def slot_rows_in(received, degree_row, stage):
    stage[...] = received[...].astype(f32)
    parts = [
        [
            jnp.concatenate(
                [
                    stage[pl.ds((j * PARTS + q) * 2 + h, GROUPS, stride=SLOT_ROWS), :]
                    for j in range(SLOTS)
                ],
                axis=0,
            )
            for h in range(2)
        ]
        for q in range(PARTS)
    ]
    rows = lax.broadcasted_iota(jnp.int32, (DEGREES, DEGREES), 0)
    pick = (rows == degree_row[...]).astype(f32).astype(bf16)
    return as_bf16(permute_rows(pick, as_bf16(to_tiles(parts))))


def table_copies(source, target, sems, bounds):
    copies = []
    for t in range(BLOCKS):
        rows = pl.ds(bounds[t], bounds[t + 1] - bounds[t])
        copies.append(pltpu.make_async_copy(source.at[rows, :], target.at[rows, :], sems.at[t]))
    return copies


PAIR_STARTS = [PAIR_ROWS * t for t in range(BLOCKS + 1)]


def spread_kernel(fields, cotangent, forward, scale, out, stage):
    for i in range(BAND):
        spectra = dot(fields[i], forward[...], TN) * scale[i]
        turned = jnp.transpose(cotangent[i].astype(f32))
        for q in range(PARTS):
            rows = slice(q * GROUPS, (q + 1) * GROUPS)
            at = (i * PARTS + q) * 2
            for h in range(2):
                stage[pl.ds(at + h, GROUPS, stride=FIRST_ROWS), :] = spectra[
                    rows, 128 * h : 128 * (h + 1)
                ]
            at = SPEC_ROWS + (i * PARTS + q) * 3
            for h in range(3):
                stage[pl.ds(at + h, GROUPS, stride=FIRST_ROWS), :] = turned[
                    rows, 128 * h : 128 * (h + 1)
                ]
    for row in range(SPEC_ROWS + BAND * PARTS * 3, FIRST_ROWS):
        stage[pl.ds(row, GROUPS, stride=FIRST_ROWS), :] = jnp.zeros((GROUPS, 128), f32)
    out[...] = stage[...].astype(bf16)


def first_kernel(received, analysis, degree_col, out, rows, stage_in, stage, table, row_sem, sems):
    copies = table_copies(analysis, table, sems, STARTS)
    fetch = pltpu.make_async_copy(received.at[:, pl.ds(0, 48), :], rows, row_sem)
    fetch.start()
    for copy in copies:
        copy.start()
    fetch.wait()
    stage_in[...] = rows[...].astype(f32).reshape(GROUPS * 48, 128)
    parts = [
        [
            jnp.concatenate(
                [
                    stage_in[pl.ds((i * PARTS + q) * 2 + h, GROUPS, stride=48), :]
                    for i in range(BAND)
                ],
                axis=0,
            )
            for h in range(2)
        ]
        for q in range(PARTS)
    ]
    tiles = as_bf16(to_tiles(parts))
    sums = analyse(tiles, table, lambda t: copies[t].wait())
    slot_rows_out(sums, degree_col, stage, out)


def gelu_slope(x):
    c = np.float32(np.sqrt(2.0 / np.pi))
    squared = x * x
    th = jnp.tanh(c * (x + 0.044715 * (x * squared)))
    return 0.5 * (1.0 + th) + (0.5 * c) * x * (1.0 - th * th) * (1.0 + (3 * 0.044715) * squared)


def middle_kernel(
    received, cotangents, analysis, synthesis, degree_row, degree_col, inverse, inverse_t, out,
    rows, stage_in, stage, table, table_s, row_sem, sems, sems_s,
):
    copies_s = table_copies(synthesis, table_s, sems_s, PAIR_STARTS)
    copies = table_copies(analysis, table, sems, STARTS)
    fetch = pltpu.make_async_copy(cotangents.at[:, pl.ds(32, 64), :], rows, row_sem)
    for copy in copies_s:
        copy.start()
    fetch.start()
    for copy in copies:
        copy.start()
    tiles = slot_rows_in(received, degree_row, stage)
    synth = from_tiles(synthesise(tiles, table_s, lambda t: copies_s[t].wait()))
    fetch.wait()
    stage_in[...] = rows[...].astype(f32).reshape(GROUPS * 64, 128)
    parts = []
    for q in range(PARTS):
        response = dot(jnp.concatenate(synth[q], axis=1).astype(bf16), inverse_t[...])
        cotangent = jnp.concatenate(
            [
                jnp.concatenate(
                    [
                        stage_in[
                            pl.ds(SPEC_ROWS - 32 + (i * PARTS + q) * 3 + h, GROUPS, stride=64), :
                        ]
                        for h in range(3)
                    ],
                    axis=1,
                )
                for i in range(BAND)
            ],
            axis=0,
        )
        upstream = (cotangent * gelu_slope(response)).astype(bf16)
        grad = dot(upstream, inverse[...])
        parts.append([grad[:, :128], grad[:, 128:]])
    sums = analyse(as_bf16(to_tiles(parts)), table, lambda t: copies[t].wait())
    slot_rows_out(sums, degree_col, stage, out)


def last_kernel(received, synthesis, degree_row, weight_rows, out, stage, stage_out, table_s, sems_s):
    copies_s = table_copies(synthesis, table_s, sems_s, PAIR_STARTS)
    for copy in copies_s:
        copy.start()
    tiles = slot_rows_in(received, degree_row, stage)
    synth = from_tiles(synthesise(tiles, table_s, lambda t: copies_s[t].wait()))
    for q in range(PARTS):
        for h in range(2):
            scaled = synth[q][h] * weight_rows[...]
            for i in range(BAND):
                at = (i * PARTS + q) * 2 + h
                stage_out[pl.ds(at, GROUPS, stride=LAST_ROWS), :] = scaled[
                    i * GROUPS : (i + 1) * GROUPS
                ]
    for row in range(SPEC_ROWS, LAST_ROWS):
        stage_out[pl.ds(row, GROUPS, stride=LAST_ROWS), :] = jnp.zeros((GROUPS, 128), f32)
    out[...] = stage_out[...].astype(bf16)


def gather_kernel(received, forward, cotangent, out, stage):
    stage[...] = received[...].astype(f32)
    for i in range(BAND):
        halves = [
            jnp.concatenate(
                [
                    stage[pl.ds((i * PARTS + q) * 2 + h, GROUPS, stride=LAST_ROWS), :]
                    for q in range(PARTS)
                ],
                axis=0,
            )
            for h in range(2)
        ]
        rows = jnp.concatenate(halves, axis=1).astype(bf16)
        delta = dot(forward[...], rows, NT)
        out[i] = (cotangent[i].astype(f32) + delta).astype(bf16)


def mix_kernel(adjoint, received, weights, turn, out, kept, stage):
    stage[...] = received[...].astype(f32)
    results = []
    for j in range(SLOTS):
        halves = [
            jnp.concatenate(
                [
                    stage[pl.ds((j * PARTS + q) * 2 + h, GROUPS, stride=SLOT_ROWS), :]
                    for q in range(PARTS)
                ],
                axis=0,
            )
            for h in range(2)
        ]
        held = jnp.concatenate(halves, axis=1).astype(bf16)
        kept[j] = held
        turned = dot(held, turn[...])
        if adjoint:
            turned = -turned
        turned = turned.astype(bf16)
        results.append(dot(weights[j, 0], held) + dot(weights[j, 1], turned))
    for j in range(SLOTS):
        for q in range(PARTS):
            for h in range(2):
                stage[pl.ds((j * PARTS + q) * 2 + h, GROUPS, stride=SLOT_ROWS), :] = results[j][
                    q * GROUPS : (q + 1) * GROUPS, 128 * h : 128 * (h + 1)
                ]
    out[...] = stage[...].astype(bf16)


VMEM = pl.BlockSpec(memory_space=pltpu.VMEM)
SMEM = pl.BlockSpec(memory_space=pltpu.SMEM)
ANY = pl.BlockSpec(memory_space=pl.ANY)


def call(kernel, out_shape, in_specs, scratch, flops, moved, name):
    several = isinstance(out_shape, list)
    return pl.pallas_call(
        kernel,
        out_shape=out_shape,
        in_specs=in_specs,
        out_specs=[VMEM] * len(out_shape) if several else VMEM,
        scratch_shapes=scratch,
        compiler_params=pltpu.CompilerParams(vmem_limit_bytes=50 * 2**20),
        cost_estimate=pl.CostEstimate(flops=flops, bytes_accessed=moved, transcendentals=0),
        name=name,
    )


def slots_shape():
    return jax.ShapeDtypeStruct((GROUPS * SLOT_ROWS, 128), bf16)


SLOT_STAGE = pltpu.VMEM((GROUPS * SLOT_ROWS, 128), f32)
TABLE = pltpu.VMEM((STARTS[-1], LATS), bf16)
TABLE_S = pltpu.VMEM((PAIR_STARTS[-1], 256), bf16)
EIGHT = pltpu.SemaphoreType.DMA((BLOCKS,))
ONE = pltpu.SemaphoreType.DMA


def spread(fields, cotangent, forward, scale):
    return call(
        spread_kernel,
        jax.ShapeDtypeStruct((GROUPS * FIRST_ROWS, 128), bf16),
        [VMEM, VMEM, VMEM, SMEM],
        [pltpu.VMEM((GROUPS * FIRST_ROWS, 128), f32)],
        3 * 10**8, 4 * 10**6, "spread",
    )(fields, cotangent, forward, scale)


def first(received, analysis, degree_col):
    return call(
        first_kernel,
        slots_shape(),
        [ANY, ANY, VMEM],
        [
            pltpu.VMEM((GROUPS, 48, 128), bf16),
            pltpu.VMEM((GROUPS * 48, 128), f32),
            SLOT_STAGE, TABLE, ONE, EIGHT,
        ],
        10**9, 6 * 10**6, "first",
    )(received, analysis, degree_col)


def middle(received, cotangents, analysis, synthesis, degree_row, degree_col, inverse, inverse_t):
    return call(
        middle_kernel,
        slots_shape(),
        [VMEM, ANY, ANY, ANY, VMEM, VMEM, VMEM, VMEM],
        [
            pltpu.VMEM((GROUPS, 64, 128), bf16),
            pltpu.VMEM((GROUPS * 64, 128), f32),
            SLOT_STAGE, TABLE, TABLE_S, ONE, EIGHT, EIGHT,
        ],
        3 * 10**9, 12 * 10**6, "middle",
    )(received, cotangents, analysis, synthesis, degree_row, degree_col, inverse, inverse_t)


def last(received, synthesis, degree_row, weight_rows):
    return call(
        last_kernel,
        jax.ShapeDtypeStruct((GROUPS * LAST_ROWS, 128), bf16),
        [VMEM, ANY, VMEM, VMEM],
        [SLOT_STAGE, pltpu.VMEM((GROUPS * LAST_ROWS, 128), f32), TABLE_S, EIGHT],
        10**9, 7 * 10**6, "last",
    )(received, synthesis, degree_row, weight_rows)


def gather(received, forward, cotangent):
    return call(
        gather_kernel,
        jax.ShapeDtypeStruct((BAND, LONS, CHANNELS), bf16),
        [VMEM, VMEM, VMEM],
        [pltpu.VMEM((GROUPS * LAST_ROWS, 128), f32)],
        3 * 10**8, 3 * 10**6, "gather",
    )(received, forward, cotangent)


def mix(adjoint, received, weights, turn):
    return call(
        functools.partial(mix_kernel, adjoint),
        [slots_shape(), jax.ShapeDtypeStruct((SLOTS, CHANNELS, COEFS), bf16)],
        [VMEM, VMEM, VMEM],
        [SLOT_STAGE],
        6 * 10**8, 3 * 10**6, "adjoint_mix" if adjoint else "mix",
    )(received, weights, turn)


def exchange(rows):
    count = rows.shape[0] // GROUPS
    out = lax.all_to_all(
        rows.reshape(GROUPS, count, 128), "lat", split_axis=0, concat_axis=0, tiled=True
    )
    return out.reshape(GROUPS * count, 128)


def weight_gradient(coeffs, grads, turn):
    turned = jnp.einsum("sjcf,fe->sjce", coeffs, turn, preferred_element_type=f32).astype(bf16)
    real = jnp.einsum("sjcf,sjdf->jcd", coeffs, grads, preferred_element_type=f32)
    imag = jnp.einsum("sjcf,sjdf->jcd", turned, grads, preferred_element_type=f32)
    return jnp.stack([real, imag], axis=1).astype(bf16)


def local(fields, cotangent, weights, degree_of):
    table = {k: jnp.asarray(v) for k, v in constants().items()}
    slots = degree_of.reshape(GROUPS, SLOTS).T.reshape(DEGREES)
    degree_col, degree_row = slots[:, None], slots[None, :]
    scale = lax.dynamic_slice(table["weight"], (lax.axis_index("lat") * BAND,), (BAND,))
    turned_weights = jnp.swapaxes(weights, 2, 3)
    on_bands = exchange(spread(fields[0], cotangent[0], table["forward"], scale))
    on_bands = on_bands.reshape(GROUPS, FIRST_ROWS, 128)
    coeffs_sent = exchange(first(on_bands, table["analysis"], degree_col))
    filtered, coeffs = mix(False, coeffs_sent, turned_weights, table["turn"])
    grad_sent = exchange(
        middle(
            exchange(filtered), on_bands, table["analysis"], table["synthesis"],
            degree_row, degree_col, table["inverse"], table["inverse_t"],
        )
    )
    grad_coeffs, grads = mix(True, grad_sent, weights, table["turn"])
    all_coeffs = lax.all_gather(coeffs, "batch", axis=0)
    all_grads = lax.all_gather(grads, "batch", axis=0)
    grad_weights = weight_gradient(all_coeffs, all_grads, table["turn"])
    returned = exchange(last(exchange(grad_coeffs), table["synthesis"], degree_row, table["weight_rows"]))
    grad_fields = gather(returned, table["forward"], cotangent[0])[None]
    return grad_fields, grad_weights


def solution(mesh):
    return jax.shard_map(
        local,
        mesh=mesh,
        in_specs=(
            P("batch", "lat", None, None),
            P("batch", "lat", None, None),
            P("lat", None, None, None),
            P(),
        ),
        out_specs=(P("batch", "lat", None, None), P("lat", None, None, None)),
        check_vma=False,
    )
```

```python
import functools

import jax
import jax.numpy as jnp
import numpy as np
from jax import lax
from jax.experimental import pallas as pl
from jax.experimental.pallas import tpu as pltpu
from jax.sharding import PartitionSpec as P

LATS = 192
LONS = 384
ORDERS = 128
DEGREES = 128
CHANNELS = 384

GROUPS = 64
BAND = LATS // GROUPS
PARTS = CHANNELS // GROUPS
SLOTS = DEGREES // GROUPS
COEFS = 2 * ORDERS
BLOCKS = ORDERS // 16
SPEC_ROWS = BAND * PARTS * 2
SENT_ROWS = 48
COT_CUTS = (0, 12, 36, 54)
SLOT_ROWS = SLOTS * PARTS * 2
LAST_ROWS = 40
REACH = [DEGREES - 16 * t for t in range(BLOCKS)]
STARTS = [16 * sum(REACH[:t]) for t in range(BLOCKS + 1)]
PAIR_ROWS = 8 * LATS

f32 = jnp.float32
bf16 = jnp.bfloat16
TN = (((0,), (0,)), ((), ()))
NN = (((1,), (0,)), ((), ()))
NT = (((1,), (1,)), ((), ()))


def legendre_table():
    colatitude = np.pi * (np.arange(LATS) + 0.5) / LATS
    cosine, sine = np.cos(colatitude), np.sin(colatitude)
    order = np.arange(ORDERS, dtype=np.float64)[:, None]
    steps = np.arange(1, ORDERS)
    growth = np.concatenate([[0.0], np.cumsum(0.5 * np.log((2.0 * steps + 1.0) / (2.0 * steps)))])
    diagonal = np.exp(0.5 * np.log(1.0 / (4.0 * np.pi)) + growth[:, None] + order * np.log(sine))
    table = np.zeros((ORDERS, DEGREES, LATS))
    for degree in range(DEGREES):
        table[degree, degree] = diagonal[degree]
        if degree >= 1:
            m = degree - 1
            table[m, degree] = np.sqrt(2.0 * m + 3.0) * cosine * table[m, m]
        if degree >= 2:
            m = order[: degree - 1]
            lead = np.sqrt((4.0 * degree**2 - 1.0) / (degree**2 - m**2))
            back = np.sqrt(((degree - 1.0) ** 2 - m**2) / (4.0 * (degree - 1.0) ** 2 - 1.0))
            table[: degree - 1, degree] = lead * (
                cosine * table[: degree - 1, degree - 1] - back * table[: degree - 1, degree - 2]
            )
    return table, 2.0 * np.pi * np.pi / LATS * sine


def fourier_tables():
    lon = np.arange(LONS)[:, None]
    order = np.arange(ORDERS)[None, :]
    phase = 2.0 * np.pi * (lon * order % LONS) / LONS
    forward = np.stack([np.cos(phase), -np.sin(phase)], axis=2).reshape(LONS, COEFS) / LONS
    doubled = np.where(order == 0, 1.0, 2.0)
    inverse = np.stack([doubled * np.cos(phase), -doubled * np.sin(phase)], axis=2)
    return forward.astype(bf16), inverse.reshape(LONS, COEFS).astype(bf16)


@functools.cache
def constants():
    table, quadrature = legendre_table()
    where = np.arange(LATS).reshape(GROUPS, BAND).T.reshape(-1)
    table = table[:, :, where]

    def by_block(values):
        values = values.astype(bf16)
        return np.concatenate(
            [values[16 * t + k, 16 * t :] for t in range(BLOCKS) for k in range(16)], axis=0
        )

    analysis, weighted = by_block(table), by_block(table * quadrature[where])
    table = table.astype(bf16)
    synthesis = np.concatenate(
        [
            np.concatenate([table[16 * t + k].T, table[16 * t + k + 8].T], axis=1)
            for t in range(BLOCKS)
            for k in range(8)
        ],
        axis=0,
    )
    forward, inverse = fourier_tables()
    turn = np.zeros((COEFS, COEFS), np.float32)
    even = np.arange(0, COEFS, 2)
    turn[even + 1, even] = -1.0
    turn[even, even + 1] = 1.0
    return dict(
        analysis=analysis,
        weighted=weighted,
        synthesis=synthesis,
        forward=forward,
        inverse=inverse,
        inverse_t=np.ascontiguousarray(inverse.T),
        turn=turn.astype(bf16),
        weight_rows=quadrature[where].astype(np.float32)[:, None],
    )


def dot(left, right, dims=NN):
    return lax.dot_general(left, right, dims, preferred_element_type=f32)


def lane_of(shape):
    return lax.broadcasted_iota(jnp.int32, shape, 1)


def join(pieces, lanes):
    rolled = [pltpu.roll(x, s % 128, 1) if s % 128 else x for x, s in pieces]
    left = jnp.where(lanes < 32, rolled[0], rolled[1])
    right = jnp.where(lanes < 96, rolled[2], rolled[3])
    return jnp.where(lanes < 64, left, right)


def join_two(first, shift_first, second, shift_second, lanes):
    a = pltpu.roll(first, shift_first % 128, 1) if shift_first % 128 else first
    b = pltpu.roll(second, shift_second % 128, 1) if shift_second % 128 else second
    return jnp.where(lanes < 64, a, b)


def to_tiles(parts):
    lanes = lane_of(parts[0][0].shape)
    tiles = []
    for pair in range(BLOCKS // 2):
        h, at = pair // 2, 64 * (pair % 2)
        x = [parts[q][h] for q in range(PARTS)]
        a = join([(x[s], 32 * s - at) for s in range(4)], lanes)
        c = join([(x[s], 32 * s - at - 32) for s in range(4)], lanes)
        b = join_two(x[4], -at, x[5], 64 - at, lanes)
        tiles.append((a, b, c))
    return tiles


def from_tiles(tiles):
    lanes = lane_of(tiles[0][0].shape)
    parts = []
    for q in range(4):
        halves = []
        for h in range(2):
            pieces = []
            for k in range(4):
                a, _, c = tiles[2 * h + k // 2]
                pieces.append((c if k % 2 else a, 32 * (k - q)))
            halves.append(join(pieces, lanes))
        parts.append(halves)
    parts.append([join_two(tiles[2 * h][1], 0, tiles[2 * h + 1][1], 64, lanes) for h in range(2)])
    parts.append([join_two(tiles[2 * h][1], 64, tiles[2 * h + 1][1], 0, lanes) for h in range(2)])
    return parts


def as_bf16(tiles):
    return [tuple(x.astype(bf16) for x in tile) for tile in tiles]


def block_operand(tiles, t):
    a, b, c = tiles[t // 2]
    return jnp.concatenate([c if t % 2 else a, b], axis=1)


def merge_blocks(sums):
    tiles = []
    for pair in range(BLOCKS // 2):
        one, two = sums[2 * pair], sums[2 * pair + 1]
        lanes = lane_of((one.shape[0], 128))
        b = jnp.where((lanes // 32) % 2 == 0, one[:, 128:], two[:, 128:])
        tiles.append((one[:, :128], b, two[:, :128]))
    return tiles


def analyse(tiles, table, ready, rows_each=4):
    sums = []
    for t in range(BLOCKS):
        ready(t)
        operand = block_operand(tiles, t)
        reach = REACH[t]
        order = (lane_of((reach, 256)) % 32) // 2
        total = jnp.zeros((reach, 256), f32)
        for k in range(0, 16, rows_each):
            part = dot(table[pl.ds(STARTS[t] + k * reach, rows_each * reach), :], operand)
            for n in range(rows_each):
                total = jnp.where(order == k + n, part[n * reach : (n + 1) * reach], total)
        if t:
            total = jnp.concatenate([jnp.zeros((16 * t, 256), f32), total], axis=0)
        sums.append(total)
    return merge_blocks(sums)


def synthesise(tiles, table, ready, rows_each=2):
    sums = []
    for t in range(BLOCKS):
        ready(t)
        operand = block_operand(tiles, t)
        low = (lane_of((DEGREES, 256)) % 32) < 16
        none = jnp.zeros_like(operand)
        stacked = jnp.concatenate(
            [jnp.where(low, operand, none), jnp.where(low, none, operand)], axis=0
        )
        order = (lane_of((LATS, 256)) % 16) // 2
        total = jnp.zeros((LATS, 256), f32)
        for k in range(0, 8, rows_each):
            part = dot(table[pl.ds(t * PAIR_ROWS + k * LATS, rows_each * LATS), :], stacked)
            for n in range(rows_each):
                total = jnp.where(order == k + n, part[n * LATS : (n + 1) * LATS], total)
        sums.append(total)
    return merge_blocks(sums)


def permute_rows(matrix, tiles):
    out = []
    for tile in tiles:
        moved = dot(matrix, jnp.concatenate(tile, axis=1))
        out.append(tuple(moved[:, 128 * n : 128 * (n + 1)] for n in range(3)))
    return out


def put_slots(parts, carried, stage, out):
    stride = SLOT_ROWS if carried is None else SENT_ROWS
    for j in range(SLOTS):
        for q in range(PARTS):
            for h in range(2):
                stage[pl.ds((j * PARTS + q) * 2 + h, GROUPS, stride=stride), :] = parts[q][h][
                    j * GROUPS : (j + 1) * GROUPS
                ]
    if carried is None:
        out[...] = stage[pl.ds(0, GROUPS * SLOT_ROWS), :].astype(bf16)
    else:
        rows = stage[...].reshape(GROUPS, SENT_ROWS, 128)[:, :SLOT_ROWS]
        more = carried[...].astype(f32).reshape(GROUPS, SLOT_ROWS, 128)
        both = jnp.concatenate([rows, more], axis=1)
        out[...] = both.reshape(GROUPS * SENT_ROWS, 128).astype(bf16)


def get_slots(received, stage):
    count = received.shape[0]
    stage[pl.ds(0, count), :] = received[...].astype(f32)
    return [
        [
            jnp.concatenate(
                [
                    stage[pl.ds((j * PARTS + q) * 2 + h, GROUPS, stride=count // GROUPS), :]
                    for j in range(SLOTS)
                ],
                axis=0,
            )
            for h in range(2)
        ]
        for q in range(PARTS)
    ]


def slot_rows_out(tiles, degree_col, carried, stage, out):
    pick = (degree_col[...] == lane_of((DEGREES, DEGREES))).astype(f32).astype(bf16)
    put_slots(from_tiles(permute_rows(pick, as_bf16(tiles))), carried, stage, out)


def slot_rows_in(received, degree_row, stage):
    rows = lax.broadcasted_iota(jnp.int32, (DEGREES, DEGREES), 0)
    pick = (rows == degree_row[...]).astype(f32).astype(bf16)
    return as_bf16(permute_rows(pick, as_bf16(to_tiles(get_slots(received, stage)))))


def table_copies(source, target, sems, bounds):
    copies = []
    for t in range(BLOCKS):
        rows = pl.ds(bounds[t], bounds[t + 1] - bounds[t])
        copies.append(pltpu.make_async_copy(source.at[rows, :], target.at[rows, :], sems.at[t]))
    return copies


PAIR_STARTS = [PAIR_ROWS * t for t in range(BLOCKS + 1)]


def cot_place(i, q, h):
    row = (i * PARTS + q) * 3 + h
    which = sum(row >= cut for cut in COT_CUTS[1:3])
    return which, row - COT_CUTS[which]


def spread_kernel(fields, cotangent, forward, out, cot_two, cot_three, field, cot, stages, sems):
    copies = []
    for i in range(BAND):
        copies.append(
            (
                pltpu.make_async_copy(fields.at[i], field.at[i], sems.at[2 * i]),
                pltpu.make_async_copy(cotangent.at[i], cot.at[i], sems.at[2 * i + 1]),
            )
        )
    for pair in copies:
        for copy in pair:
            copy.start()
    stage, stage_two, stage_three = stages.at[0], stages.at[1], stages.at[2]
    spots = ((stage, SPEC_ROWS, SENT_ROWS), (stage_two, 0, SLOT_ROWS), (stage_three, 0, SLOT_ROWS))
    for i in range(BAND):
        copies[i][0].wait()
        spectra = dot(field[i], forward[...], TN)
        for q in range(PARTS):
            rows = slice(q * GROUPS, (q + 1) * GROUPS)
            at = (i * PARTS + q) * 2
            for h in range(2):
                stage[pl.ds(at + h, GROUPS, stride=SENT_ROWS), :] = spectra[
                    rows, 128 * h : 128 * (h + 1)
                ]
        copies[i][1].wait()
        turned = jnp.transpose(cot[i].astype(f32))
        for q in range(PARTS):
            rows = slice(q * GROUPS, (q + 1) * GROUPS)
            for h in range(3):
                which, at = cot_place(i, q, h)
                place, base, stride = spots[which]
                place[pl.ds(base + at, GROUPS, stride=stride), :] = turned[
                    rows, 128 * h : 128 * (h + 1)
                ]
    for row in range(COT_CUTS[3] - COT_CUTS[2], SLOT_ROWS):
        stage_three[pl.ds(row, GROUPS, stride=SLOT_ROWS), :] = jnp.zeros((GROUPS, 128), f32)
    out[...] = stage[...].astype(bf16)
    short = GROUPS * SLOT_ROWS
    cot_two[...] = stage_two[pl.ds(0, short), :].astype(bf16)
    cot_three[...] = stage_three[pl.ds(0, short), :].astype(bf16)


def first_kernel(
    received, analysis, degree_col, carried, early, out, stage_in, stage, table, sems
):
    copies = table_copies(analysis, table, sems, STARTS)
    for copy in copies:
        copy.start()
    stage_in[...] = received[...].astype(f32)
    parts = [
        [
            jnp.concatenate(
                [
                    stage_in[pl.ds((i * PARTS + q) * 2 + h, GROUPS, stride=SENT_ROWS), :]
                    for i in range(BAND)
                ],
                axis=0,
            )
            for h in range(2)
        ]
        for q in range(PARTS)
    ]
    tiles = as_bf16(to_tiles(parts))
    sums = analyse(tiles, table, lambda t: copies[t].wait())
    slot_rows_out(sums, degree_col, carried, stage, out)


def gelu_slope(x):
    c = np.float32(np.sqrt(2.0 / np.pi))
    squared = x * x
    th = jnp.tanh(c * (x + 0.044715 * (x * squared)))
    return 0.5 * (1.0 + th) + (0.5 * c) * x * (1.0 - th * th) * (1.0 + (3 * 0.044715) * squared)


def middle_kernel(
    received, one, two, analysis, synthesis, degree_row, degree_col, inverse, inverse_t, out,
    rows_one, rows_two, stage_one, stage_two, stage, table, table_s, row_sems, sems, sems_s,
):
    copies_s = table_copies(synthesis, table_s, sems_s, PAIR_STARTS)
    copies = table_copies(analysis, table, sems, STARTS)
    fetches = (
        pltpu.make_async_copy(one.at[:, pl.ds(32, 16), :], rows_one, row_sems.at[0]),
        pltpu.make_async_copy(two.at[:, pl.ds(16, 32), :], rows_two, row_sems.at[1]),
    )
    for copy in (*copies_s, *fetches, *copies):
        copy.start()
    tiles = slot_rows_in(received, degree_row, stage)
    synth = from_tiles(synthesise(tiles, table_s, lambda t: copies_s[t].wait()))
    for fetch in fetches:
        fetch.wait()
    stage_one[...] = rows_one[...].astype(f32).reshape(GROUPS * 16, 128)
    stage_two[...] = rows_two[...].astype(f32).reshape(GROUPS * 32, 128)
    spots = ((stage_one, SPEC_ROWS - 32, 16), (stage_two, 8, 32), (stage, SLOT_ROWS, SENT_ROWS))

    def cot_rows(i, q, h):
        which, at = cot_place(i, q, h)
        place, base, stride = spots[which]
        return place[pl.ds(base + at, GROUPS, stride=stride), :]

    parts = []
    for q in range(PARTS):
        response = dot(jnp.concatenate(synth[q], axis=1).astype(bf16), inverse_t[...])
        cotangent = jnp.concatenate(
            [
                jnp.concatenate([cot_rows(i, q, h) for h in range(3)], axis=1)
                for i in range(BAND)
            ],
            axis=0,
        )
        upstream = (cotangent * gelu_slope(response)).astype(bf16)
        grad = dot(upstream, inverse[...])
        parts.append([grad[:, :128], grad[:, 128:]])
    sums = analyse(as_bf16(to_tiles(parts)), table, lambda t: copies[t].wait())
    slot_rows_out(sums, degree_col, None, stage, out)


def last_kernel(received, synthesis, degree_row, weight_rows, out, stage, stage_out, table_s, sems_s):
    copies_s = table_copies(synthesis, table_s, sems_s, PAIR_STARTS)
    for copy in copies_s:
        copy.start()
    tiles = slot_rows_in(received, degree_row, stage)
    synth = from_tiles(synthesise(tiles, table_s, lambda t: copies_s[t].wait()))
    for q in range(PARTS):
        for h in range(2):
            scaled = synth[q][h] * weight_rows[...]
            for i in range(BAND):
                at = (i * PARTS + q) * 2 + h
                stage_out[pl.ds(at, GROUPS, stride=LAST_ROWS), :] = scaled[
                    i * GROUPS : (i + 1) * GROUPS
                ]
    for row in range(SPEC_ROWS, LAST_ROWS):
        stage_out[pl.ds(row, GROUPS, stride=LAST_ROWS), :] = jnp.zeros((GROUPS, 128), f32)
    out[...] = stage_out[...].astype(bf16)


def gather_kernel(received, forward, cotangent, weight_grads, out, stage):
    stage[...] = received[...].astype(f32)
    for i in range(BAND):
        halves = [
            jnp.concatenate(
                [
                    stage[pl.ds((i * PARTS + q) * 2 + h, GROUPS, stride=LAST_ROWS), :]
                    for q in range(PARTS)
                ],
                axis=0,
            )
            for h in range(2)
        ]
        rows = jnp.concatenate(halves, axis=1).astype(bf16)
        delta = dot(forward[...], rows, NT)
        out[i] = (cotangent[i].astype(f32) + delta).astype(bf16)


def mix_kernel(adjoint, received, weights, turn, *rest):
    carried, out, kept, stage = (None, *rest) if adjoint else rest
    parts = get_slots(received, stage)
    results = []
    for j in range(SLOTS):
        own = slice(j * GROUPS, (j + 1) * GROUPS)
        held = jnp.concatenate(
            [jnp.concatenate([x[own] for x in parts[q]], axis=1) for q in range(PARTS)], axis=0
        ).astype(bf16)
        kept[j] = held
        turned = dot(held, turn[...])
        if adjoint:
            turned = -turned
        turned = turned.astype(bf16)
        results.append(dot(weights[j, 0], held) + dot(weights[j, 1], turned))
    mixed = [
        [
            jnp.concatenate(
                [x[q * GROUPS : (q + 1) * GROUPS, 128 * h : 128 * (h + 1)] for x in results],
                axis=0,
            )
            for h in range(2)
        ]
        for q in range(PARTS)
    ]
    put_slots(mixed, carried, stage, out)


VMEM = pl.BlockSpec(memory_space=pltpu.VMEM)
SMEM = pl.BlockSpec(memory_space=pltpu.SMEM)
ANY = pl.BlockSpec(memory_space=pl.ANY)


def call(kernel, out_shape, in_specs, scratch, flops, moved, name, limit=50):
    several = isinstance(out_shape, list)
    return pl.pallas_call(
        kernel,
        out_shape=out_shape,
        in_specs=in_specs,
        out_specs=[VMEM] * len(out_shape) if several else VMEM,
        scratch_shapes=scratch,
        compiler_params=pltpu.CompilerParams(vmem_limit_bytes=limit * 2**20),
        cost_estimate=pl.CostEstimate(flops=flops, bytes_accessed=moved, transcendentals=0),
        name=name,
    )


def message(rows):
    return jax.ShapeDtypeStruct((GROUPS * rows, 128), bf16)


def stage_of(rows):
    return pltpu.VMEM((GROUPS * rows, 128), f32)


TABLE = pltpu.VMEM((STARTS[-1], LATS), bf16)
TABLE_S = pltpu.VMEM((PAIR_STARTS[-1], 256), bf16)


def sems(count):
    return pltpu.SemaphoreType.DMA((count,))


def spread(fields, cotangent, forward):
    cycle = pltpu.VMEM((BAND, LONS, CHANNELS), bf16)
    return call(
        spread_kernel,
        [message(SENT_ROWS), message(SLOT_ROWS), message(SLOT_ROWS)],
        [ANY, ANY, VMEM],
        [cycle, cycle, pltpu.VMEM((3, GROUPS * SENT_ROWS, 128), f32), sems(2 * BAND)],
        3 * 10**8, 4 * 10**6, "spread", 60,
    )(fields, cotangent, forward)


def first(received, weighted, degree_col, carried, early):
    return call(
        first_kernel,
        message(SENT_ROWS),
        [VMEM, ANY, VMEM, VMEM, ANY],
        [stage_of(SENT_ROWS), stage_of(SENT_ROWS), TABLE, sems(BLOCKS)],
        10**9, 6 * 10**6, "first",
    )(received, weighted, degree_col, carried, early)


def middle(received, one, two, analysis, synthesis, degree_row, degree_col, inverse, inverse_t):
    return call(
        middle_kernel,
        message(SLOT_ROWS),
        [VMEM, ANY, ANY, ANY, ANY, VMEM, VMEM, VMEM, VMEM],
        [
            pltpu.VMEM((GROUPS, 16, 128), bf16), pltpu.VMEM((GROUPS, 32, 128), bf16),
            stage_of(16), stage_of(32), stage_of(SENT_ROWS),
            TABLE, TABLE_S, sems(2), sems(BLOCKS), sems(BLOCKS),
        ],
        3 * 10**9, 12 * 10**6, "middle",
    )(received, one, two, analysis, synthesis, degree_row, degree_col, inverse, inverse_t)


def last(received, synthesis, degree_row, weight_rows):
    return call(
        last_kernel,
        message(LAST_ROWS),
        [VMEM, ANY, VMEM, VMEM],
        [stage_of(SLOT_ROWS), stage_of(LAST_ROWS), TABLE_S, sems(BLOCKS)],
        10**9, 7 * 10**6, "last",
    )(received, synthesis, degree_row, weight_rows)


def gather(received, forward, cotangent, weight_grads):
    return call(
        gather_kernel,
        jax.ShapeDtypeStruct((BAND, LONS, CHANNELS), bf16),
        [VMEM, VMEM, VMEM, ANY],
        [stage_of(LAST_ROWS)],
        3 * 10**8, 3 * 10**6, "gather",
    )(received, forward, cotangent, weight_grads)


def mix(adjoint, received, weights, turn, *carried):
    rows = SLOT_ROWS if adjoint else SENT_ROWS
    return call(
        functools.partial(mix_kernel, adjoint),
        [message(rows), jax.ShapeDtypeStruct((SLOTS, CHANNELS, COEFS), bf16)],
        [VMEM, VMEM, VMEM] + [VMEM] * len(carried),
        [stage_of(rows)],
        6 * 10**8, 3 * 10**6, "adjoint_mix" if adjoint else "mix",
    )(received, weights, turn, *carried)


def exchange(rows):
    count = rows.shape[0] // GROUPS
    out = lax.all_to_all(
        rows.reshape(GROUPS, count, 128), "lat", split_axis=0, concat_axis=0, tiled=True
    )
    return out.reshape(GROUPS * count, 128)


def weight_gradient(coeffs, grads, turn):
    turned = jnp.einsum("sjcf,fe->sjce", coeffs, turn, preferred_element_type=f32).astype(bf16)
    both = jnp.stack([coeffs, turned], axis=2)
    total = jnp.einsum("sjpcf,sjdf->jpcd", both, grads, preferred_element_type=f32)
    return total.astype(bf16)


def local(fields, cotangent, weights, degree_of):
    table = {k: jnp.asarray(v) for k, v in constants().items()}
    slots = degree_of.reshape(GROUPS, SLOTS).T.reshape(DEGREES)
    degree_col, degree_row = slots[:, None], slots[None, :]
    turned_weights = jnp.swapaxes(weights, 2, 3)
    sent, cot_two, cot_three = spread(fields[0], cotangent[0], table["forward"])
    one = exchange(sent)
    two = exchange(first(one, table["weighted"], degree_col, cot_two, turned_weights))
    filtered, coeffs = mix(False, two, turned_weights, table["turn"], cot_three)
    all_coeffs = lax.all_gather(coeffs, "batch", axis=0)
    three = exchange(filtered)
    as_sent = (GROUPS, SENT_ROWS, 128)
    four = exchange(
        middle(
            three, one.reshape(as_sent), two.reshape(as_sent), table["analysis"],
            table["synthesis"], degree_row, degree_col, table["inverse"], table["inverse_t"],
        )
    )
    grad_coeffs, grads = mix(True, four, weights, table["turn"])
    all_grads = lax.all_gather(grads, "batch", axis=0)
    grad_weights = weight_gradient(all_coeffs, all_grads, table["turn"])
    five = exchange(grad_coeffs)
    six = exchange(last(five, table["synthesis"], degree_row, table["weight_rows"]))
    grad_fields = gather(six, table["forward"], cotangent[0], grad_weights)[None]
    return grad_fields, grad_weights


def solution(mesh):
    return jax.shard_map(
        local,
        mesh=mesh,
        in_specs=(
            P("batch", "lat", None, None),
            P("batch", "lat", None, None),
            P("lat", None, None, None),
            P(),
        ),
        out_specs=(P("batch", "lat", None, None), P("lat", None, None, None)),
        check_vma=False,
    )
```

```python
import functools

import jax
import jax.numpy as jnp
import numpy as np
from jax import lax
from jax.experimental import pallas as pl
from jax.experimental.pallas import tpu as pltpu
from jax.sharding import PartitionSpec as P

LATS = 192
LONS = 384
ORDERS = 128
DEGREES = 128
CHANNELS = 384

GROUPS = 64
BAND = LATS // GROUPS
PARTS = CHANNELS // GROUPS
SLOTS = DEGREES // GROUPS
COEFS = 2 * ORDERS
BLOCKS = ORDERS // 16
SPEC_ROWS = BAND * PARTS * 2
SENT_ROWS = 48
COT_CUTS = (0, 12, 36, 54)
SLOT_ROWS = SLOTS * PARTS * 2
LAST_ROWS = 40
HALF = GROUPS // 2
LOW = LATS // 2
REACH = [DEGREES // 2 - 8 * t for t in range(BLOCKS)]
STARTS = [16 * sum(REACH[:t]) for t in range(BLOCKS + 1)]
STEPS = [8 * LOW * t for t in range(BLOCKS + 1)]
PLACES = [*range(HALF), *range(GROUPS - 1, HALF - 1, -1)]

f32 = jnp.float32
bf16 = jnp.bfloat16
TN = (((0,), (0,)), ((), ()))
NN = (((1,), (0,)), ((), ()))
NT = (((1,), (1,)), ((), ()))


def legendre_table():
    colatitude = np.pi * (np.arange(LATS) + 0.5) / LATS
    cosine, sine = np.cos(colatitude), np.sin(colatitude)
    order = np.arange(ORDERS, dtype=np.float64)[:, None]
    steps = np.arange(1, ORDERS)
    growth = np.concatenate([[0.0], np.cumsum(0.5 * np.log((2.0 * steps + 1.0) / (2.0 * steps)))])
    diagonal = np.exp(0.5 * np.log(1.0 / (4.0 * np.pi)) + growth[:, None] + order * np.log(sine))
    table = np.zeros((ORDERS, DEGREES, LATS))
    for degree in range(DEGREES):
        table[degree, degree] = diagonal[degree]
        if degree >= 1:
            m = degree - 1
            table[m, degree] = np.sqrt(2.0 * m + 3.0) * cosine * table[m, m]
        if degree >= 2:
            m = order[: degree - 1]
            lead = np.sqrt((4.0 * degree**2 - 1.0) / (degree**2 - m**2))
            back = np.sqrt(((degree - 1.0) ** 2 - m**2) / (4.0 * (degree - 1.0) ** 2 - 1.0))
            table[: degree - 1, degree] = lead * (
                cosine * table[: degree - 1, degree - 1] - back * table[: degree - 1, degree - 2]
            )
    return table, 2.0 * np.pi * np.pi / LATS * sine


def fourier_tables():
    lon = np.arange(LONS)[:, None]
    order = np.arange(ORDERS)[None, :]
    phase = 2.0 * np.pi * (lon * order % LONS) / LONS
    forward = np.stack([np.cos(phase), -np.sin(phase)], axis=2).reshape(LONS, COEFS) / LONS
    doubled = np.where(order == 0, 1.0, 2.0)
    inverse = np.stack([doubled * np.cos(phase), -doubled * np.sin(phase)], axis=2)
    return forward.astype(bf16), inverse.reshape(LONS, COEFS).astype(bf16)


@functools.cache
def constants():
    table, quadrature = legendre_table()
    where = (np.array(PLACES)[None, :] * BAND + np.arange(BAND)[:, None]).reshape(-1)
    low = (np.arange(HALF)[None, :] * BAND + np.arange(BAND)[:, None]).reshape(-1)

    def for_analysis(values):
        values = values.astype(bf16)
        return np.concatenate(
            [
                np.concatenate([values[16 * t + k + 8 * g, 16 * t + odd :: 2] for g in (0, 1)], axis=1)
                for t in range(BLOCKS)
                for odd in (0, 1)
                for k in range(8)
            ],
            axis=0,
        )

    analysis = for_analysis(table[:, :, low])
    weighted = for_analysis((table * quadrature)[:, :, low])
    below = table[:, :, low].astype(bf16)
    synthesis = np.concatenate(
        [
            np.concatenate([below[16 * t + k + 4 * g, odd::2].T for g in range(4)], axis=1)
            for t in range(BLOCKS)
            for odd in (0, 1)
            for k in range(4)
        ],
        axis=0,
    )
    forward, inverse = fourier_tables()
    turn = np.zeros((COEFS, COEFS), np.float32)
    even = np.arange(0, COEFS, 2)
    turn[even + 1, even] = -1.0
    turn[even, even + 1] = 1.0
    return dict(
        analysis=analysis,
        weighted=weighted,
        synthesis=synthesis,
        forward=forward,
        inverse=inverse,
        inverse_t=np.ascontiguousarray(inverse.T),
        turn=turn.astype(bf16),
        weight_rows=quadrature[where].astype(np.float32)[:, None],
    )


def dot(left, right, dims=NN):
    return lax.dot_general(left, right, dims, preferred_element_type=f32)


def lane_of(shape):
    return lax.broadcasted_iota(jnp.int32, shape, 1)


def join(pieces, lanes):
    rolled = [pltpu.roll(x, s % 128, 1) if s % 128 else x for x, s in pieces]
    left = jnp.where(lanes < 32, rolled[0], rolled[1])
    right = jnp.where(lanes < 96, rolled[2], rolled[3])
    return jnp.where(lanes < 64, left, right)


def join_two(first, shift_first, second, shift_second, lanes):
    a = pltpu.roll(first, shift_first % 128, 1) if shift_first % 128 else first
    b = pltpu.roll(second, shift_second % 128, 1) if shift_second % 128 else second
    return jnp.where(lanes < 64, a, b)


def to_tiles(parts):
    lanes = lane_of(parts[0][0].shape)
    tiles = []
    for pair in range(BLOCKS // 2):
        h, at = pair // 2, 64 * (pair % 2)
        x = [parts[q][h] for q in range(PARTS)]
        a = join([(x[s], 32 * s - at) for s in range(4)], lanes)
        c = join([(x[s], 32 * s - at - 32) for s in range(4)], lanes)
        b = join_two(x[4], -at, x[5], 64 - at, lanes)
        tiles.append((a, b, c))
    return tiles


def from_tiles(tiles):
    lanes = lane_of(tiles[0][0].shape)
    parts = []
    for q in range(4):
        halves = []
        for h in range(2):
            pieces = []
            for k in range(4):
                a, _, c = tiles[2 * h + k // 2]
                pieces.append((c if k % 2 else a, 32 * (k - q)))
            halves.append(join(pieces, lanes))
        parts.append(halves)
    parts.append([join_two(tiles[2 * h][1], 0, tiles[2 * h + 1][1], 64, lanes) for h in range(2)])
    parts.append([join_two(tiles[2 * h][1], 64, tiles[2 * h + 1][1], 0, lanes) for h in range(2)])
    return parts


def as_bf16(tiles):
    return [tuple(x.astype(bf16) for x in tile) for tile in tiles]


def block_operand(tiles, t):
    a, b, c = tiles[t // 2]
    return jnp.concatenate([c if t % 2 else a, b], axis=1)


def merge_blocks(sums):
    tiles = []
    for pair in range(BLOCKS // 2):
        one, two = sums[2 * pair], sums[2 * pair + 1]
        lanes = lane_of((one.shape[0], 128))
        b = jnp.where((lanes // 32) % 2 == 0, one[:, 128:], two[:, 128:])
        tiles.append((one[:, :128], b, two[:, :128]))
    return tiles


def order_sign(lanes):
    return jnp.where((lanes // 2) % 2 == 0, 1.0, -1.0).astype(f32)


def fold(x):
    low = jnp.concatenate([x[i * GROUPS : i * GROUPS + HALF] for i in range(BAND)], axis=0)
    high = jnp.concatenate(
        [x[i * GROUPS + HALF : (i + 1) * GROUPS] for i in reversed(range(BAND))], axis=0
    )
    high = high * order_sign(lane_of(high.shape))
    return low + high, low - high


def unfold(even, odd):
    low = even + odd
    high = (even - odd) * order_sign(lane_of(low.shape))
    pieces = []
    for i in range(BAND):
        pieces.append(low[i * HALF : (i + 1) * HALF])
        pieces.append(high[(BAND - 1 - i) * HALF : (BAND - i) * HALF])
    return jnp.concatenate(pieces, axis=0)


def stacked(operand, groups, width):
    order = (lane_of(operand.shape) % 32) // 2
    none = jnp.zeros_like(operand)
    return jnp.concatenate(
        [jnp.where(order // width == g, operand, none) for g in range(groups)], axis=0
    )


def analyse(parts, table, ready):
    folded = [[fold(x) for x in pair] for pair in parts]
    tiles = [as_bf16(to_tiles([[x[odd] for x in pair] for pair in folded])) for odd in (0, 1)]
    sums = []
    for t in range(BLOCKS):
        ready(t)
        reach = REACH[t]
        order = (lane_of((reach, 256)) % 16) // 2
        pieces = []
        for odd in (0, 1):
            operand = stacked(block_operand(tiles[odd], t), 2, 8)
            rows = pl.ds(STARTS[t] + odd * 8 * reach, 8 * reach)
            part = dot(table[rows, :], operand)
            total = part[:reach]
            for k in range(1, 8):
                total = jnp.where(order == k, part[k * reach : (k + 1) * reach], total)
            if t:
                pieces.append(jnp.zeros((8 * t, 256), f32))
            pieces.append(total)
        sums.append(jnp.concatenate(pieces, axis=0))
    return merge_blocks(sums)


def synthesise(tiles, table, ready):
    sums = ([], [])
    order = (lane_of((LOW, 256)) % 8) // 2
    for t in range(BLOCKS):
        ready(t)
        operand = block_operand(tiles, t)
        for odd in (0, 1):
            rows = operand[odd * GROUPS : (odd + 1) * GROUPS]
            part = dot(table[pl.ds(STEPS[t] + odd * 4 * LOW, 4 * LOW), :], stacked(rows, 4, 4))
            total = part[:LOW]
            for k in range(1, 4):
                total = jnp.where(order == k, part[k * LOW : (k + 1) * LOW], total)
            sums[odd].append(total)
    even, odd = merge_blocks(sums[0]), merge_blocks(sums[1])
    return from_tiles([tuple(unfold(x, y) for x, y in zip(e, o)) for e, o in zip(even, odd)])


def permute_rows(matrix, tiles):
    out = []
    for tile in tiles:
        moved = dot(matrix, jnp.concatenate(tile, axis=1))
        out.append(tuple(moved[:, 128 * n : 128 * (n + 1)] for n in range(3)))
    return out


def put_slots(parts, carried, stage, out):
    stride = SLOT_ROWS if carried is None else SENT_ROWS
    for j in range(SLOTS):
        for q in range(PARTS):
            for h in range(2):
                stage[pl.ds((j * PARTS + q) * 2 + h, GROUPS, stride=stride), :] = parts[q][h][
                    j * GROUPS : (j + 1) * GROUPS
                ]
    if carried is None:
        out[...] = stage[pl.ds(0, GROUPS * SLOT_ROWS), :].astype(bf16)
    else:
        rows = stage[...].reshape(GROUPS, SENT_ROWS, 128)[:, :SLOT_ROWS]
        more = carried[...].astype(f32).reshape(GROUPS, SLOT_ROWS, 128)
        both = jnp.concatenate([rows, more], axis=1)
        out[...] = both.reshape(GROUPS * SENT_ROWS, 128).astype(bf16)


def get_slots(received, stage):
    count = received.shape[0]
    stage[pl.ds(0, count), :] = received[...].astype(f32)
    return [
        [
            jnp.concatenate(
                [
                    stage[pl.ds((j * PARTS + q) * 2 + h, GROUPS, stride=count // GROUPS), :]
                    for j in range(SLOTS)
                ],
                axis=0,
            )
            for h in range(2)
        ]
        for q in range(PARTS)
    ]


def slot_rows_out(tiles, degree_col, carried, stage, out):
    row = lane_of((DEGREES, DEGREES))
    pick = (degree_col[...] == 2 * (row % GROUPS) + row // GROUPS).astype(f32).astype(bf16)
    put_slots(from_tiles(permute_rows(pick, as_bf16(tiles))), carried, stage, out)


def slot_rows_in(received, degree_row, stage):
    row = lax.broadcasted_iota(jnp.int32, (DEGREES, DEGREES), 0)
    pick = (degree_row[...] == 2 * (row % GROUPS) + row // GROUPS).astype(f32).astype(bf16)
    return as_bf16(permute_rows(pick, as_bf16(to_tiles(get_slots(received, stage)))))


def table_copies(source, target, sems, bounds):
    copies = []
    for t in range(BLOCKS):
        rows = pl.ds(bounds[t], bounds[t + 1] - bounds[t])
        copies.append(pltpu.make_async_copy(source.at[rows, :], target.at[rows, :], sems.at[t]))
    return copies


def cot_place(i, q, h):
    row = (i * PARTS + q) * 3 + h
    which = sum(row >= cut for cut in COT_CUTS[1:3])
    return which, row - COT_CUTS[which]


def spread_kernel(
    fields, cotangent, forward_source, out, cot_two, cot_three, field, cot, forward, stages, sems
):
    copies = []
    fetch = pltpu.make_async_copy(forward_source, forward, sems.at[2 * BAND])
    fetch.start()
    for i in range(BAND):
        copies.append(
            (
                pltpu.make_async_copy(fields.at[i], field.at[i], sems.at[2 * i]),
                pltpu.make_async_copy(cotangent.at[i], cot.at[i], sems.at[2 * i + 1]),
            )
        )
    for pair in copies:
        for copy in pair:
            copy.start()
    stage, stage_two, stage_three = stages.at[0], stages.at[1], stages.at[2]
    spots = ((stage, SPEC_ROWS, SENT_ROWS), (stage_two, 0, SLOT_ROWS), (stage_three, 0, SLOT_ROWS))
    for i in range(BAND):
        if i == 0:
            fetch.wait()
        copies[i][0].wait()
        spectra = dot(field[i], forward[...], TN)
        for q in range(PARTS):
            rows = slice(q * GROUPS, (q + 1) * GROUPS)
            at = (i * PARTS + q) * 2
            for h in range(2):
                stage[pl.ds(at + h, GROUPS, stride=SENT_ROWS), :] = spectra[
                    rows, 128 * h : 128 * (h + 1)
                ]
        copies[i][1].wait()
        turned = jnp.transpose(cot[i].astype(f32))
        for q in range(PARTS):
            rows = slice(q * GROUPS, (q + 1) * GROUPS)
            for h in range(3):
                which, at = cot_place(i, q, h)
                place, base, stride = spots[which]
                place[pl.ds(base + at, GROUPS, stride=stride), :] = turned[
                    rows, 128 * h : 128 * (h + 1)
                ]
    for row in range(COT_CUTS[3] - COT_CUTS[2], SLOT_ROWS):
        stage_three[pl.ds(row, GROUPS, stride=SLOT_ROWS), :] = jnp.zeros((GROUPS, 128), f32)
    out[...] = stage[...].astype(bf16)
    short = GROUPS * SLOT_ROWS
    cot_two[...] = stage_two[pl.ds(0, short), :].astype(bf16)
    cot_three[...] = stage_three[pl.ds(0, short), :].astype(bf16)


def first_kernel(
    received, analysis, degree_col, carried, early, out, stage_in, stage, table, sems
):
    copies = table_copies(analysis, table, sems, STARTS)
    for copy in copies:
        copy.start()
    stage_in[...] = received[...].astype(f32)
    parts = [
        [
            jnp.concatenate(
                [
                    stage_in[pl.ds((i * PARTS + q) * 2 + h, GROUPS, stride=SENT_ROWS), :]
                    for i in range(BAND)
                ],
                axis=0,
            )
            for h in range(2)
        ]
        for q in range(PARTS)
    ]
    sums = analyse(parts, table, lambda t: copies[t].wait())
    slot_rows_out(sums, degree_col, carried, stage, out)


def gelu_slope(x):
    c = np.float32(np.sqrt(2.0 / np.pi))
    squared = x * x
    th = jnp.tanh(c * (x + 0.044715 * (x * squared)))
    return 0.5 * (1.0 + th) + (0.5 * c) * x * (1.0 - th * th) * (1.0 + (3 * 0.044715) * squared)


def middle_kernel(
    received, one, two, analysis, synthesis, degree_row, degree_col, inverse_source, turned_source, out,
    inverse, inverse_t, rows_one, rows_two, stage_one, stage_two, stage, table, table_s, row_sems, sems, sems_s,
):
    copies_s = table_copies(synthesis, table_s, sems_s, STEPS)
    copies = table_copies(analysis, table, sems, STARTS)
    fetches = (
        pltpu.make_async_copy(one.at[:, pl.ds(32, 16), :], rows_one, row_sems.at[0]),
        pltpu.make_async_copy(two.at[:, pl.ds(16, 32), :], rows_two, row_sems.at[1]),
        pltpu.make_async_copy(inverse_source, inverse, row_sems.at[2]),
        pltpu.make_async_copy(turned_source, inverse_t, row_sems.at[3]),
    )
    for copy in (*copies_s, *fetches, *copies):
        copy.start()
    tiles = slot_rows_in(received, degree_row, stage)
    synth = synthesise(tiles, table_s, lambda t: copies_s[t].wait())
    for fetch in fetches:
        fetch.wait()
    stage_one[...] = rows_one[...].astype(f32).reshape(GROUPS * 16, 128)
    stage_two[...] = rows_two[...].astype(f32).reshape(GROUPS * 32, 128)
    spots = ((stage_one, SPEC_ROWS - 32, 16), (stage_two, 8, 32), (stage, SLOT_ROWS, SENT_ROWS))

    def cot_rows(i, q, h):
        which, at = cot_place(i, q, h)
        place, base, stride = spots[which]
        return place[pl.ds(base + at, GROUPS, stride=stride), :]

    parts = []
    for q in range(PARTS):
        response = dot(jnp.concatenate(synth[q], axis=1).astype(bf16), inverse_t[...])
        cotangent = jnp.concatenate(
            [
                jnp.concatenate([cot_rows(i, q, h) for h in range(3)], axis=1)
                for i in range(BAND)
            ],
            axis=0,
        )
        upstream = (cotangent * gelu_slope(response)).astype(bf16)
        grad = dot(upstream, inverse[...])
        parts.append([grad[:, :128], grad[:, 128:]])
    sums = analyse(parts, table, lambda t: copies[t].wait())
    slot_rows_out(sums, degree_col, None, stage, out)


def last_kernel(received, synthesis, degree_row, weight_rows, out, stage, stage_out, table_s, sems_s):
    copies_s = table_copies(synthesis, table_s, sems_s, STEPS)
    for copy in copies_s:
        copy.start()
    tiles = slot_rows_in(received, degree_row, stage)
    synth = synthesise(tiles, table_s, lambda t: copies_s[t].wait())
    for q in range(PARTS):
        for h in range(2):
            scaled = synth[q][h] * weight_rows[...]
            for i in range(BAND):
                at = (i * PARTS + q) * 2 + h
                stage_out[pl.ds(at, GROUPS, stride=LAST_ROWS), :] = scaled[
                    i * GROUPS : (i + 1) * GROUPS
                ]
    for row in range(SPEC_ROWS, LAST_ROWS):
        stage_out[pl.ds(row, GROUPS, stride=LAST_ROWS), :] = jnp.zeros((GROUPS, 128), f32)
    out[...] = stage_out[...].astype(bf16)


def gather_kernel(received, forward, cotangent, weight_grads, out, stage):
    stage[...] = received[...].astype(f32)
    for i in range(BAND):
        halves = [
            jnp.concatenate(
                [
                    stage[pl.ds((i * PARTS + q) * 2 + h, GROUPS, stride=LAST_ROWS), :]
                    for q in range(PARTS)
                ],
                axis=0,
            )
            for h in range(2)
        ]
        rows = jnp.concatenate(halves, axis=1).astype(bf16)
        delta = dot(forward[...], rows, NT)
        out[i] = (cotangent[i].astype(f32) + delta).astype(bf16)


def mix_kernel(adjoint, received, weights, turn, *rest):
    carried, out, kept, stage = (None, *rest) if adjoint else rest
    parts = get_slots(received, stage)
    results = []
    for j in range(SLOTS):
        own = slice(j * GROUPS, (j + 1) * GROUPS)
        held = jnp.concatenate(
            [jnp.concatenate([x[own] for x in parts[q]], axis=1) for q in range(PARTS)], axis=0
        ).astype(bf16)
        kept[j] = held
        turned = dot(held, turn[...])
        if adjoint:
            turned = -turned
        turned = turned.astype(bf16)
        results.append(dot(weights[j, 0], held) + dot(weights[j, 1], turned))
    mixed = [
        [
            jnp.concatenate(
                [x[q * GROUPS : (q + 1) * GROUPS, 128 * h : 128 * (h + 1)] for x in results],
                axis=0,
            )
            for h in range(2)
        ]
        for q in range(PARTS)
    ]
    put_slots(mixed, carried, stage, out)


VMEM = pl.BlockSpec(memory_space=pltpu.VMEM)
SMEM = pl.BlockSpec(memory_space=pltpu.SMEM)
ANY = pl.BlockSpec(memory_space=pl.ANY)


def call(kernel, out_shape, in_specs, scratch, flops, moved, name, limit=24):
    several = isinstance(out_shape, list)
    return pl.pallas_call(
        kernel,
        out_shape=out_shape,
        in_specs=in_specs,
        out_specs=[VMEM] * len(out_shape) if several else VMEM,
        scratch_shapes=scratch,
        compiler_params=pltpu.CompilerParams(vmem_limit_bytes=limit * 2**20),
        cost_estimate=pl.CostEstimate(flops=flops, bytes_accessed=moved, transcendentals=0),
        name=name,
    )


def message(rows):
    return jax.ShapeDtypeStruct((GROUPS * rows, 128), bf16)


def stage_of(rows):
    return pltpu.VMEM((GROUPS * rows, 128), f32)


TABLE = pltpu.VMEM((STARTS[-1], LATS), bf16)
TABLE_S = pltpu.VMEM((STEPS[-1], 256), bf16)


def sems(count):
    return pltpu.SemaphoreType.DMA((count,))


def in_hbm(array):
    return pltpu.with_memory_space_constraint(array, pltpu.HBM)


def spread(fields, cotangent, forward):
    cycle = pltpu.VMEM((BAND, LONS, CHANNELS), bf16)
    return call(
        spread_kernel,
        [message(SENT_ROWS), message(SLOT_ROWS), message(SLOT_ROWS)],
        [ANY, ANY, ANY],
        [
            cycle, cycle, pltpu.VMEM((LONS, COEFS), bf16),
            pltpu.VMEM((3, GROUPS * SENT_ROWS, 128), f32), sems(2 * BAND + 1),
        ],
        3 * 10**8, 4 * 10**6, "spread",
    )(in_hbm(fields), in_hbm(cotangent), in_hbm(forward))


def first(received, weighted, degree_col, carried, early):
    return call(
        first_kernel,
        message(SENT_ROWS),
        [VMEM, ANY, VMEM, VMEM, ANY],
        [stage_of(SENT_ROWS), stage_of(SENT_ROWS), TABLE, sems(BLOCKS)],
        10**9, 6 * 10**6, "first",
    )(received, in_hbm(weighted), degree_col, carried, early)


def middle(received, one, two, analysis, synthesis, degree_row, degree_col, inverse, inverse_t):
    return call(
        middle_kernel,
        message(SLOT_ROWS),
        [VMEM, ANY, ANY, ANY, ANY, VMEM, VMEM, ANY, ANY],
        [
            pltpu.VMEM((LONS, COEFS), bf16), pltpu.VMEM((COEFS, LONS), bf16),
            pltpu.VMEM((GROUPS, 16, 128), bf16), pltpu.VMEM((GROUPS, 32, 128), bf16),
            stage_of(16), stage_of(32), stage_of(SENT_ROWS),
            TABLE, TABLE_S, sems(4), sems(BLOCKS), sems(BLOCKS),
        ],
        3 * 10**9, 12 * 10**6, "middle",
    )(received, one, two, in_hbm(analysis), in_hbm(synthesis), degree_row, degree_col,
      in_hbm(inverse), in_hbm(inverse_t))


def last(received, synthesis, degree_row, weight_rows):
    return call(
        last_kernel,
        message(LAST_ROWS),
        [VMEM, ANY, VMEM, VMEM],
        [stage_of(SLOT_ROWS), stage_of(LAST_ROWS), TABLE_S, sems(BLOCKS)],
        10**9, 7 * 10**6, "last",
    )(received, in_hbm(synthesis), degree_row, weight_rows)


def gather(received, forward, cotangent, weight_grads):
    return call(
        gather_kernel,
        jax.ShapeDtypeStruct((BAND, LONS, CHANNELS), bf16),
        [VMEM, VMEM, VMEM, ANY],
        [stage_of(LAST_ROWS)],
        3 * 10**8, 3 * 10**6, "gather",
    )(received, forward, cotangent, weight_grads)


def mix(adjoint, received, weights, turn, *carried):
    rows = SLOT_ROWS if adjoint else SENT_ROWS
    return call(
        functools.partial(mix_kernel, adjoint),
        [message(rows), jax.ShapeDtypeStruct((SLOTS, CHANNELS, COEFS), bf16)],
        [VMEM, VMEM, VMEM] + [VMEM] * len(carried),
        [stage_of(rows)],
        6 * 10**8, 3 * 10**6, "adjoint_mix" if adjoint else "mix",
    )(received, weights, turn, *carried)


def exchange(rows):
    count = rows.shape[0] // GROUPS
    out = lax.all_to_all(
        rows.reshape(GROUPS, count, 128), "lat", split_axis=0, concat_axis=0, tiled=True,
        axis_index_groups=[PLACES],
    )
    return out.reshape(GROUPS * count, 128)


def weight_gradient(coeffs, grads, turn):
    turned = jnp.einsum("sjcf,fe->sjce", coeffs, turn, preferred_element_type=f32).astype(bf16)
    both = jnp.stack([coeffs, turned], axis=2)
    total = jnp.einsum("sjpcf,sjdf->jpcd", both, grads, preferred_element_type=f32)
    return total.astype(bf16)


def local(fields, cotangent, weights, degree_of):
    table = {k: jnp.asarray(v) for k, v in constants().items()}
    slots = degree_of.reshape(GROUPS, SLOTS)
    slots = jnp.concatenate([slots[:HALF], slots[HALF:][::-1]], axis=0).T.reshape(DEGREES)
    degree_col, degree_row = slots[:, None], slots[None, :]
    turned_weights = jnp.swapaxes(weights, 2, 3)
    sent, cot_two, cot_three = spread(fields[0], cotangent[0], table["forward"])
    one = exchange(sent)
    two = exchange(first(one, table["weighted"], degree_col, cot_two, turned_weights))
    filtered, coeffs = mix(False, two, turned_weights, table["turn"], cot_three)
    all_coeffs = lax.all_gather(coeffs, "batch", axis=0)
    three = exchange(filtered)
    as_sent = (GROUPS, SENT_ROWS, 128)
    four = exchange(
        middle(
            three, one.reshape(as_sent), two.reshape(as_sent), table["analysis"],
            table["synthesis"], degree_row, degree_col, table["inverse"], table["inverse_t"],
        )
    )
    grad_coeffs, grads = mix(True, four, weights, table["turn"])
    all_grads = lax.all_gather(grads, "batch", axis=0)
    grad_weights = weight_gradient(all_coeffs, all_grads, table["turn"])
    five = exchange(grad_coeffs)
    six = exchange(last(five, table["synthesis"], degree_row, table["weight_rows"]))
    grad_fields = gather(six, table["forward"], cotangent[0], grad_weights)[None]
    return grad_fields, grad_weights


def solution(mesh):
    return jax.shard_map(
        local,
        mesh=mesh,
        in_specs=(
            P("batch", "lat", None, None),
            P("batch", "lat", None, None),
            P("lat", None, None, None),
            P(),
        ),
        out_specs=(P("batch", "lat", None, None), P("lat", None, None, None)),
        check_vma=False,
    )
```

```python
import functools

import jax
import jax.numpy as jnp
import numpy as np
from jax import lax
from jax.experimental import pallas as pl
from jax.experimental.pallas import tpu as pltpu
from jax.sharding import PartitionSpec as P

LATS = 192
LONS = 384
ORDERS = 128
DEGREES = 128
CHANNELS = 384

GROUPS = 64
BAND = LATS // GROUPS
PARTS = CHANNELS // GROUPS
SLOTS = DEGREES // GROUPS
COEFS = 2 * ORDERS
BLOCKS = ORDERS // 16
SPEC_ROWS = BAND * PARTS * 2
SENT_ROWS = 48
COT_CUTS = (0, 12, 36, 54)
SLOT_ROWS = SLOTS * PARTS * 2
LAST_ROWS = 40
PIECES = 4
HALF = GROUPS // 2
LOW = LATS // 2
REACH = [DEGREES // 2 - 8 * t for t in range(BLOCKS)]
STARTS = [16 * sum(REACH[:t]) for t in range(BLOCKS + 1)]
STEPS = [8 * LOW * t for t in range(BLOCKS + 1)]

f32 = jnp.float32
bf16 = jnp.bfloat16
TN = (((0,), (0,)), ((), ()))
NN = (((1,), (0,)), ((), ()))
NT = (((1,), (1,)), ((), ()))


def legendre_table():
    colatitude = np.pi * (np.arange(LATS) + 0.5) / LATS
    cosine, sine = np.cos(colatitude), np.sin(colatitude)
    order = np.arange(ORDERS, dtype=np.float64)[:, None]
    steps = np.arange(1, ORDERS)
    growth = np.concatenate([[0.0], np.cumsum(0.5 * np.log((2.0 * steps + 1.0) / (2.0 * steps)))])
    diagonal = np.exp(0.5 * np.log(1.0 / (4.0 * np.pi)) + growth[:, None] + order * np.log(sine))
    table = np.zeros((ORDERS, DEGREES, LATS))
    for degree in range(DEGREES):
        table[degree, degree] = diagonal[degree]
        if degree >= 1:
            m = degree - 1
            table[m, degree] = np.sqrt(2.0 * m + 3.0) * cosine * table[m, m]
        if degree >= 2:
            m = order[: degree - 1]
            lead = np.sqrt((4.0 * degree**2 - 1.0) / (degree**2 - m**2))
            back = np.sqrt(((degree - 1.0) ** 2 - m**2) / (4.0 * (degree - 1.0) ** 2 - 1.0))
            table[: degree - 1, degree] = lead * (
                cosine * table[: degree - 1, degree - 1] - back * table[: degree - 1, degree - 2]
            )
    return table, 2.0 * np.pi * np.pi / LATS * sine


def fourier_tables():
    lon = np.arange(LONS)[:, None]
    order = np.arange(ORDERS)[None, :]
    phase = 2.0 * np.pi * (lon * order % LONS) / LONS
    forward = np.stack([np.cos(phase), -np.sin(phase)], axis=2).reshape(LONS, COEFS) / LONS
    doubled = np.where(order == 0, 1.0, 2.0)
    inverse = np.stack([doubled * np.cos(phase), -doubled * np.sin(phase)], axis=2)
    return forward.astype(bf16), inverse.reshape(LONS, COEFS).astype(bf16)


@functools.cache
def constants():
    table, quadrature = legendre_table()
    low = (np.arange(HALF)[None, :] * BAND + np.arange(BAND)[:, None]).reshape(-1)

    def for_analysis(values):
        values = values.astype(bf16)
        return np.concatenate(
            [
                np.concatenate([values[16 * t + k + 8 * g, 16 * t + odd :: 2] for g in (0, 1)], axis=1)
                for t in range(BLOCKS)
                for odd in (0, 1)
                for k in range(8)
            ],
            axis=0,
        )

    analysis = for_analysis(table[:, :, low])
    weighted = for_analysis((table * quadrature)[:, :, low])
    below = table[:, :, low].astype(bf16)
    synthesis = np.concatenate(
        [
            np.concatenate([below[16 * t + k + 4 * g, odd::2].T for g in range(4)], axis=1)
            for t in range(BLOCKS)
            for odd in (0, 1)
            for k in range(4)
        ],
        axis=0,
    )
    forward, inverse = fourier_tables()
    turn = np.zeros((COEFS, COEFS), np.float32)
    even = np.arange(0, COEFS, 2)
    turn[even + 1, even] = -1.0
    turn[even, even + 1] = 1.0
    return dict(
        analysis=analysis,
        weighted=weighted,
        synthesis=synthesis,
        forward=forward,
        inverse=inverse,
        inverse_t=np.ascontiguousarray(inverse.T),
        turn=turn.astype(bf16),
        flip=np.eye(LOW)[::-1].astype(bf16),
        weight_rows=quadrature[low].astype(np.float32)[:, None],
    )


def dot(left, right, dims=NN):
    return lax.dot_general(left, right, dims, preferred_element_type=f32)


def lane_of(shape):
    return lax.broadcasted_iota(jnp.int32, shape, 1)


def join(pieces, lanes):
    rolled = [pltpu.roll(x, s % 128, 1) if s % 128 else x for x, s in pieces]
    left = jnp.where(lanes < 32, rolled[0], rolled[1])
    right = jnp.where(lanes < 96, rolled[2], rolled[3])
    return jnp.where(lanes < 64, left, right)


def join_two(first, shift_first, second, shift_second, lanes):
    a = pltpu.roll(first, shift_first % 128, 1) if shift_first % 128 else first
    b = pltpu.roll(second, shift_second % 128, 1) if shift_second % 128 else second
    return jnp.where(lanes < 64, a, b)


def to_tiles(parts):
    lanes = lane_of(parts[0][0].shape)
    tiles = []
    for pair in range(BLOCKS // 2):
        h, at = pair // 2, 64 * (pair % 2)
        x = [parts[q][h] for q in range(PARTS)]
        a = join([(x[s], 32 * s - at) for s in range(4)], lanes)
        c = join([(x[s], 32 * s - at - 32) for s in range(4)], lanes)
        b = join_two(x[4], -at, x[5], 64 - at, lanes)
        tiles.append((a, b, c))
    return tiles


def from_tiles(tiles):
    lanes = lane_of(tiles[0][0].shape)
    parts = []
    for q in range(4):
        halves = []
        for h in range(2):
            pieces = []
            for k in range(4):
                a, _, c = tiles[2 * h + k // 2]
                pieces.append((c if k % 2 else a, 32 * (k - q)))
            halves.append(join(pieces, lanes))
        parts.append(halves)
    parts.append([join_two(tiles[2 * h][1], 0, tiles[2 * h + 1][1], 64, lanes) for h in range(2)])
    parts.append([join_two(tiles[2 * h][1], 64, tiles[2 * h + 1][1], 0, lanes) for h in range(2)])
    return parts


def as_bf16(tiles):
    return [tuple(x.astype(bf16) for x in tile) for tile in tiles]


def block_operand(tiles, t):
    a, b, c = tiles[t // 2]
    return jnp.concatenate([c if t % 2 else a, b], axis=1)


def merge_blocks(sums):
    tiles = []
    for pair in range(BLOCKS // 2):
        one, two = sums[2 * pair], sums[2 * pair + 1]
        lanes = lane_of((one.shape[0], 128))
        b = jnp.where((lanes // 32) % 2 == 0, one[:, 128:], two[:, 128:])
        tiles.append((one[:, :128], b, two[:, :128]))
    return tiles


def order_sign(lanes):
    return jnp.where((lanes // 2) % 2 == 0, 1.0, -1.0).astype(f32)


def fold(pair, flip):
    x = jnp.concatenate(pair, axis=1)
    low = jnp.concatenate([x[i * GROUPS : i * GROUPS + HALF] for i in range(BAND)], axis=0)
    high = jnp.concatenate([x[i * GROUPS + HALF : (i + 1) * GROUPS] for i in range(BAND)], axis=0)
    high = dot(flip, high.astype(bf16)) * order_sign(lane_of(high.shape))
    both = (low.astype(bf16).astype(f32) + high, low.astype(bf16).astype(f32) - high)
    return [[x[:, :128], x[:, 128:]] for x in both]


def unfold(even, odd, flip, weight):
    even, odd = jnp.concatenate(even, axis=1), jnp.concatenate(odd, axis=1)
    low = even + odd
    high = (even - odd) * order_sign(lane_of(low.shape))
    if weight is not None:
        low, high = low * weight, high * weight
    high = dot(flip, high.astype(bf16))
    pieces = []
    for i in range(BAND):
        rows = slice(i * HALF, (i + 1) * HALF)
        pieces += [low[rows], high[rows]]
    whole = jnp.concatenate(pieces, axis=0)
    return tuple(whole[:, 128 * n : 128 * (n + 1)] for n in range(3))


def stacked(operand, groups, width):
    order = (lane_of(operand.shape) % 32) // 2
    none = jnp.zeros_like(operand)
    return jnp.concatenate(
        [jnp.where(order // width == g, operand, none) for g in range(groups)], axis=0
    )


def analyse(parts, flip, table, ready):
    folded = [fold(pair, flip) for pair in parts]
    tiles = [as_bf16(to_tiles([x[odd] for x in folded])) for odd in (0, 1)]
    sums = []
    for t in range(BLOCKS):
        ready(t)
        reach = REACH[t]
        order = (lane_of((reach, 256)) % 16) // 2
        pieces = []
        for odd in (0, 1):
            operand = stacked(block_operand(tiles[odd], t), 2, 8)
            rows = pl.ds(STARTS[t] + odd * 8 * reach, 8 * reach)
            part = dot(table[rows, :], operand)
            total = part[:reach]
            for k in range(1, 8):
                total = jnp.where(order == k, part[k * reach : (k + 1) * reach], total)
            if t:
                pieces.append(jnp.zeros((8 * t, 256), f32))
            pieces.append(total)
        sums.append(jnp.concatenate(pieces, axis=0))
    return merge_blocks(sums)


def synthesise(tiles, flip, weight, table, ready):
    sums = ([], [])
    order = (lane_of((LOW, 256)) % 8) // 2
    for t in range(BLOCKS):
        ready(t)
        operand = block_operand(tiles, t)
        for odd in (0, 1):
            rows = operand[odd * GROUPS : (odd + 1) * GROUPS]
            part = dot(table[pl.ds(STEPS[t] + odd * 4 * LOW, 4 * LOW), :], stacked(rows, 4, 4))
            total = part[:LOW]
            for k in range(1, 4):
                total = jnp.where(order == k, part[k * LOW : (k + 1) * LOW], total)
            sums[odd].append(total)
    even, odd = merge_blocks(sums[0]), merge_blocks(sums[1])
    return from_tiles([unfold(e, o, flip, weight) for e, o in zip(even, odd)])


def permute_rows(matrix, tiles):
    out = []
    for tile in tiles:
        moved = dot(matrix, jnp.concatenate(tile, axis=1))
        out.append(tuple(moved[:, 128 * n : 128 * (n + 1)] for n in range(3)))
    return out


def put_slots(parts, carried, stage, out):
    stride = SLOT_ROWS if carried is None else SENT_ROWS
    for j in range(SLOTS):
        for q in range(PARTS):
            for h in range(2):
                stage[pl.ds((j * PARTS + q) * 2 + h, GROUPS, stride=stride), :] = parts[q][h][
                    j * GROUPS : (j + 1) * GROUPS
                ]
    if carried is None:
        out[...] = stage[pl.ds(0, GROUPS * SLOT_ROWS), :].astype(bf16)
    else:
        rows = stage[...].reshape(GROUPS, SENT_ROWS, 128)[:, :SLOT_ROWS]
        more = carried[...].astype(f32).reshape(GROUPS, SLOT_ROWS, 128)
        both = jnp.concatenate([rows, more], axis=1)
        out[...] = both.reshape(GROUPS * SENT_ROWS, 128).astype(bf16)


def get_slots(received, stage):
    count = received.shape[0]
    stage[pl.ds(0, count), :] = received[...].astype(f32)
    return [
        [
            jnp.concatenate(
                [
                    stage[pl.ds((j * PARTS + q) * 2 + h, GROUPS, stride=count // GROUPS), :]
                    for j in range(SLOTS)
                ],
                axis=0,
            )
            for h in range(2)
        ]
        for q in range(PARTS)
    ]


def slot_rows_out(tiles, degree_col, carried, stage, out):
    row = lane_of((DEGREES, DEGREES))
    pick = (degree_col[...] == 2 * (row % GROUPS) + row // GROUPS).astype(f32).astype(bf16)
    put_slots(from_tiles(permute_rows(pick, as_bf16(tiles))), carried, stage, out)


def slot_rows_in(received, degree_row, stage):
    row = lax.broadcasted_iota(jnp.int32, (DEGREES, DEGREES), 0)
    pick = (degree_row[...] == 2 * (row % GROUPS) + row // GROUPS).astype(f32).astype(bf16)
    return as_bf16(permute_rows(pick, as_bf16(to_tiles(get_slots(received, stage)))))


def table_copies(source, target, sems, bounds):
    copies = []
    for t in range(BLOCKS):
        rows = pl.ds(bounds[t], bounds[t + 1] - bounds[t])
        copies.append(pltpu.make_async_copy(source.at[rows, :], target.at[rows, :], sems.at[t]))
    return copies


def cot_place(i, q, h):
    row = (i * PARTS + q) * 3 + h
    which = sum(row >= cut for cut in COT_CUTS[1:3])
    return which, row - COT_CUTS[which]


def spread_kernel(
    fields, cotangent, forward_source, out, cot_two, cot_three, field, cot, forward, stages, sems
):
    copies = []
    fetch = pltpu.make_async_copy(forward_source, forward, sems.at[2 * BAND])
    fetch.start()
    for i in range(BAND):
        copies.append(
            (
                pltpu.make_async_copy(fields.at[i], field.at[i], sems.at[2 * i]),
                pltpu.make_async_copy(cotangent.at[i], cot.at[i], sems.at[2 * i + 1]),
            )
        )
    for pair in copies:
        for copy in pair:
            copy.start()
    stage, stage_two, stage_three = stages.at[0], stages.at[1], stages.at[2]
    spots = ((stage, SPEC_ROWS, SENT_ROWS), (stage_two, 0, SLOT_ROWS), (stage_three, 0, SLOT_ROWS))
    for i in range(BAND):
        if i == 0:
            fetch.wait()
        copies[i][0].wait()
        spectra = dot(field[i], forward[...], TN)
        for q in range(PARTS):
            rows = slice(q * GROUPS, (q + 1) * GROUPS)
            at = (i * PARTS + q) * 2
            for h in range(2):
                stage[pl.ds(at + h, GROUPS, stride=SENT_ROWS), :] = spectra[
                    rows, 128 * h : 128 * (h + 1)
                ]
        copies[i][1].wait()
        turned = jnp.transpose(cot[i].astype(f32))
        for q in range(PARTS):
            rows = slice(q * GROUPS, (q + 1) * GROUPS)
            for h in range(3):
                which, at = cot_place(i, q, h)
                place, base, stride = spots[which]
                place[pl.ds(base + at, GROUPS, stride=stride), :] = turned[
                    rows, 128 * h : 128 * (h + 1)
                ]
    for row in range(COT_CUTS[3] - COT_CUTS[2], SLOT_ROWS):
        stage_three[pl.ds(row, GROUPS, stride=SLOT_ROWS), :] = jnp.zeros((GROUPS, 128), f32)
    out[...] = stage[...].astype(bf16)
    short = GROUPS * SLOT_ROWS
    cot_two[...] = stage_two[pl.ds(0, short), :].astype(bf16)
    cot_three[...] = stage_three[pl.ds(0, short), :].astype(bf16)


def first_kernel(
    received, analysis, degree_col, flip, carried, early, out, stage_in, stage, table, sems
):
    copies = table_copies(analysis, table, sems, STARTS)
    for copy in copies:
        copy.start()
    stage_in[...] = received[...].astype(f32)
    parts = [
        [
            jnp.concatenate(
                [
                    stage_in[pl.ds((i * PARTS + q) * 2 + h, GROUPS, stride=SENT_ROWS), :]
                    for i in range(BAND)
                ],
                axis=0,
            )
            for h in range(2)
        ]
        for q in range(PARTS)
    ]
    sums = analyse(parts, flip[...], table, lambda t: copies[t].wait())
    slot_rows_out(sums, degree_col, carried, stage, out)


def gelu_slope(x):
    c = np.float32(np.sqrt(2.0 / np.pi))
    squared = x * x
    th = jnp.tanh(c * (x + 0.044715 * (x * squared)))
    return 0.5 * (1.0 + th) + (0.5 * c) * x * (1.0 - th * th) * (1.0 + (3 * 0.044715) * squared)


def middle_kernel(
    received, one, two, analysis, synthesis, degree_row, degree_col, flip, inverse_source, turned_source, early, also, out,
    inverse, inverse_t, rows_one, rows_two, stage_one, stage_two, stage, table, table_s, row_sems, sems, sems_s,
):
    copies_s = table_copies(synthesis, table_s, sems_s, STEPS)
    copies = table_copies(analysis, table, sems, STARTS)
    fetches = (
        pltpu.make_async_copy(one.at[:, pl.ds(32, 16), :], rows_one, row_sems.at[0]),
        pltpu.make_async_copy(two.at[:, pl.ds(16, 32), :], rows_two, row_sems.at[1]),
        pltpu.make_async_copy(inverse_source, inverse, row_sems.at[2]),
        pltpu.make_async_copy(turned_source, inverse_t, row_sems.at[3]),
    )
    for copy in (*copies_s, *fetches, *copies):
        copy.start()
    tiles = slot_rows_in(received, degree_row, stage)
    synth = synthesise(tiles, flip[...], None, table_s, lambda t: copies_s[t].wait())
    for fetch in fetches:
        fetch.wait()
    stage_one[...] = rows_one[...].astype(f32).reshape(GROUPS * 16, 128)
    stage_two[...] = rows_two[...].astype(f32).reshape(GROUPS * 32, 128)
    spots = ((stage_one, SPEC_ROWS - 32, 16), (stage_two, 8, 32), (stage, SLOT_ROWS, SENT_ROWS))

    def cot_rows(i, q, h):
        which, at = cot_place(i, q, h)
        place, base, stride = spots[which]
        return place[pl.ds(base + at, GROUPS, stride=stride), :]

    parts = []
    for q in range(PARTS):
        response = dot(jnp.concatenate(synth[q], axis=1).astype(bf16), inverse_t[...])
        cotangent = jnp.concatenate(
            [
                jnp.concatenate([cot_rows(i, q, h) for h in range(3)], axis=1)
                for i in range(BAND)
            ],
            axis=0,
        )
        upstream = (cotangent * gelu_slope(response)).astype(bf16)
        grad = dot(upstream, inverse[...])
        parts.append([grad[:, :128], grad[:, 128:]])
    sums = analyse(parts, flip[...], table, lambda t: copies[t].wait())
    slot_rows_out(sums, degree_col, None, stage, out)


def last_kernel(received, synthesis, degree_row, weight_rows, flip, early, also, out, stage, stage_out, table_s, sems_s):
    copies_s = table_copies(synthesis, table_s, sems_s, STEPS)
    for copy in copies_s:
        copy.start()
    tiles = slot_rows_in(received, degree_row, stage)
    synth = synthesise(
        tiles, flip[...], weight_rows[...], table_s, lambda t: copies_s[t].wait()
    )
    for q in range(PARTS):
        for h in range(2):
            scaled = synth[q][h]
            for i in range(BAND):
                at = (i * PARTS + q) * 2 + h
                stage_out[pl.ds(at, GROUPS, stride=LAST_ROWS), :] = scaled[
                    i * GROUPS : (i + 1) * GROUPS
                ]
    for row in range(SPEC_ROWS, LAST_ROWS):
        stage_out[pl.ds(row, GROUPS, stride=LAST_ROWS), :] = jnp.zeros((GROUPS, 128), f32)
    out[...] = stage_out[...].astype(bf16)


def gather_kernel(received, forward, cotangent, weight_grads, out, stage):
    stage[...] = received[...].astype(f32)
    for i in range(BAND):
        halves = [
            jnp.concatenate(
                [
                    stage[pl.ds((i * PARTS + q) * 2 + h, GROUPS, stride=LAST_ROWS), :]
                    for q in range(PARTS)
                ],
                axis=0,
            )
            for h in range(2)
        ]
        rows = jnp.concatenate(halves, axis=1).astype(bf16)
        delta = dot(forward[...], rows, NT)
        out[i] = (cotangent[i].astype(f32) + delta).astype(bf16)


def mix_kernel(adjoint, received, weights, turn, *rest):
    carried, out, kept, stage = (None, *rest[2:]) if adjoint else rest
    parts = get_slots(received, stage)
    results = []
    for j in range(SLOTS):
        own = slice(j * GROUPS, (j + 1) * GROUPS)
        held = jnp.concatenate(
            [jnp.concatenate([x[own] for x in parts[q]], axis=1) for q in range(PARTS)], axis=0
        ).astype(bf16)
        kept[j] = held
        turned = dot(held, turn[...])
        if adjoint:
            turned = -turned
        turned = turned.astype(bf16)
        results.append(dot(weights[j, 0], held) + dot(weights[j, 1], turned))
    mixed = [
        [
            jnp.concatenate(
                [x[q * GROUPS : (q + 1) * GROUPS, 128 * h : 128 * (h + 1)] for x in results],
                axis=0,
            )
            for h in range(2)
        ]
        for q in range(PARTS)
    ]
    put_slots(mixed, carried, stage, out)


VMEM = pl.BlockSpec(memory_space=pltpu.VMEM)
SMEM = pl.BlockSpec(memory_space=pltpu.SMEM)
ANY = pl.BlockSpec(memory_space=pl.ANY)


def call(kernel, out_shape, in_specs, scratch, flops, moved, name, limit=24):
    several = isinstance(out_shape, list)
    return pl.pallas_call(
        kernel,
        out_shape=out_shape,
        in_specs=in_specs,
        out_specs=[VMEM] * len(out_shape) if several else VMEM,
        scratch_shapes=scratch,
        compiler_params=pltpu.CompilerParams(vmem_limit_bytes=limit * 2**20),
        cost_estimate=pl.CostEstimate(flops=flops, bytes_accessed=moved, transcendentals=0),
        name=name,
    )


def message(rows):
    return jax.ShapeDtypeStruct((GROUPS * rows, 128), bf16)


def stage_of(rows):
    return pltpu.VMEM((GROUPS * rows, 128), f32)


TABLE = pltpu.VMEM((STARTS[-1], LATS), bf16)
TABLE_S = pltpu.VMEM((STEPS[-1], 256), bf16)


def sems(count):
    return pltpu.SemaphoreType.DMA((count,))


def in_hbm(array):
    return pltpu.with_memory_space_constraint(array, pltpu.HBM)


def spread(fields, cotangent, forward):
    cycle = pltpu.VMEM((BAND, LONS, CHANNELS), bf16)
    return call(
        spread_kernel,
        [message(SENT_ROWS), message(SLOT_ROWS), message(SLOT_ROWS)],
        [ANY, ANY, ANY],
        [
            cycle, cycle, pltpu.VMEM((LONS, COEFS), bf16),
            pltpu.VMEM((3, GROUPS * SENT_ROWS, 128), f32), sems(2 * BAND + 1),
        ],
        3 * 10**8, 4 * 10**6, "spread",
    )(in_hbm(fields), in_hbm(cotangent), in_hbm(forward))


def first(received, weighted, degree_col, flip, carried, early):
    return call(
        first_kernel,
        message(SENT_ROWS),
        [VMEM, ANY, VMEM, VMEM, VMEM, ANY],
        [stage_of(SENT_ROWS), stage_of(SENT_ROWS), TABLE, sems(BLOCKS)],
        10**9, 6 * 10**6, "first",
    )(received, in_hbm(weighted), degree_col, flip, carried, early)


def middle(
    received, one, two, analysis, synthesis, degree_row, degree_col, flip, inverse, inverse_t, early, also
):
    return call(
        middle_kernel,
        message(SLOT_ROWS),
        [VMEM, ANY, ANY, ANY, ANY, VMEM, VMEM, VMEM, ANY, ANY, ANY, ANY],
        [
            pltpu.VMEM((LONS, COEFS), bf16), pltpu.VMEM((COEFS, LONS), bf16),
            pltpu.VMEM((GROUPS, 16, 128), bf16), pltpu.VMEM((GROUPS, 32, 128), bf16),
            stage_of(16), stage_of(32), stage_of(SENT_ROWS),
            TABLE, TABLE_S, sems(4), sems(BLOCKS), sems(BLOCKS),
        ],
        3 * 10**9, 12 * 10**6, "middle",
    )(received, in_hbm(one), in_hbm(two), in_hbm(analysis), in_hbm(synthesis), degree_row, degree_col, flip,
      in_hbm(inverse), in_hbm(inverse_t), in_hbm(early), in_hbm(also))


def last(received, synthesis, degree_row, weight_rows, flip, early, also):
    return call(
        last_kernel,
        message(LAST_ROWS),
        [VMEM, ANY, VMEM, VMEM, VMEM, ANY, ANY],
        [stage_of(SLOT_ROWS), stage_of(LAST_ROWS), TABLE_S, sems(BLOCKS)],
        10**9, 7 * 10**6, "last",
    )(received, in_hbm(synthesis), degree_row, weight_rows, flip, in_hbm(early), in_hbm(also))


def gather(received, forward, cotangent, weight_grads):
    return call(
        gather_kernel,
        jax.ShapeDtypeStruct((BAND, LONS, CHANNELS), bf16),
        [VMEM, VMEM, VMEM, ANY],
        [stage_of(LAST_ROWS)],
        3 * 10**8, 3 * 10**6, "gather",
    )(received, forward, cotangent, weight_grads)


def mix(adjoint, received, weights, turn, *carried):
    rows = SLOT_ROWS if adjoint else SENT_ROWS
    return call(
        functools.partial(mix_kernel, adjoint),
        [message(rows), jax.ShapeDtypeStruct((SLOTS, CHANNELS, COEFS), bf16)],
        [VMEM, VMEM, VMEM] + [ANY if adjoint else VMEM] * len(carried),
        [stage_of(rows)],
        6 * 10**8, 3 * 10**6, "adjoint_mix" if adjoint else "mix",
    )(received, weights, turn, *carried)


def exchange(rows):
    count = rows.shape[0] // GROUPS
    out = lax.all_to_all(
        rows.reshape(GROUPS, count, 128), "lat", split_axis=0, concat_axis=0, tiled=True,
    )
    return out.reshape(GROUPS * count, 128)


def gradient_kernel(*refs):
    coeffs, grads, turn, out = refs[:PIECES], refs[PIECES:-2], refs[-2], refs[-1]

    def rows_of(pieces, j):
        return jnp.concatenate(
            [jnp.concatenate([p[s, j] for s in range(p.shape[0])], axis=1) for p in pieces], axis=0
        )

    for j in range(SLOTS):
        right = rows_of(grads, j)
        left = rows_of(coeffs, j)
        turned = [
            dot(left[:, COEFS * s : COEFS * (s + 1)], turn[...]).astype(bf16)
            for s in range(coeffs[0].shape[0])
        ]
        out[j, 0] = dot(left, right, NT).astype(bf16)
        out[j, 1] = dot(jnp.concatenate(turned, axis=1), right, NT).astype(bf16)


def gather_pieces(x):
    return [lax.all_gather(p, "batch", axis=0) for p in jnp.split(x, PIECES, axis=1)]


def weight_gradient(coeffs, grads, turn):
    return call(
        gradient_kernel,
        jax.ShapeDtypeStruct((SLOTS, 2, CHANNELS, CHANNELS), bf16),
        [VMEM] * (2 * PIECES + 1),
        [],
        5 * 10**9, 8 * 10**6, "weight_gradient",
    )(*coeffs, *grads, turn)


def local(fields, cotangent, weights, degree_of):
    table = {k: jnp.asarray(v) for k, v in constants().items()}
    slots = degree_of.reshape(GROUPS, SLOTS).T.reshape(DEGREES)
    degree_col, degree_row = slots[:, None], slots[None, :]
    turned_weights = jnp.swapaxes(weights, 2, 3)
    sent, cot_two, cot_three = spread(fields[0], cotangent[0], table["forward"])
    one = exchange(sent)
    two = exchange(first(one, table["weighted"], degree_col, table["flip"], cot_two, turned_weights))
    filtered, coeffs = mix(False, two, turned_weights, table["turn"], cot_three)
    all_coeffs = gather_pieces(coeffs)
    three = exchange(filtered)
    as_sent = (GROUPS, SENT_ROWS, 128)
    four = exchange(
        middle(
            three, one.reshape(as_sent), two.reshape(as_sent), table["analysis"],
            table["synthesis"], degree_row, degree_col, table["flip"],
            table["inverse"], table["inverse_t"], *all_coeffs[:2],
        )
    )
    grad_coeffs, grads = mix(True, four, weights, table["turn"], *map(in_hbm, all_coeffs[2:]))
    all_grads = gather_pieces(grads)
    grad_weights = weight_gradient(all_coeffs, all_grads, table["turn"])
    five = exchange(grad_coeffs)
    six = exchange(
        last(
            five, table["synthesis"], degree_row, table["weight_rows"], table["flip"], *all_grads[:2]
        )
    )
    grad_fields = gather(six, table["forward"], cotangent[0], grad_weights)[None]
    return grad_fields, grad_weights


def solution(mesh):
    return jax.shard_map(
        local,
        mesh=mesh,
        in_specs=(
            P("batch", "lat", None, None),
            P("batch", "lat", None, None),
            P("lat", None, None, None),
            P(),
        ),
        out_specs=(P("batch", "lat", None, None), P("lat", None, None, None)),
        check_vma=False,
    )
```

```python
import functools

import jax
import jax.numpy as jnp
import numpy as np
from jax import lax
from jax.experimental import pallas as pl
from jax.experimental.pallas import tpu as pltpu
from jax.sharding import PartitionSpec as P

LATS = 192
LONS = 384
ORDERS = 128
DEGREES = 128
CHANNELS = 384

GROUPS = 64
BAND = LATS // GROUPS
PARTS = CHANNELS // GROUPS
SLOTS = DEGREES // GROUPS
COEFS = 2 * ORDERS
BLOCKS = ORDERS // 16
SPEC_ROWS = BAND * PARTS * 2
SENT_ROWS = 48
COT_CUTS = (0, 12, 36, 54)
SLOT_ROWS = SLOTS * PARTS * 2
LAST_ROWS = 40
HALF = GROUPS // 2
LOW = LATS // 2
REACH = [DEGREES // 2 - 8 * t for t in range(BLOCKS)]
STARTS = [16 * sum(REACH[:t]) for t in range(BLOCKS + 1)]
STEPS = [8 * LOW * t for t in range(BLOCKS + 1)]

f32 = jnp.float32
bf16 = jnp.bfloat16
TN = (((0,), (0,)), ((), ()))
NN = (((1,), (0,)), ((), ()))
NT = (((1,), (1,)), ((), ()))


def legendre_table():
    colatitude = np.pi * (np.arange(LATS) + 0.5) / LATS
    cosine, sine = np.cos(colatitude), np.sin(colatitude)
    order = np.arange(ORDERS, dtype=np.float64)[:, None]
    steps = np.arange(1, ORDERS)
    growth = np.concatenate([[0.0], np.cumsum(0.5 * np.log((2.0 * steps + 1.0) / (2.0 * steps)))])
    diagonal = np.exp(0.5 * np.log(1.0 / (4.0 * np.pi)) + growth[:, None] + order * np.log(sine))
    table = np.zeros((ORDERS, DEGREES, LATS))
    for degree in range(DEGREES):
        table[degree, degree] = diagonal[degree]
        if degree >= 1:
            m = degree - 1
            table[m, degree] = np.sqrt(2.0 * m + 3.0) * cosine * table[m, m]
        if degree >= 2:
            m = order[: degree - 1]
            lead = np.sqrt((4.0 * degree**2 - 1.0) / (degree**2 - m**2))
            back = np.sqrt(((degree - 1.0) ** 2 - m**2) / (4.0 * (degree - 1.0) ** 2 - 1.0))
            table[: degree - 1, degree] = lead * (
                cosine * table[: degree - 1, degree - 1] - back * table[: degree - 1, degree - 2]
            )
    return table, 2.0 * np.pi * np.pi / LATS * sine


def fourier_tables():
    lon = np.arange(LONS)[:, None]
    order = np.arange(ORDERS)[None, :]
    phase = 2.0 * np.pi * (lon * order % LONS) / LONS
    forward = np.stack([np.cos(phase), -np.sin(phase)], axis=2).reshape(LONS, COEFS) / LONS
    doubled = np.where(order == 0, 1.0, 2.0)
    inverse = np.stack([doubled * np.cos(phase), -doubled * np.sin(phase)], axis=2)
    return forward.astype(bf16), inverse.reshape(LONS, COEFS).astype(bf16)


@functools.cache
def constants():
    table, quadrature = legendre_table()
    low = (np.arange(HALF)[None, :] * BAND + np.arange(BAND)[:, None]).reshape(-1)

    def for_analysis(values):
        values = values.astype(bf16)
        return np.concatenate(
            [
                np.concatenate([values[16 * t + k + 8 * g, 16 * t + odd :: 2] for g in (0, 1)], axis=1)
                for t in range(BLOCKS)
                for odd in (0, 1)
                for k in range(8)
            ],
            axis=0,
        )

    analysis = for_analysis(table[:, :, low])
    weighted = for_analysis((table * quadrature)[:, :, low])
    below = table[:, :, low].astype(bf16)
    synthesis = np.concatenate(
        [
            np.concatenate([below[16 * t + k + 4 * g, odd::2].T for g in range(4)], axis=1)
            for t in range(BLOCKS)
            for odd in (0, 1)
            for k in range(4)
        ],
        axis=0,
    )
    forward, inverse = fourier_tables()
    turn = np.zeros((COEFS, COEFS), np.float32)
    even = np.arange(0, COEFS, 2)
    turn[even + 1, even] = -1.0
    turn[even, even + 1] = 1.0
    return dict(
        analysis=analysis,
        weighted=weighted,
        synthesis=synthesis,
        forward=forward,
        inverse=inverse,
        inverse_t=np.ascontiguousarray(inverse.T),
        turn=turn.astype(bf16),
        flip=np.eye(LOW)[::-1].astype(bf16),
        weight_rows=quadrature[low].astype(np.float32)[:, None],
    )


def dot(left, right, dims=NN):
    return lax.dot_general(left, right, dims, preferred_element_type=f32)


def lane_of(shape):
    return lax.broadcasted_iota(jnp.int32, shape, 1)


def join(pieces, lanes):
    rolled = [pltpu.roll(x, s % 128, 1) if s % 128 else x for x, s in pieces]
    left = jnp.where(lanes < 32, rolled[0], rolled[1])
    right = jnp.where(lanes < 96, rolled[2], rolled[3])
    return jnp.where(lanes < 64, left, right)


def join_two(first, shift_first, second, shift_second, lanes):
    a = pltpu.roll(first, shift_first % 128, 1) if shift_first % 128 else first
    b = pltpu.roll(second, shift_second % 128, 1) if shift_second % 128 else second
    return jnp.where(lanes < 64, a, b)


def to_tiles(parts):
    lanes = lane_of(parts[0][0].shape)
    tiles = []
    for pair in range(BLOCKS // 2):
        h, at = pair // 2, 64 * (pair % 2)
        x = [parts[q][h] for q in range(PARTS)]
        a = join([(x[s], 32 * s - at) for s in range(4)], lanes)
        c = join([(x[s], 32 * s - at - 32) for s in range(4)], lanes)
        b = join_two(x[4], -at, x[5], 64 - at, lanes)
        tiles.append((a, b, c))
    return tiles


def from_tiles(tiles):
    lanes = lane_of(tiles[0][0].shape)
    parts = []
    for q in range(4):
        halves = []
        for h in range(2):
            pieces = []
            for k in range(4):
                a, _, c = tiles[2 * h + k // 2]
                pieces.append((c if k % 2 else a, 32 * (k - q)))
            halves.append(join(pieces, lanes))
        parts.append(halves)
    parts.append([join_two(tiles[2 * h][1], 0, tiles[2 * h + 1][1], 64, lanes) for h in range(2)])
    parts.append([join_two(tiles[2 * h][1], 64, tiles[2 * h + 1][1], 0, lanes) for h in range(2)])
    return parts


def as_bf16(tiles):
    return [tuple(x.astype(bf16) for x in tile) for tile in tiles]


def block_operand(tiles, t):
    a, b, c = tiles[t // 2]
    return jnp.concatenate([c if t % 2 else a, b], axis=1)


def merge_blocks(sums):
    tiles = []
    for pair in range(BLOCKS // 2):
        one, two = sums[2 * pair], sums[2 * pair + 1]
        lanes = lane_of((one.shape[0], 128))
        b = jnp.where((lanes // 32) % 2 == 0, one[:, 128:], two[:, 128:])
        tiles.append((one[:, :128], b, two[:, :128]))
    return tiles


def order_sign(lanes):
    return jnp.where((lanes // 2) % 2 == 0, 1.0, -1.0).astype(f32)


def fold(pair, flip):
    x = jnp.concatenate(pair, axis=1)
    low = jnp.concatenate([x[i * GROUPS : i * GROUPS + HALF] for i in range(BAND)], axis=0)
    high = jnp.concatenate([x[i * GROUPS + HALF : (i + 1) * GROUPS] for i in range(BAND)], axis=0)
    high = dot(flip, high.astype(bf16)) * order_sign(lane_of(high.shape))
    both = (low.astype(bf16).astype(f32) + high, low.astype(bf16).astype(f32) - high)
    return [[x[:, :128], x[:, 128:]] for x in both]


def unfold(even, odd, flip, weight):
    even, odd = jnp.concatenate(even, axis=1), jnp.concatenate(odd, axis=1)
    low = even + odd
    high = (even - odd) * order_sign(lane_of(low.shape))
    if weight is not None:
        low, high = low * weight, high * weight
    high = dot(flip, high.astype(bf16))
    pieces = []
    for i in range(BAND):
        rows = slice(i * HALF, (i + 1) * HALF)
        pieces += [low[rows], high[rows]]
    whole = jnp.concatenate(pieces, axis=0)
    return tuple(whole[:, 128 * n : 128 * (n + 1)] for n in range(3))


def stacked(operand, groups, width):
    order = (lane_of(operand.shape) % 32) // 2
    none = jnp.zeros_like(operand)
    return jnp.concatenate(
        [jnp.where(order // width == g, operand, none) for g in range(groups)], axis=0
    )


def analyse(parts, flip, table, ready):
    folded = [fold(pair, flip) for pair in parts]
    tiles = [as_bf16(to_tiles([x[odd] for x in folded])) for odd in (0, 1)]
    sums = []
    for t in range(BLOCKS):
        ready(t)
        reach = REACH[t]
        order = (lane_of((reach, 256)) % 16) // 2
        pieces = []
        for odd in (0, 1):
            operand = stacked(block_operand(tiles[odd], t), 2, 8)
            rows = pl.ds(STARTS[t] + odd * 8 * reach, 8 * reach)
            part = dot(table[rows, :], operand)
            total = part[:reach]
            for k in range(1, 8):
                total = jnp.where(order == k, part[k * reach : (k + 1) * reach], total)
            if t:
                pieces.append(jnp.zeros((8 * t, 256), f32))
            pieces.append(total)
        sums.append(jnp.concatenate(pieces, axis=0))
    return merge_blocks(sums)


def synthesise(tiles, flip, weight, table, ready):
    sums = ([], [])
    order = (lane_of((LOW, 256)) % 8) // 2
    for t in range(BLOCKS):
        ready(t)
        operand = block_operand(tiles, t)
        for odd in (0, 1):
            rows = operand[odd * GROUPS : (odd + 1) * GROUPS]
            part = dot(table[pl.ds(STEPS[t] + odd * 4 * LOW, 4 * LOW), :], stacked(rows, 4, 4))
            total = part[:LOW]
            for k in range(1, 4):
                total = jnp.where(order == k, part[k * LOW : (k + 1) * LOW], total)
            sums[odd].append(total)
    even, odd = merge_blocks(sums[0]), merge_blocks(sums[1])
    return from_tiles([unfold(e, o, flip, weight) for e, o in zip(even, odd)])


def permute_rows(matrix, tiles):
    out = []
    for tile in tiles:
        moved = dot(matrix, jnp.concatenate(tile, axis=1))
        out.append(tuple(moved[:, 128 * n : 128 * (n + 1)] for n in range(3)))
    return out


def put_slots(parts, carried, stage, out):
    stride = SLOT_ROWS if carried is None else SENT_ROWS
    for j in range(SLOTS):
        for q in range(PARTS):
            for h in range(2):
                stage[pl.ds((j * PARTS + q) * 2 + h, GROUPS, stride=stride), :] = parts[q][h][
                    j * GROUPS : (j + 1) * GROUPS
                ]
    if carried is None:
        out[...] = stage[pl.ds(0, GROUPS * SLOT_ROWS), :].astype(bf16)
    else:
        rows = stage[...].reshape(GROUPS, SENT_ROWS, 128)[:, :SLOT_ROWS]
        more = carried[...].astype(f32).reshape(GROUPS, SLOT_ROWS, 128)
        both = jnp.concatenate([rows, more], axis=1)
        out[...] = both.reshape(GROUPS * SENT_ROWS, 128).astype(bf16)


def get_slots(received, stage):
    count = received.shape[0]
    stage[pl.ds(0, count), :] = received[...].astype(f32)
    return [
        [
            jnp.concatenate(
                [
                    stage[pl.ds((j * PARTS + q) * 2 + h, GROUPS, stride=count // GROUPS), :]
                    for j in range(SLOTS)
                ],
                axis=0,
            )
            for h in range(2)
        ]
        for q in range(PARTS)
    ]


def slot_rows_out(tiles, degree_col, carried, stage, out):
    row = lane_of((DEGREES, DEGREES))
    pick = (degree_col[...] == 2 * (row % GROUPS) + row // GROUPS).astype(f32).astype(bf16)
    put_slots(from_tiles(permute_rows(pick, as_bf16(tiles))), carried, stage, out)


def slot_rows_in(received, degree_row, stage):
    row = lax.broadcasted_iota(jnp.int32, (DEGREES, DEGREES), 0)
    pick = (degree_row[...] == 2 * (row % GROUPS) + row // GROUPS).astype(f32).astype(bf16)
    return as_bf16(permute_rows(pick, as_bf16(to_tiles(get_slots(received, stage)))))


def table_copies(source, target, sems, bounds):
    copies = []
    for t in range(BLOCKS):
        rows = pl.ds(bounds[t], bounds[t + 1] - bounds[t])
        copies.append(pltpu.make_async_copy(source.at[rows, :], target.at[rows, :], sems.at[t]))
    return copies


def cot_place(i, q, h):
    row = (i * PARTS + q) * 3 + h
    which = sum(row >= cut for cut in COT_CUTS[1:3])
    return which, row - COT_CUTS[which]


def spread_kernel(
    fields, cotangent, forward_source, out, cot_two, cot_three, field, cot, forward, stages, sems
):
    copies = []
    fetch = pltpu.make_async_copy(forward_source, forward, sems.at[2 * BAND])
    fetch.start()
    for i in range(BAND):
        copies.append(
            (
                pltpu.make_async_copy(fields.at[i], field.at[i], sems.at[2 * i]),
                pltpu.make_async_copy(cotangent.at[i], cot.at[i], sems.at[2 * i + 1]),
            )
        )
    for pair in copies:
        for copy in pair:
            copy.start()
    stage, stage_two, stage_three = stages.at[0], stages.at[1], stages.at[2]
    spots = ((stage, SPEC_ROWS, SENT_ROWS), (stage_two, 0, SLOT_ROWS), (stage_three, 0, SLOT_ROWS))
    for i in range(BAND):
        if i == 0:
            fetch.wait()
        copies[i][0].wait()
        spectra = dot(field[i], forward[...], TN)
        for q in range(PARTS):
            rows = slice(q * GROUPS, (q + 1) * GROUPS)
            at = (i * PARTS + q) * 2
            for h in range(2):
                stage[pl.ds(at + h, GROUPS, stride=SENT_ROWS), :] = spectra[
                    rows, 128 * h : 128 * (h + 1)
                ]
        copies[i][1].wait()
        turned = jnp.transpose(cot[i].astype(f32))
        for q in range(PARTS):
            rows = slice(q * GROUPS, (q + 1) * GROUPS)
            for h in range(3):
                which, at = cot_place(i, q, h)
                place, base, stride = spots[which]
                place[pl.ds(base + at, GROUPS, stride=stride), :] = turned[
                    rows, 128 * h : 128 * (h + 1)
                ]
    for row in range(COT_CUTS[3] - COT_CUTS[2], SLOT_ROWS):
        stage_three[pl.ds(row, GROUPS, stride=SLOT_ROWS), :] = jnp.zeros((GROUPS, 128), f32)
    out[...] = stage[...].astype(bf16)
    short = GROUPS * SLOT_ROWS
    cot_two[...] = stage_two[pl.ds(0, short), :].astype(bf16)
    cot_three[...] = stage_three[pl.ds(0, short), :].astype(bf16)


def first_kernel(
    received, analysis, degree_col, flip, carried, early, out, stage_in, stage, table, sems
):
    copies = table_copies(analysis, table, sems, STARTS)
    for copy in copies:
        copy.start()
    stage_in[...] = received[...].astype(f32)
    parts = [
        [
            jnp.concatenate(
                [
                    stage_in[pl.ds((i * PARTS + q) * 2 + h, GROUPS, stride=SENT_ROWS), :]
                    for i in range(BAND)
                ],
                axis=0,
            )
            for h in range(2)
        ]
        for q in range(PARTS)
    ]
    sums = analyse(parts, flip[...], table, lambda t: copies[t].wait())
    slot_rows_out(sums, degree_col, carried, stage, out)


def gelu_slope(x):
    c = np.float32(np.sqrt(2.0 / np.pi))
    squared = x * x
    th = jnp.tanh(c * (x + 0.044715 * (x * squared)))
    return 0.5 * (1.0 + th) + (0.5 * c) * x * (1.0 - th * th) * (1.0 + (3 * 0.044715) * squared)


def middle_kernel(
    received, one, two, analysis, synthesis, degree_row, degree_col, flip, inverse_source, turned_source, out,
    inverse, inverse_t, rows_one, rows_two, stage_one, stage_two, stage, table, table_s, row_sems, sems, sems_s,
):
    copies_s = table_copies(synthesis, table_s, sems_s, STEPS)
    copies = table_copies(analysis, table, sems, STARTS)
    fetches = (
        pltpu.make_async_copy(one.at[:, pl.ds(32, 16), :], rows_one, row_sems.at[0]),
        pltpu.make_async_copy(two.at[:, pl.ds(16, 32), :], rows_two, row_sems.at[1]),
        pltpu.make_async_copy(inverse_source, inverse, row_sems.at[2]),
        pltpu.make_async_copy(turned_source, inverse_t, row_sems.at[3]),
    )
    for copy in (*copies_s, *fetches, *copies):
        copy.start()
    tiles = slot_rows_in(received, degree_row, stage)
    synth = synthesise(tiles, flip[...], None, table_s, lambda t: copies_s[t].wait())
    for fetch in fetches:
        fetch.wait()
    stage_one[...] = rows_one[...].astype(f32).reshape(GROUPS * 16, 128)
    stage_two[...] = rows_two[...].astype(f32).reshape(GROUPS * 32, 128)
    spots = ((stage_one, SPEC_ROWS - 32, 16), (stage_two, 8, 32), (stage, SLOT_ROWS, SENT_ROWS))

    def cot_rows(i, q, h):
        which, at = cot_place(i, q, h)
        place, base, stride = spots[which]
        return place[pl.ds(base + at, GROUPS, stride=stride), :]

    parts = []
    for q in range(PARTS):
        response = dot(jnp.concatenate(synth[q], axis=1).astype(bf16), inverse_t[...])
        cotangent = jnp.concatenate(
            [
                jnp.concatenate([cot_rows(i, q, h) for h in range(3)], axis=1)
                for i in range(BAND)
            ],
            axis=0,
        )
        upstream = (cotangent * gelu_slope(response)).astype(bf16)
        grad = dot(upstream, inverse[...])
        parts.append([grad[:, :128], grad[:, 128:]])
    sums = analyse(parts, flip[...], table, lambda t: copies[t].wait())
    slot_rows_out(sums, degree_col, None, stage, out)


def last_kernel(received, synthesis, degree_row, weight_rows, flip, out, stage, stage_out, table_s, sems_s):
    copies_s = table_copies(synthesis, table_s, sems_s, STEPS)
    for copy in copies_s:
        copy.start()
    tiles = slot_rows_in(received, degree_row, stage)
    synth = synthesise(
        tiles, flip[...], weight_rows[...], table_s, lambda t: copies_s[t].wait()
    )
    for q in range(PARTS):
        for h in range(2):
            scaled = synth[q][h]
            for i in range(BAND):
                at = (i * PARTS + q) * 2 + h
                stage_out[pl.ds(at, GROUPS, stride=LAST_ROWS), :] = scaled[
                    i * GROUPS : (i + 1) * GROUPS
                ]
    for row in range(SPEC_ROWS, LAST_ROWS):
        stage_out[pl.ds(row, GROUPS, stride=LAST_ROWS), :] = jnp.zeros((GROUPS, 128), f32)
    out[...] = stage_out[...].astype(bf16)


def gather_kernel(received, forward, cotangent, weight_grads, out, stage):
    stage[...] = received[...].astype(f32)
    for i in range(BAND):
        halves = [
            jnp.concatenate(
                [
                    stage[pl.ds((i * PARTS + q) * 2 + h, GROUPS, stride=LAST_ROWS), :]
                    for q in range(PARTS)
                ],
                axis=0,
            )
            for h in range(2)
        ]
        rows = jnp.concatenate(halves, axis=1).astype(bf16)
        delta = dot(forward[...], rows, NT)
        out[i] = (cotangent[i].astype(f32) + delta).astype(bf16)


def mix_kernel(adjoint, received, weights, turn, *rest):
    carried, out, kept, stage = (None, *rest) if adjoint else rest
    parts = get_slots(received, stage)
    results = []
    for j in range(SLOTS):
        own = slice(j * GROUPS, (j + 1) * GROUPS)
        held = jnp.concatenate(
            [jnp.concatenate([x[own] for x in parts[q]], axis=1) for q in range(PARTS)], axis=0
        ).astype(bf16)
        kept[j] = held
        turned = dot(held, turn[...])
        if adjoint:
            turned = -turned
        turned = turned.astype(bf16)
        results.append(dot(weights[j, 0], held) + dot(weights[j, 1], turned))
    mixed = [
        [
            jnp.concatenate(
                [x[q * GROUPS : (q + 1) * GROUPS, 128 * h : 128 * (h + 1)] for x in results],
                axis=0,
            )
            for h in range(2)
        ]
        for q in range(PARTS)
    ]
    put_slots(mixed, carried, stage, out)


VMEM = pl.BlockSpec(memory_space=pltpu.VMEM)
SMEM = pl.BlockSpec(memory_space=pltpu.SMEM)
ANY = pl.BlockSpec(memory_space=pl.ANY)


def call(kernel, out_shape, in_specs, scratch, flops, moved, name, limit=24):
    several = isinstance(out_shape, list)
    return pl.pallas_call(
        kernel,
        out_shape=out_shape,
        in_specs=in_specs,
        out_specs=[VMEM] * len(out_shape) if several else VMEM,
        scratch_shapes=scratch,
        compiler_params=pltpu.CompilerParams(vmem_limit_bytes=limit * 2**20),
        cost_estimate=pl.CostEstimate(flops=flops, bytes_accessed=moved, transcendentals=0),
        name=name,
    )


def message(rows):
    return jax.ShapeDtypeStruct((GROUPS * rows, 128), bf16)


def stage_of(rows):
    return pltpu.VMEM((GROUPS * rows, 128), f32)


TABLE = pltpu.VMEM((STARTS[-1], LATS), bf16)
TABLE_S = pltpu.VMEM((STEPS[-1], 256), bf16)


def sems(count):
    return pltpu.SemaphoreType.DMA((count,))


def in_hbm(array):
    return pltpu.with_memory_space_constraint(array, pltpu.HBM)


def spread(fields, cotangent, forward):
    cycle = pltpu.VMEM((BAND, LONS, CHANNELS), bf16)
    return call(
        spread_kernel,
        [message(SENT_ROWS), message(SLOT_ROWS), message(SLOT_ROWS)],
        [ANY, ANY, ANY],
        [
            cycle, cycle, pltpu.VMEM((LONS, COEFS), bf16),
            pltpu.VMEM((3, GROUPS * SENT_ROWS, 128), f32), sems(2 * BAND + 1),
        ],
        3 * 10**8, 4 * 10**6, "spread",
    )(in_hbm(fields), in_hbm(cotangent), in_hbm(forward))


def first(received, weighted, degree_col, flip, carried, early):
    return call(
        first_kernel,
        message(SENT_ROWS),
        [VMEM, ANY, VMEM, VMEM, VMEM, ANY],
        [stage_of(SENT_ROWS), stage_of(SENT_ROWS), TABLE, sems(BLOCKS)],
        10**9, 6 * 10**6, "first",
    )(received, in_hbm(weighted), degree_col, flip, carried, early)


def middle(
    received, one, two, analysis, synthesis, degree_row, degree_col, flip, inverse, inverse_t
):
    return call(
        middle_kernel,
        message(SLOT_ROWS),
        [VMEM, ANY, ANY, ANY, ANY, VMEM, VMEM, VMEM, ANY, ANY],
        [
            pltpu.VMEM((LONS, COEFS), bf16), pltpu.VMEM((COEFS, LONS), bf16),
            pltpu.VMEM((GROUPS, 16, 128), bf16), pltpu.VMEM((GROUPS, 32, 128), bf16),
            stage_of(16), stage_of(32), stage_of(SENT_ROWS),
            TABLE, TABLE_S, sems(4), sems(BLOCKS), sems(BLOCKS),
        ],
        3 * 10**9, 12 * 10**6, "middle",
    )(received, one, two, in_hbm(analysis), in_hbm(synthesis), degree_row, degree_col, flip,
      in_hbm(inverse), in_hbm(inverse_t))


def last(received, synthesis, degree_row, weight_rows, flip):
    return call(
        last_kernel,
        message(LAST_ROWS),
        [VMEM, ANY, VMEM, VMEM, VMEM],
        [stage_of(SLOT_ROWS), stage_of(LAST_ROWS), TABLE_S, sems(BLOCKS)],
        10**9, 7 * 10**6, "last",
    )(received, in_hbm(synthesis), degree_row, weight_rows, flip)


def gather(received, forward, cotangent, weight_grads):
    return call(
        gather_kernel,
        jax.ShapeDtypeStruct((BAND, LONS, CHANNELS), bf16),
        [VMEM, VMEM, VMEM, ANY],
        [stage_of(LAST_ROWS)],
        3 * 10**8, 3 * 10**6, "gather",
    )(received, forward, cotangent, in_hbm(weight_grads))


def mix(adjoint, received, weights, turn, *carried):
    rows = SLOT_ROWS if adjoint else SENT_ROWS
    return call(
        functools.partial(mix_kernel, adjoint),
        [message(rows), jax.ShapeDtypeStruct((SLOTS, CHANNELS, COEFS), bf16)],
        [VMEM, VMEM, VMEM] + [VMEM] * len(carried),
        [stage_of(rows)],
        6 * 10**8, 3 * 10**6, "adjoint_mix" if adjoint else "mix",
    )(received, weights, turn, *carried)


def exchange(rows):
    count = rows.shape[0] // GROUPS
    out = lax.all_to_all(
        rows.reshape(GROUPS, count, 128), "lat", split_axis=0, concat_axis=0, tiled=True,
    )
    return out.reshape(GROUPS * count, 128)


def gradient_kernel(coeffs_source, grads_source, turn, out, coeffs, grads, sems):
    copies = []
    for j in range(SLOTS):
        copies.append(
            [
                pltpu.make_async_copy(source.at[:, j], held.at[:, j], sems.at[2 * j + n])
                for n, (source, held) in enumerate(((coeffs_source, coeffs), (grads_source, grads)))
            ]
        )
    for pair in copies:
        for copy in pair:
            copy.start()
    samples = range(coeffs.shape[0])
    for j in range(SLOTS):
        copies[j][0].wait()
        left = [coeffs[s, j] for s in samples]
        turned = [dot(x, turn[...]).astype(bf16) for x in left]
        copies[j][1].wait()
        right = jnp.concatenate([grads[s, j] for s in samples], axis=1)
        out[j, 0] = dot(jnp.concatenate(left, axis=1), right, NT).astype(bf16)
        out[j, 1] = dot(jnp.concatenate(turned, axis=1), right, NT).astype(bf16)


def weight_gradient(coeffs, grads, turn):
    held = pltpu.VMEM(coeffs.shape, bf16)
    return call(
        gradient_kernel,
        jax.ShapeDtypeStruct((SLOTS, 2, CHANNELS, CHANNELS), bf16),
        [ANY, ANY, VMEM],
        [held, held, sems(2 * SLOTS)],
        5 * 10**9, 8 * 10**6, "weight_gradient",
    )(in_hbm(coeffs), in_hbm(grads), turn)


def local(fields, cotangent, weights, degree_of):
    table = {k: jnp.asarray(v) for k, v in constants().items()}
    slots = degree_of.reshape(GROUPS, SLOTS).T.reshape(DEGREES)
    degree_col, degree_row = slots[:, None], slots[None, :]
    turned_weights = jnp.swapaxes(weights, 2, 3)
    sent, cot_two, cot_three = spread(fields[0], cotangent[0], table["forward"])
    one = exchange(sent)
    two = exchange(first(one, table["weighted"], degree_col, table["flip"], cot_two, turned_weights))
    filtered, coeffs = mix(False, two, turned_weights, table["turn"], cot_three)
    all_coeffs = lax.all_gather(coeffs, "batch", axis=0)
    three = exchange(filtered)
    as_sent = (GROUPS, SENT_ROWS, 128)
    four = exchange(
        middle(
            three, one.reshape(as_sent), two.reshape(as_sent), table["analysis"],
            table["synthesis"], degree_row, degree_col, table["flip"],
            table["inverse"], table["inverse_t"],
        )
    )
    grad_coeffs, grads = mix(True, four, weights, table["turn"])
    all_grads = lax.all_gather(grads, "batch", axis=0)
    grad_weights = weight_gradient(all_coeffs, all_grads, table["turn"])
    five = exchange(grad_coeffs)
    six = exchange(last(five, table["synthesis"], degree_row, table["weight_rows"], table["flip"]))
    grad_fields = gather(six, table["forward"], cotangent[0], grad_weights)[None]
    return grad_fields, grad_weights


def solution(mesh):
    return jax.shard_map(
        local,
        mesh=mesh,
        in_specs=(
            P("batch", "lat", None, None),
            P("batch", "lat", None, None),
            P("lat", None, None, None),
            P(),
        ),
        out_specs=(P("batch", "lat", None, None), P("lat", None, None, None)),
        check_vma=False,
    )
```

```python
import functools

import jax
import jax.numpy as jnp
import numpy as np
from jax import lax
from jax.experimental import pallas as pl
from jax.experimental.pallas import tpu as pltpu
from jax.sharding import PartitionSpec as P

LATS = 192
LONS = 384
ORDERS = 128
DEGREES = 128
CHANNELS = 384

GROUPS = 64
BAND = LATS // GROUPS
PARTS = CHANNELS // GROUPS
SLOTS = DEGREES // GROUPS
COEFS = 2 * ORDERS
BLOCKS = ORDERS // 16
SPEC_ROWS = BAND * PARTS * 2
SENT_ROWS = 48
COT_CUTS = (0, 12, 36, 54)
SLOT_ROWS = SLOTS * PARTS * 2
LAST_ROWS = 40
HALF = GROUPS // 2
LOW = LATS // 2
REACH = [DEGREES // 2 - 8 * t for t in range(BLOCKS)]
STARTS = [16 * sum(REACH[:t]) for t in range(BLOCKS + 1)]
STEPS = [8 * LOW * t for t in range(BLOCKS + 1)]

f32 = jnp.float32
bf16 = jnp.bfloat16
TN = (((0,), (0,)), ((), ()))
NN = (((1,), (0,)), ((), ()))
NT = (((1,), (1,)), ((), ()))


def legendre_table():
    colatitude = np.pi * (np.arange(LATS) + 0.5) / LATS
    cosine, sine = np.cos(colatitude), np.sin(colatitude)
    order = np.arange(ORDERS, dtype=np.float64)[:, None]
    steps = np.arange(1, ORDERS)
    growth = np.concatenate([[0.0], np.cumsum(0.5 * np.log((2.0 * steps + 1.0) / (2.0 * steps)))])
    diagonal = np.exp(0.5 * np.log(1.0 / (4.0 * np.pi)) + growth[:, None] + order * np.log(sine))
    table = np.zeros((ORDERS, DEGREES, LATS))
    for degree in range(DEGREES):
        table[degree, degree] = diagonal[degree]
        if degree >= 1:
            m = degree - 1
            table[m, degree] = np.sqrt(2.0 * m + 3.0) * cosine * table[m, m]
        if degree >= 2:
            m = order[: degree - 1]
            lead = np.sqrt((4.0 * degree**2 - 1.0) / (degree**2 - m**2))
            back = np.sqrt(((degree - 1.0) ** 2 - m**2) / (4.0 * (degree - 1.0) ** 2 - 1.0))
            table[: degree - 1, degree] = lead * (
                cosine * table[: degree - 1, degree - 1] - back * table[: degree - 1, degree - 2]
            )
    return table, 2.0 * np.pi * np.pi / LATS * sine


def fourier_tables():
    lon = np.arange(LONS)[:, None]
    order = np.arange(ORDERS)[None, :]
    phase = 2.0 * np.pi * (lon * order % LONS) / LONS
    forward = np.stack([np.cos(phase), -np.sin(phase)], axis=2).reshape(LONS, COEFS) / LONS
    doubled = np.where(order == 0, 1.0, 2.0)
    inverse = np.stack([doubled * np.cos(phase), -doubled * np.sin(phase)], axis=2)
    return forward.astype(bf16), inverse.reshape(LONS, COEFS).astype(bf16)


@functools.cache
def constants():
    table, quadrature = legendre_table()
    low = (np.arange(HALF)[None, :] * BAND + np.arange(BAND)[:, None]).reshape(-1)

    def for_analysis(values):
        values = values.astype(bf16)
        return np.concatenate(
            [
                np.concatenate([values[16 * t + k + 8 * g, 16 * t + odd :: 2] for g in (0, 1)], axis=1)
                for t in range(BLOCKS)
                for odd in (0, 1)
                for k in range(8)
            ],
            axis=0,
        )

    analysis = for_analysis(table[:, :, low])
    weighted = for_analysis((table * quadrature)[:, :, low])

    def for_synthesis(values):
        values = values.astype(bf16)
        return np.concatenate(
            [
                np.concatenate([values[16 * t + k + 4 * g, odd::2].T for g in range(4)], axis=1)
                for t in range(BLOCKS)
                for odd in (0, 1)
                for k in range(4)
            ],
            axis=0,
        )

    synthesis = for_synthesis(table[:, :, low])
    weighted_synthesis = for_synthesis((table * quadrature)[:, :, low])
    forward, inverse = fourier_tables()
    turn = np.zeros((COEFS, COEFS), np.float32)
    even = np.arange(0, COEFS, 2)
    turn[even + 1, even] = -1.0
    turn[even, even + 1] = 1.0
    return dict(
        analysis=analysis,
        weighted=weighted,
        synthesis=synthesis,
        weighted_synthesis=weighted_synthesis,
        forward=forward,
        inverse=inverse,
        inverse_t=np.ascontiguousarray(inverse.T),
        turn=turn.astype(bf16),
    )


def dot(left, right, dims=NN):
    return lax.dot_general(left, right, dims, preferred_element_type=f32)


def lane_of(shape):
    return lax.broadcasted_iota(jnp.int32, shape, 1)


def join(pieces, lanes):
    rolled = [pltpu.roll(x, s % 128, 1) if s % 128 else x for x, s in pieces]
    left = jnp.where(lanes < 32, rolled[0], rolled[1])
    right = jnp.where(lanes < 96, rolled[2], rolled[3])
    return jnp.where(lanes < 64, left, right)


def join_two(first, shift_first, second, shift_second, lanes):
    a = pltpu.roll(first, shift_first % 128, 1) if shift_first % 128 else first
    b = pltpu.roll(second, shift_second % 128, 1) if shift_second % 128 else second
    return jnp.where(lanes < 64, a, b)


def to_tiles(parts):
    lanes = lane_of(parts[0][0].shape)
    tiles = []
    for pair in range(BLOCKS // 2):
        h, at = pair // 2, 64 * (pair % 2)
        x = [parts[q][h] for q in range(PARTS)]
        a = join([(x[s], 32 * s - at) for s in range(4)], lanes)
        c = join([(x[s], 32 * s - at - 32) for s in range(4)], lanes)
        b = join_two(x[4], -at, x[5], 64 - at, lanes)
        tiles.append((a, b, c))
    return tiles


def from_tiles(tiles):
    lanes = lane_of(tiles[0][0].shape)
    parts = []
    for q in range(4):
        halves = []
        for h in range(2):
            pieces = []
            for k in range(4):
                a, _, c = tiles[2 * h + k // 2]
                pieces.append((c if k % 2 else a, 32 * (k - q)))
            halves.append(join(pieces, lanes))
        parts.append(halves)
    parts.append([join_two(tiles[2 * h][1], 0, tiles[2 * h + 1][1], 64, lanes) for h in range(2)])
    parts.append([join_two(tiles[2 * h][1], 64, tiles[2 * h + 1][1], 0, lanes) for h in range(2)])
    return parts


def as_bf16(tiles):
    return [tuple(x.astype(bf16) for x in tile) for tile in tiles]


def block_operand(tiles, t):
    a, b, c = tiles[t // 2]
    return jnp.concatenate([c if t % 2 else a, b], axis=1)


def merge_blocks(sums):
    tiles = []
    for pair in range(BLOCKS // 2):
        one, two = sums[2 * pair], sums[2 * pair + 1]
        lanes = lane_of((one.shape[0], 128))
        b = jnp.where((lanes // 32) % 2 == 0, one[:, 128:], two[:, 128:])
        tiles.append((one[:, :128], b, two[:, :128]))
    return tiles


def order_sign(lanes):
    return jnp.where((lanes // 2) % 2 == 0, 1.0, -1.0).astype(f32)


def reversal():
    row = lax.broadcasted_iota(jnp.int32, (LOW, LOW), 0)
    return (row + lane_of((LOW, LOW)) == LOW - 1).astype(f32).astype(bf16)


def fold(pair, flip):
    x = jnp.concatenate(pair, axis=1)
    low = jnp.concatenate([x[i * GROUPS : i * GROUPS + HALF] for i in range(BAND)], axis=0)
    high = jnp.concatenate([x[i * GROUPS + HALF : (i + 1) * GROUPS] for i in range(BAND)], axis=0)
    high = dot(flip, high.astype(bf16)) * order_sign(lane_of(high.shape))
    both = (low.astype(bf16).astype(f32) + high, low.astype(bf16).astype(f32) - high)
    return [[x[:, :128], x[:, 128:]] for x in both]


def unfold(even, odd, flip):
    even, odd = jnp.concatenate(even, axis=1), jnp.concatenate(odd, axis=1)
    low = even + odd
    high = (even - odd) * order_sign(lane_of(low.shape))
    high = dot(flip, high.astype(bf16))
    pieces = []
    for i in range(BAND):
        rows = slice(i * HALF, (i + 1) * HALF)
        pieces += [low[rows], high[rows]]
    whole = jnp.concatenate(pieces, axis=0)
    return tuple(whole[:, 128 * n : 128 * (n + 1)] for n in range(3))


def stacked(operand, groups, width):
    order = (lane_of(operand.shape) % 32) // 2
    none = jnp.zeros_like(operand)
    return jnp.concatenate(
        [jnp.where(order // width == g, operand, none) for g in range(groups)], axis=0
    )


def analyse(parts, flip, table, ready):
    folded = [fold(pair, flip) for pair in parts]
    tiles = [as_bf16(to_tiles([x[odd] for x in folded])) for odd in (0, 1)]
    sums = []
    for t in range(BLOCKS):
        ready(t)
        reach = REACH[t]
        order = (lane_of((reach, 256)) % 16) // 2
        pieces = []
        for odd in (0, 1):
            operand = stacked(block_operand(tiles[odd], t), 2, 8)
            rows = pl.ds(STARTS[t] + odd * 8 * reach, 8 * reach)
            part = dot(table[rows, :], operand)
            total = part[:reach]
            for k in range(1, 8):
                total = jnp.where(order == k, part[k * reach : (k + 1) * reach], total)
            if t:
                pieces.append(jnp.zeros((8 * t, 256), f32))
            pieces.append(total)
        sums.append(jnp.concatenate(pieces, axis=0))
    return merge_blocks(sums)


def synthesise(tiles, table, ready):
    sums = ([], [])
    order = (lane_of((LOW, 256)) % 8) // 2
    for t in range(BLOCKS):
        ready(t)
        operand = block_operand(tiles, t)
        for odd in (0, 1):
            rows = operand[odd * GROUPS : (odd + 1) * GROUPS]
            part = dot(table[pl.ds(STEPS[t] + odd * 4 * LOW, 4 * LOW), :], stacked(rows, 4, 4))
            total = part[:LOW]
            for k in range(1, 4):
                total = jnp.where(order == k, part[k * LOW : (k + 1) * LOW], total)
            sums[odd].append(total)
    even, odd = merge_blocks(sums[0]), merge_blocks(sums[1])
    flip = reversal()
    return from_tiles([unfold(e, o, flip) for e, o in zip(even, odd)])


def permute_rows(matrix, tiles):
    out = []
    for tile in tiles:
        moved = dot(matrix, jnp.concatenate(tile, axis=1))
        out.append(tuple(moved[:, 128 * n : 128 * (n + 1)] for n in range(3)))
    return out


def put_slots(parts, carried, stage, out):
    stride = SLOT_ROWS if carried is None else SENT_ROWS
    for j in range(SLOTS):
        for q in range(PARTS):
            for h in range(2):
                stage[pl.ds((j * PARTS + q) * 2 + h, GROUPS, stride=stride), :] = parts[q][h][
                    j * GROUPS : (j + 1) * GROUPS
                ]
    if carried is None:
        out[...] = stage[pl.ds(0, GROUPS * SLOT_ROWS), :].astype(bf16)
    else:
        rows = stage[...].reshape(GROUPS, SENT_ROWS, 128)[:, :SLOT_ROWS]
        more = carried[...].astype(f32).reshape(GROUPS, SLOT_ROWS, 128)
        both = jnp.concatenate([rows, more], axis=1)
        out[...] = both.reshape(GROUPS * SENT_ROWS, 128).astype(bf16)


def get_slots(received, stage):
    count = received.shape[0]
    stage[pl.ds(0, count), :] = received[...].astype(f32)
    return [
        [
            jnp.concatenate(
                [
                    stage[pl.ds((j * PARTS + q) * 2 + h, GROUPS, stride=count // GROUPS), :]
                    for j in range(SLOTS)
                ],
                axis=0,
            )
            for h in range(2)
        ]
        for q in range(PARTS)
    ]


def slot_rows_out(tiles, degree_col, carried, stage, out):
    row = lane_of((DEGREES, DEGREES))
    pick = (degree_col[...] == 2 * (row % GROUPS) + row // GROUPS).astype(f32).astype(bf16)
    put_slots(from_tiles(permute_rows(pick, as_bf16(tiles))), carried, stage, out)


def slot_rows_in(received, degree_row, stage):
    row = lax.broadcasted_iota(jnp.int32, (DEGREES, DEGREES), 0)
    pick = (degree_row[...] == 2 * (row % GROUPS) + row // GROUPS).astype(f32).astype(bf16)
    return as_bf16(permute_rows(pick, as_bf16(to_tiles(get_slots(received, stage)))))


def table_copies(source, target, sems, bounds):
    copies = []
    for t in range(BLOCKS):
        rows = pl.ds(bounds[t], bounds[t + 1] - bounds[t])
        copies.append(pltpu.make_async_copy(source.at[rows, :], target.at[rows, :], sems.at[t]))
    return copies


def cot_place(i, q, h):
    row = (i * PARTS + q) * 3 + h
    which = sum(row >= cut for cut in COT_CUTS[1:3])
    return which, row - COT_CUTS[which]


def spread_kernel(
    fields, cotangent, forward_source, out, cot_two, cot_three, field, cot, forward, stages, sems
):
    copies = []
    fetch = pltpu.make_async_copy(forward_source, forward, sems.at[2 * BAND])
    fetch.start()
    for i in range(BAND):
        copies.append(
            (
                pltpu.make_async_copy(fields.at[i], field.at[i], sems.at[2 * i]),
                pltpu.make_async_copy(cotangent.at[i], cot.at[i], sems.at[2 * i + 1]),
            )
        )
    for pair in copies:
        for copy in pair:
            copy.start()
    stage, stage_two, stage_three = stages.at[0], stages.at[1], stages.at[2]
    spots = ((stage, SPEC_ROWS, SENT_ROWS), (stage_two, 0, SLOT_ROWS), (stage_three, 0, SLOT_ROWS))
    for i in range(BAND):
        if i == 0:
            fetch.wait()
        copies[i][0].wait()
        spectra = dot(field[i], forward[...], TN)
        for q in range(PARTS):
            rows = slice(q * GROUPS, (q + 1) * GROUPS)
            at = (i * PARTS + q) * 2
            for h in range(2):
                stage[pl.ds(at + h, GROUPS, stride=SENT_ROWS), :] = spectra[
                    rows, 128 * h : 128 * (h + 1)
                ]
        copies[i][1].wait()
        turned = jnp.transpose(cot[i].astype(f32))
        for q in range(PARTS):
            rows = slice(q * GROUPS, (q + 1) * GROUPS)
            for h in range(3):
                which, at = cot_place(i, q, h)
                place, base, stride = spots[which]
                place[pl.ds(base + at, GROUPS, stride=stride), :] = turned[
                    rows, 128 * h : 128 * (h + 1)
                ]
    for row in range(COT_CUTS[3] - COT_CUTS[2], SLOT_ROWS):
        stage_three[pl.ds(row, GROUPS, stride=SLOT_ROWS), :] = jnp.zeros((GROUPS, 128), f32)
    out[...] = stage[...].astype(bf16)
    short = GROUPS * SLOT_ROWS
    cot_two[...] = stage_two[pl.ds(0, short), :].astype(bf16)
    cot_three[...] = stage_three[pl.ds(0, short), :].astype(bf16)


def first_kernel(
    received, analysis, degree_col, carried, early, out, stage_in, stage, table, sems
):
    copies = table_copies(analysis, table, sems, STARTS)
    for copy in copies:
        copy.start()
    stage_in[...] = received[...].astype(f32)
    parts = [
        [
            jnp.concatenate(
                [
                    stage_in[pl.ds((i * PARTS + q) * 2 + h, GROUPS, stride=SENT_ROWS), :]
                    for i in range(BAND)
                ],
                axis=0,
            )
            for h in range(2)
        ]
        for q in range(PARTS)
    ]
    sums = analyse(parts, reversal(), table, lambda t: copies[t].wait())
    slot_rows_out(sums, degree_col, carried, stage, out)


def gelu_slope(x):
    c = np.float32(np.sqrt(2.0 / np.pi))
    squared = x * x
    th = jnp.tanh(c * (x + 0.044715 * (x * squared)))
    return 0.5 * (1.0 + th) + (0.5 * c) * x * (1.0 - th * th) * (1.0 + (3 * 0.044715) * squared)


def middle_kernel(
    received, one, two, analysis, synthesis, degree_row, degree_col, inverse_source, turned_source, out,
    inverse, inverse_t, rows_one, rows_two, stage_one, stage_two, stage, table, table_s, row_sems, sems, sems_s,
):
    copies_s = table_copies(synthesis, table_s, sems_s, STEPS)
    copies = table_copies(analysis, table, sems, STARTS)
    fetches = (
        pltpu.make_async_copy(one.at[:, pl.ds(32, 16), :], rows_one, row_sems.at[0]),
        pltpu.make_async_copy(two.at[:, pl.ds(16, 32), :], rows_two, row_sems.at[1]),
        pltpu.make_async_copy(inverse_source, inverse, row_sems.at[2]),
        pltpu.make_async_copy(turned_source, inverse_t, row_sems.at[3]),
    )
    for copy in (*copies_s, *fetches, *copies):
        copy.start()
    tiles = slot_rows_in(received, degree_row, stage)
    synth = synthesise(tiles, table_s, lambda t: copies_s[t].wait())
    for fetch in fetches:
        fetch.wait()
    stage_one[...] = rows_one[...].astype(f32).reshape(GROUPS * 16, 128)
    stage_two[...] = rows_two[...].astype(f32).reshape(GROUPS * 32, 128)
    spots = ((stage_one, SPEC_ROWS - 32, 16), (stage_two, 8, 32), (stage, SLOT_ROWS, SENT_ROWS))

    def cot_rows(i, q, h):
        which, at = cot_place(i, q, h)
        place, base, stride = spots[which]
        return place[pl.ds(base + at, GROUPS, stride=stride), :]

    parts = []
    for q in range(PARTS):
        response = dot(jnp.concatenate(synth[q], axis=1).astype(bf16), inverse_t[...])
        cotangent = jnp.concatenate(
            [
                jnp.concatenate([cot_rows(i, q, h) for h in range(3)], axis=1)
                for i in range(BAND)
            ],
            axis=0,
        )
        upstream = (cotangent * gelu_slope(response)).astype(bf16)
        grad = dot(upstream, inverse[...])
        parts.append([grad[:, :128], grad[:, 128:]])
    sums = analyse(parts, reversal(), table, lambda t: copies[t].wait())
    slot_rows_out(sums, degree_col, None, stage, out)


def last_kernel(received, table, degree_row, out, stage, stage_out):
    tiles = slot_rows_in(received, degree_row, stage)
    synth = synthesise(tiles, table, lambda t: None)
    for q in range(PARTS):
        for h in range(2):
            scaled = synth[q][h]
            for i in range(BAND):
                at = (i * PARTS + q) * 2 + h
                stage_out[pl.ds(at, GROUPS, stride=LAST_ROWS), :] = scaled[
                    i * GROUPS : (i + 1) * GROUPS
                ]
    for row in range(SPEC_ROWS, LAST_ROWS):
        stage_out[pl.ds(row, GROUPS, stride=LAST_ROWS), :] = jnp.zeros((GROUPS, 128), f32)
    out[...] = stage_out[...].astype(bf16)


def gather_kernel(received, forward, cotangent, weight_grads, out, stage):
    stage[...] = received[...].astype(f32)
    for i in range(BAND):
        halves = [
            jnp.concatenate(
                [
                    stage[pl.ds((i * PARTS + q) * 2 + h, GROUPS, stride=LAST_ROWS), :]
                    for q in range(PARTS)
                ],
                axis=0,
            )
            for h in range(2)
        ]
        rows = jnp.concatenate(halves, axis=1).astype(bf16)
        delta = dot(forward[...], rows, NT)
        out[i] = (cotangent[i].astype(f32) + delta).astype(bf16)


def mix_kernel(adjoint, received, weights, turn, *rest):
    carried, out, kept, stage = (None, *rest) if adjoint else rest
    parts = get_slots(received, stage)
    results = []
    for j in range(SLOTS):
        own = slice(j * GROUPS, (j + 1) * GROUPS)
        held = jnp.concatenate(
            [jnp.concatenate([x[own] for x in parts[q]], axis=1) for q in range(PARTS)], axis=0
        ).astype(bf16)
        kept[j] = held
        turned = dot(held, turn[...])
        if adjoint:
            turned = -turned
        turned = turned.astype(bf16)
        results.append(dot(weights[j, 0], held) + dot(weights[j, 1], turned))
    mixed = [
        [
            jnp.concatenate(
                [x[q * GROUPS : (q + 1) * GROUPS, 128 * h : 128 * (h + 1)] for x in results],
                axis=0,
            )
            for h in range(2)
        ]
        for q in range(PARTS)
    ]
    put_slots(mixed, carried, stage, out)


VMEM = pl.BlockSpec(memory_space=pltpu.VMEM)
SMEM = pl.BlockSpec(memory_space=pltpu.SMEM)
ANY = pl.BlockSpec(memory_space=pl.ANY)


def call(kernel, out_shape, in_specs, scratch, flops, moved, name, limit=24):
    several = isinstance(out_shape, list)
    return pl.pallas_call(
        kernel,
        out_shape=out_shape,
        in_specs=in_specs,
        out_specs=[VMEM] * len(out_shape) if several else VMEM,
        scratch_shapes=scratch,
        compiler_params=pltpu.CompilerParams(vmem_limit_bytes=limit * 2**20),
        cost_estimate=pl.CostEstimate(flops=flops, bytes_accessed=moved, transcendentals=0),
        name=name,
    )


def message(rows):
    return jax.ShapeDtypeStruct((GROUPS * rows, 128), bf16)


def stage_of(rows):
    return pltpu.VMEM((GROUPS * rows, 128), f32)


TABLE = pltpu.VMEM((STARTS[-1], LATS), bf16)
TABLE_S = pltpu.VMEM((STEPS[-1], 256), bf16)


def sems(count):
    return pltpu.SemaphoreType.DMA((count,))


def in_hbm(array):
    return pltpu.with_memory_space_constraint(array, pltpu.HBM)


def spread(fields, cotangent, forward):
    cycle = pltpu.VMEM((BAND, LONS, CHANNELS), bf16)
    return call(
        spread_kernel,
        [message(SENT_ROWS), message(SLOT_ROWS), message(SLOT_ROWS)],
        [ANY, ANY, ANY],
        [
            cycle, cycle, pltpu.VMEM((LONS, COEFS), bf16),
            pltpu.VMEM((3, GROUPS * SENT_ROWS, 128), f32), sems(2 * BAND + 1),
        ],
        3 * 10**8, 4 * 10**6, "spread",
    )(in_hbm(fields), in_hbm(cotangent), in_hbm(forward))


def first(received, weighted, degree_col, carried, early):
    return call(
        first_kernel,
        message(SENT_ROWS),
        [VMEM, ANY, VMEM, VMEM, ANY],
        [stage_of(SENT_ROWS), stage_of(SENT_ROWS), TABLE, sems(BLOCKS)],
        10**9, 6 * 10**6, "first",
    )(received, in_hbm(weighted), degree_col, carried, early)


def middle(
    received, one, two, analysis, synthesis, degree_row, degree_col, inverse, inverse_t
):
    return call(
        middle_kernel,
        message(SLOT_ROWS),
        [VMEM, ANY, ANY, ANY, ANY, VMEM, VMEM, ANY, ANY],
        [
            pltpu.VMEM((LONS, COEFS), bf16), pltpu.VMEM((COEFS, LONS), bf16),
            pltpu.VMEM((GROUPS, 16, 128), bf16), pltpu.VMEM((GROUPS, 32, 128), bf16),
            stage_of(16), stage_of(32), stage_of(SENT_ROWS),
            TABLE, TABLE_S, sems(4), sems(BLOCKS), sems(BLOCKS),
        ],
        3 * 10**9, 12 * 10**6, "middle",
    )(received, one, two, in_hbm(analysis), in_hbm(synthesis), degree_row, degree_col,
      in_hbm(inverse), in_hbm(inverse_t))


def last(received, table, degree_row):
    return call(
        last_kernel,
        pltpu.HBM((GROUPS * LAST_ROWS, 128), bf16),
        [VMEM, VMEM, VMEM],
        [stage_of(SLOT_ROWS), stage_of(LAST_ROWS)],
        10**9, 7 * 10**6, "last",
    )(received, table, degree_row)


def gather(received, forward, cotangent, weight_grads):
    return call(
        gather_kernel,
        jax.ShapeDtypeStruct((BAND, LONS, CHANNELS), bf16),
        [VMEM, VMEM, VMEM, ANY],
        [stage_of(LAST_ROWS)],
        3 * 10**8, 3 * 10**6, "gather",
    )(received, forward, cotangent, in_hbm(weight_grads))


def mix(adjoint, received, weights, turn, *carried):
    rows = SLOT_ROWS if adjoint else SENT_ROWS
    return call(
        functools.partial(mix_kernel, adjoint),
        [message(rows), jax.ShapeDtypeStruct((SLOTS, CHANNELS, COEFS), bf16)],
        [VMEM, VMEM, VMEM] + [VMEM] * len(carried),
        [stage_of(rows)],
        6 * 10**8, 3 * 10**6, "adjoint_mix" if adjoint else "mix",
    )(received, weights, turn, *carried)


def exchange(rows):
    count = rows.shape[0] // GROUPS
    out = lax.all_to_all(
        rows.reshape(GROUPS, count, 128), "lat", split_axis=0, concat_axis=0, tiled=True,
    )
    return out.reshape(GROUPS * count, 128)


def gradient_kernel(coeffs_source, grads_source, turn, out, coeffs, grads, sems):
    copies = []
    for j in range(SLOTS):
        copies.append(
            [
                pltpu.make_async_copy(source.at[:, j], held.at[:, j], sems.at[2 * j + n])
                for n, (source, held) in enumerate(((coeffs_source, coeffs), (grads_source, grads)))
            ]
        )
    for pair in copies:
        for copy in pair:
            copy.start()
    samples = range(coeffs.shape[0])
    for j in range(SLOTS):
        copies[j][0].wait()
        left = [coeffs[s, j] for s in samples]
        turned = [dot(x, turn[...]).astype(bf16) for x in left]
        copies[j][1].wait()
        right = jnp.concatenate([grads[s, j] for s in samples], axis=1)
        out[j, 0] = dot(jnp.concatenate(left, axis=1), right, NT).astype(bf16)
        out[j, 1] = dot(jnp.concatenate(turned, axis=1), right, NT).astype(bf16)


def weight_gradient(coeffs, grads, turn):
    held = pltpu.VMEM(coeffs.shape, bf16)
    return call(
        gradient_kernel,
        jax.ShapeDtypeStruct((SLOTS, 2, CHANNELS, CHANNELS), bf16),
        [ANY, ANY, VMEM],
        [held, held, sems(2 * SLOTS)],
        5 * 10**9, 8 * 10**6, "weight_gradient",
    )(in_hbm(coeffs), in_hbm(grads), turn)


def local(fields, cotangent, weights, degree_of):
    table = {k: jnp.asarray(v) for k, v in constants().items()}
    slots = degree_of.reshape(GROUPS, SLOTS).T.reshape(DEGREES)
    degree_col, degree_row = slots[:, None], slots[None, :]
    turned_weights = jnp.swapaxes(weights, 2, 3)
    sent, cot_two, cot_three = spread(fields[0], cotangent[0], table["forward"])
    one = exchange(sent)
    two = exchange(first(one, table["weighted"], degree_col, cot_two, turned_weights))
    filtered, coeffs = mix(False, two, turned_weights, table["turn"], cot_three)
    all_coeffs = lax.all_gather(coeffs, "batch", axis=0)
    three = exchange(filtered)
    as_sent = (GROUPS, SENT_ROWS, 128)
    four = exchange(
        middle(
            three, one.reshape(as_sent), two.reshape(as_sent), table["analysis"],
            table["synthesis"], degree_row, degree_col,
            table["inverse"], table["inverse_t"],
        )
    )
    grad_coeffs, grads = mix(True, four, weights, table["turn"])
    all_grads = lax.all_gather(grads, "batch", axis=0)
    grad_weights = weight_gradient(all_coeffs, all_grads, table["turn"])
    five = exchange(grad_coeffs)
    six = exchange(last(five, table["weighted_synthesis"], degree_row))
    grad_fields = gather(six, table["forward"], cotangent[0], grad_weights)[None]
    return grad_fields, grad_weights


def solution(mesh):
    return jax.shard_map(
        local,
        mesh=mesh,
        in_specs=(
            P("batch", "lat", None, None),
            P("batch", "lat", None, None),
            P("lat", None, None, None),
            P(),
        ),
        out_specs=(P("batch", "lat", None, None), P("lat", None, None, None)),
        check_vma=False,
    )
```

```python
import functools

import jax
import jax.numpy as jnp
import numpy as np
from jax import lax
from jax.experimental import pallas as pl
from jax.experimental.pallas import tpu as pltpu
from jax.sharding import PartitionSpec as P

LATS = 192
LONS = 384
ORDERS = 128
DEGREES = 128
CHANNELS = 384

GROUPS = 64
BAND = LATS // GROUPS
PARTS = CHANNELS // GROUPS
SLOTS = DEGREES // GROUPS
COEFS = 2 * ORDERS
BLOCKS = ORDERS // 16
SPEC_ROWS = BAND * PARTS * 2
SENT_ROWS = 48
COT_CUTS = (0, 12, 36, 54)
SLOT_ROWS = SLOTS * PARTS * 2
LAST_ROWS = 40
HALF = GROUPS // 2
LOW = LATS // 2
REACH = [DEGREES // 2 - 8 * t for t in range(BLOCKS)]
STARTS = [16 * sum(REACH[:t]) for t in range(BLOCKS + 1)]
STEPS = [8 * LOW * t for t in range(BLOCKS + 1)]

f32 = jnp.float32
bf16 = jnp.bfloat16
TN = (((0,), (0,)), ((), ()))
NN = (((1,), (0,)), ((), ()))
NT = (((1,), (1,)), ((), ()))


def legendre_table():
    colatitude = np.pi * (np.arange(LATS) + 0.5) / LATS
    cosine, sine = np.cos(colatitude), np.sin(colatitude)
    order = np.arange(ORDERS, dtype=np.float64)[:, None]
    steps = np.arange(1, ORDERS)
    growth = np.concatenate([[0.0], np.cumsum(0.5 * np.log((2.0 * steps + 1.0) / (2.0 * steps)))])
    diagonal = np.exp(0.5 * np.log(1.0 / (4.0 * np.pi)) + growth[:, None] + order * np.log(sine))
    table = np.zeros((ORDERS, DEGREES, LATS))
    for degree in range(DEGREES):
        table[degree, degree] = diagonal[degree]
        if degree >= 1:
            m = degree - 1
            table[m, degree] = np.sqrt(2.0 * m + 3.0) * cosine * table[m, m]
        if degree >= 2:
            m = order[: degree - 1]
            lead = np.sqrt((4.0 * degree**2 - 1.0) / (degree**2 - m**2))
            back = np.sqrt(((degree - 1.0) ** 2 - m**2) / (4.0 * (degree - 1.0) ** 2 - 1.0))
            table[: degree - 1, degree] = lead * (
                cosine * table[: degree - 1, degree - 1] - back * table[: degree - 1, degree - 2]
            )
    return table, 2.0 * np.pi * np.pi / LATS * sine


def fourier_tables():
    lon = np.arange(LONS)[:, None]
    order = np.arange(ORDERS)[None, :]
    phase = 2.0 * np.pi * (lon * order % LONS) / LONS
    forward = np.stack([np.cos(phase), -np.sin(phase)], axis=2).reshape(LONS, COEFS) / LONS
    doubled = np.where(order == 0, 1.0, 2.0)
    inverse = np.stack([doubled * np.cos(phase), -doubled * np.sin(phase)], axis=2)
    return forward.astype(bf16), inverse.reshape(LONS, COEFS).astype(bf16)


@functools.cache
def constants():
    table, quadrature = legendre_table()
    low = (np.arange(HALF)[None, :] * BAND + np.arange(BAND)[:, None]).reshape(-1)

    def for_analysis(values):
        values = values.astype(bf16)
        return np.concatenate(
            [
                np.concatenate([values[16 * t + k + 8 * g, 16 * t + odd :: 2] for g in (0, 1)], axis=1)
                for t in range(BLOCKS)
                for odd in (0, 1)
                for k in range(8)
            ],
            axis=0,
        )

    analysis = for_analysis(table[:, :, low])
    weighted = for_analysis((table * quadrature)[:, :, low])

    def for_synthesis(values):
        values = values.astype(bf16)
        return np.concatenate(
            [
                np.concatenate([values[16 * t + k + 4 * g, odd::2].T for g in range(4)], axis=1)
                for t in range(BLOCKS)
                for odd in (0, 1)
                for k in range(4)
            ],
            axis=0,
        )

    synthesis = for_synthesis(table[:, :, low])
    weighted_synthesis = for_synthesis((table * quadrature)[:, :, low])
    forward, inverse = fourier_tables()
    turn = np.zeros((COEFS, COEFS), np.float32)
    even = np.arange(0, COEFS, 2)
    turn[even + 1, even] = -1.0
    turn[even, even + 1] = 1.0
    return dict(
        analysis=analysis,
        weighted=weighted,
        synthesis=synthesis,
        weighted_synthesis=weighted_synthesis,
        forward=forward,
        inverse=inverse,
        inverse_t=np.ascontiguousarray(inverse.T),
        turn=turn.astype(bf16),
    )


def dot(left, right, dims=NN):
    return lax.dot_general(left, right, dims, preferred_element_type=f32)


def lane_of(shape):
    return lax.broadcasted_iota(jnp.int32, shape, 1)


def join(pieces, lanes):
    rolled = [pltpu.roll(x, s % 128, 1) if s % 128 else x for x, s in pieces]
    left = jnp.where(lanes < 32, rolled[0], rolled[1])
    right = jnp.where(lanes < 96, rolled[2], rolled[3])
    return jnp.where(lanes < 64, left, right)


def join_two(first, shift_first, second, shift_second, lanes):
    a = pltpu.roll(first, shift_first % 128, 1) if shift_first % 128 else first
    b = pltpu.roll(second, shift_second % 128, 1) if shift_second % 128 else second
    return jnp.where(lanes < 64, a, b)


def to_tiles(parts):
    lanes = lane_of(parts[0][0].shape)
    tiles = []
    for pair in range(BLOCKS // 2):
        h, at = pair // 2, 64 * (pair % 2)
        x = [parts[q][h] for q in range(PARTS)]
        a = join([(x[s], 32 * s - at) for s in range(4)], lanes)
        c = join([(x[s], 32 * s - at - 32) for s in range(4)], lanes)
        b = join_two(x[4], -at, x[5], 64 - at, lanes)
        tiles.append((a, b, c))
    return tiles


def from_tiles(tiles):
    lanes = lane_of(tiles[0][0].shape)
    parts = []
    for q in range(4):
        halves = []
        for h in range(2):
            pieces = []
            for k in range(4):
                a, _, c = tiles[2 * h + k // 2]
                pieces.append((c if k % 2 else a, 32 * (k - q)))
            halves.append(join(pieces, lanes))
        parts.append(halves)
    parts.append([join_two(tiles[2 * h][1], 0, tiles[2 * h + 1][1], 64, lanes) for h in range(2)])
    parts.append([join_two(tiles[2 * h][1], 64, tiles[2 * h + 1][1], 0, lanes) for h in range(2)])
    return parts


def as_bf16(tiles):
    return [tuple(x.astype(bf16) for x in tile) for tile in tiles]


def block_operand(tiles, t):
    a, b, c = tiles[t // 2]
    return jnp.concatenate([c if t % 2 else a, b], axis=1)


def merge_blocks(sums):
    tiles = []
    for pair in range(BLOCKS // 2):
        one, two = sums[2 * pair], sums[2 * pair + 1]
        lanes = lane_of((one.shape[0], 128))
        b = jnp.where((lanes // 32) % 2 == 0, one[:, 128:], two[:, 128:])
        tiles.append((one[:, :128], b, two[:, :128]))
    return tiles


def order_sign(lanes):
    return jnp.where((lanes // 2) % 2 == 0, 1.0, -1.0).astype(f32)


def reversal():
    row = lax.broadcasted_iota(jnp.int32, (LOW, LOW), 0)
    return (row + lane_of((LOW, LOW)) == LOW - 1).astype(f32).astype(bf16)


def fold(pair, flip):
    x = jnp.concatenate(pair, axis=1)
    low = jnp.concatenate([x[i * GROUPS : i * GROUPS + HALF] for i in range(BAND)], axis=0)
    high = jnp.concatenate([x[i * GROUPS + HALF : (i + 1) * GROUPS] for i in range(BAND)], axis=0)
    high = dot(flip, high.astype(bf16)) * order_sign(lane_of(high.shape))
    both = (low.astype(bf16).astype(f32) + high, low.astype(bf16).astype(f32) - high)
    return [[x[:, :128], x[:, 128:]] for x in both]


def unfold(even, odd, flip):
    even, odd = jnp.concatenate(even, axis=1), jnp.concatenate(odd, axis=1)
    low = even + odd
    high = (even - odd) * order_sign(lane_of(low.shape))
    high = dot(flip, high.astype(bf16))
    pieces = []
    for i in range(BAND):
        rows = slice(i * HALF, (i + 1) * HALF)
        pieces += [low[rows], high[rows]]
    whole = jnp.concatenate(pieces, axis=0)
    return tuple(whole[:, 128 * n : 128 * (n + 1)] for n in range(3))


def stacked(operand, groups, width):
    order = (lane_of(operand.shape) % 32) // 2
    none = jnp.zeros_like(operand)
    return jnp.concatenate(
        [jnp.where(order // width == g, operand, none) for g in range(groups)], axis=0
    )


def analyse(parts, flip, table, ready):
    folded = [fold(pair, flip) for pair in parts]
    tiles = [as_bf16(to_tiles([x[odd] for x in folded])) for odd in (0, 1)]
    sums = []
    for t in range(BLOCKS):
        ready(t)
        reach = REACH[t]
        order = (lane_of((reach, 256)) % 16) // 2
        pieces = []
        for odd in (0, 1):
            operand = stacked(block_operand(tiles[odd], t), 2, 8)
            rows = pl.ds(STARTS[t] + odd * 8 * reach, 8 * reach)
            part = dot(table[rows, :], operand)
            total = part[:reach]
            for k in range(1, 8):
                total = jnp.where(order == k, part[k * reach : (k + 1) * reach], total)
            if t:
                pieces.append(jnp.zeros((8 * t, 256), f32))
            pieces.append(total)
        sums.append(jnp.concatenate(pieces, axis=0))
    return merge_blocks(sums)


def synthesise(tiles, table, ready):
    sums = ([], [])
    order = (lane_of((LOW, 256)) % 8) // 2
    for t in range(BLOCKS):
        ready(t)
        operand = block_operand(tiles, t)
        for odd in (0, 1):
            rows = operand[odd * GROUPS : (odd + 1) * GROUPS]
            part = dot(table[pl.ds(STEPS[t] + odd * 4 * LOW, 4 * LOW), :], stacked(rows, 4, 4))
            total = part[:LOW]
            for k in range(1, 4):
                total = jnp.where(order == k, part[k * LOW : (k + 1) * LOW], total)
            sums[odd].append(total)
    even, odd = merge_blocks(sums[0]), merge_blocks(sums[1])
    flip = reversal()
    return from_tiles([unfold(e, o, flip) for e, o in zip(even, odd)])


def slot_choice(degrees):
    shape = (DEGREES, DEGREES)
    row, column = lax.broadcasted_iota(jnp.int32, shape, 0), lane_of(shape)
    held = degrees[...] == 2 * (row % GROUPS) + row // GROUPS
    moved = row == SLOTS * (column % GROUPS) + column // GROUPS
    return dot(*[x.astype(f32).astype(bf16) for x in (held, moved)]).astype(bf16)


def permute_rows(matrix, tiles, dims=NN):
    out = []
    for tile in tiles:
        moved = dot(matrix, jnp.concatenate(tile, axis=1), dims)
        out.append(tuple(moved[:, 128 * n : 128 * (n + 1)] for n in range(3)))
    return out


def put_slots(parts, carried, stage, out):
    stride = SLOT_ROWS if carried is None else SENT_ROWS
    for j in range(SLOTS):
        for q in range(PARTS):
            for h in range(2):
                stage[pl.ds((j * PARTS + q) * 2 + h, GROUPS, stride=stride), :] = parts[q][h][
                    j * GROUPS : (j + 1) * GROUPS
                ]
    if carried is None:
        out[...] = stage[pl.ds(0, GROUPS * SLOT_ROWS), :].astype(bf16)
    else:
        rows = stage[...].reshape(GROUPS, SENT_ROWS, 128)[:, :SLOT_ROWS]
        more = carried[...].astype(f32).reshape(GROUPS, SLOT_ROWS, 128)
        both = jnp.concatenate([rows, more], axis=1)
        out[...] = both.reshape(GROUPS * SENT_ROWS, 128).astype(bf16)


def get_slots(received, stage):
    count = received.shape[0]
    stage[pl.ds(0, count), :] = received[...].astype(f32)
    return [
        [
            jnp.concatenate(
                [
                    stage[pl.ds((j * PARTS + q) * 2 + h, GROUPS, stride=count // GROUPS), :]
                    for j in range(SLOTS)
                ],
                axis=0,
            )
            for h in range(2)
        ]
        for q in range(PARTS)
    ]


def slot_rows_out(tiles, degrees, carried, stage, out):
    moved = permute_rows(slot_choice(degrees), as_bf16(tiles), TN)
    put_slots(from_tiles(moved), carried, stage, out)


def slot_rows_in(received, degrees, stage):
    tiles = as_bf16(to_tiles(get_slots(received, stage)))
    return as_bf16(permute_rows(slot_choice(degrees), tiles))


def table_copies(source, target, sems, bounds):
    copies = []
    for t in range(BLOCKS):
        rows = pl.ds(bounds[t], bounds[t + 1] - bounds[t])
        copies.append(pltpu.make_async_copy(source.at[rows, :], target.at[rows, :], sems.at[t]))
    return copies


def cot_place(i, q, h):
    row = (i * PARTS + q) * 3 + h
    which = sum(row >= cut for cut in COT_CUTS[1:3])
    return which, row - COT_CUTS[which]


def spread_kernel(
    fields, cotangent, forward_source, out, cot_two, cot_three, field, cot, forward, stages, sems
):
    copies = []
    fetch = pltpu.make_async_copy(forward_source, forward, sems.at[2 * BAND])
    fetch.start()
    for i in range(BAND):
        copies.append(
            (
                pltpu.make_async_copy(fields.at[i], field.at[i], sems.at[2 * i]),
                pltpu.make_async_copy(cotangent.at[i], cot.at[i], sems.at[2 * i + 1]),
            )
        )
    for pair in copies:
        for copy in pair:
            copy.start()
    stage, stage_two, stage_three = stages.at[0], stages.at[1], stages.at[2]
    spots = ((stage, SPEC_ROWS, SENT_ROWS), (stage_two, 0, SLOT_ROWS), (stage_three, 0, SLOT_ROWS))
    for i in range(BAND):
        if i == 0:
            fetch.wait()
        copies[i][0].wait()
        spectra = dot(field[i], forward[...], TN)
        for q in range(PARTS):
            rows = slice(q * GROUPS, (q + 1) * GROUPS)
            at = (i * PARTS + q) * 2
            for h in range(2):
                stage[pl.ds(at + h, GROUPS, stride=SENT_ROWS), :] = spectra[
                    rows, 128 * h : 128 * (h + 1)
                ]
        copies[i][1].wait()
        turned = jnp.transpose(cot[i].astype(f32))
        for q in range(PARTS):
            rows = slice(q * GROUPS, (q + 1) * GROUPS)
            for h in range(3):
                which, at = cot_place(i, q, h)
                place, base, stride = spots[which]
                place[pl.ds(base + at, GROUPS, stride=stride), :] = turned[
                    rows, 128 * h : 128 * (h + 1)
                ]
    for row in range(COT_CUTS[3] - COT_CUTS[2], SLOT_ROWS):
        stage_three[pl.ds(row, GROUPS, stride=SLOT_ROWS), :] = jnp.zeros((GROUPS, 128), f32)
    out[...] = stage[...].astype(bf16)
    short = GROUPS * SLOT_ROWS
    cot_two[...] = stage_two[pl.ds(0, short), :].astype(bf16)
    cot_three[...] = stage_three[pl.ds(0, short), :].astype(bf16)


def first_kernel(
    received, table, degrees, carried, out, stage_in, stage
):
    stage_in[...] = received[...].astype(f32)
    parts = [
        [
            jnp.concatenate(
                [
                    stage_in[pl.ds((i * PARTS + q) * 2 + h, GROUPS, stride=SENT_ROWS), :]
                    for i in range(BAND)
                ],
                axis=0,
            )
            for h in range(2)
        ]
        for q in range(PARTS)
    ]
    sums = analyse(parts, reversal(), table, lambda t: None)
    slot_rows_out(sums, degrees, carried, stage, out)


def gelu_slope(x):
    c = np.float32(np.sqrt(2.0 / np.pi))
    squared = x * x
    th = jnp.tanh(c * (x + 0.044715 * (x * squared)))
    return 0.5 * (1.0 + th) + (0.5 * c) * x * (1.0 - th * th) * (1.0 + (3 * 0.044715) * squared)


def middle_kernel(
    received, one, two, analysis, synthesis, degrees, inverse_source, turned_source, out,
    inverse, inverse_t, rows_one, rows_two, stage_one, stage_two, stage, table, table_s, row_sems, sems, sems_s,
):
    copies_s = table_copies(synthesis, table_s, sems_s, STEPS)
    copies = table_copies(analysis, table, sems, STARTS)
    fetches = (
        pltpu.make_async_copy(one.at[:, pl.ds(32, 16), :], rows_one, row_sems.at[0]),
        pltpu.make_async_copy(two.at[:, pl.ds(16, 32), :], rows_two, row_sems.at[1]),
        pltpu.make_async_copy(inverse_source, inverse, row_sems.at[2]),
        pltpu.make_async_copy(turned_source, inverse_t, row_sems.at[3]),
    )
    for copy in (*copies_s, *fetches, *copies):
        copy.start()
    tiles = slot_rows_in(received, degrees, stage)
    synth = synthesise(tiles, table_s, lambda t: copies_s[t].wait())
    for fetch in fetches:
        fetch.wait()
    stage_one[...] = rows_one[...].astype(f32).reshape(GROUPS * 16, 128)
    stage_two[...] = rows_two[...].astype(f32).reshape(GROUPS * 32, 128)
    spots = ((stage_one, SPEC_ROWS - 32, 16), (stage_two, 8, 32), (stage, SLOT_ROWS, SENT_ROWS))

    def cot_rows(i, q, h):
        which, at = cot_place(i, q, h)
        place, base, stride = spots[which]
        return place[pl.ds(base + at, GROUPS, stride=stride), :]

    parts = []
    for q in range(PARTS):
        response = dot(jnp.concatenate(synth[q], axis=1).astype(bf16), inverse_t[...])
        cotangent = jnp.concatenate(
            [
                jnp.concatenate([cot_rows(i, q, h) for h in range(3)], axis=1)
                for i in range(BAND)
            ],
            axis=0,
        )
        upstream = (cotangent * gelu_slope(response)).astype(bf16)
        grad = dot(upstream, inverse[...])
        parts.append([grad[:, :128], grad[:, 128:]])
    sums = analyse(parts, reversal(), table, lambda t: copies[t].wait())
    slot_rows_out(sums, degrees, None, stage, out)


def last_kernel(received, table, degrees, out, stage, stage_out):
    tiles = slot_rows_in(received, degrees, stage)
    synth = synthesise(tiles, table, lambda t: None)
    for q in range(PARTS):
        for h in range(2):
            scaled = synth[q][h]
            for i in range(BAND):
                at = (i * PARTS + q) * 2 + h
                stage_out[pl.ds(at, GROUPS, stride=LAST_ROWS), :] = scaled[
                    i * GROUPS : (i + 1) * GROUPS
                ]
    for row in range(SPEC_ROWS, LAST_ROWS):
        stage_out[pl.ds(row, GROUPS, stride=LAST_ROWS), :] = jnp.zeros((GROUPS, 128), f32)
    out[...] = stage_out[...].astype(bf16)


def gather_kernel(received, forward, cotangent, weight_grads, out, stage):
    stage[...] = received[...].astype(f32)
    for i in range(BAND):
        halves = [
            jnp.concatenate(
                [
                    stage[pl.ds((i * PARTS + q) * 2 + h, GROUPS, stride=LAST_ROWS), :]
                    for q in range(PARTS)
                ],
                axis=0,
            )
            for h in range(2)
        ]
        rows = jnp.concatenate(halves, axis=1).astype(bf16)
        delta = dot(forward[...], rows, NT)
        out[i] = (cotangent[i].astype(f32) + delta).astype(bf16)


def mix_kernel(adjoint, received, weights, turn, *rest):
    carried, out, kept, stage = (None, *rest) if adjoint else rest
    parts = get_slots(received, stage)
    results = []
    for j in range(SLOTS):
        own = slice(j * GROUPS, (j + 1) * GROUPS)
        held = jnp.concatenate(
            [jnp.concatenate([x[own] for x in parts[q]], axis=1) for q in range(PARTS)], axis=0
        ).astype(bf16)
        kept[j] = held
        turned = dot(held, turn[...])
        if adjoint:
            turned = -turned
        turned = turned.astype(bf16)
        dims = NN if adjoint else TN
        results.append(dot(weights[j, 0], held, dims) + dot(weights[j, 1], turned, dims))
    mixed = [
        [
            jnp.concatenate(
                [x[q * GROUPS : (q + 1) * GROUPS, 128 * h : 128 * (h + 1)] for x in results],
                axis=0,
            )
            for h in range(2)
        ]
        for q in range(PARTS)
    ]
    put_slots(mixed, carried, stage, out)


VMEM = pl.BlockSpec(memory_space=pltpu.VMEM)
SMEM = pl.BlockSpec(memory_space=pltpu.SMEM)
ANY = pl.BlockSpec(memory_space=pl.ANY)


def call(kernel, out_shape, in_specs, scratch, flops, moved, name, limit=24):
    several = isinstance(out_shape, list)
    return pl.pallas_call(
        kernel,
        out_shape=out_shape,
        in_specs=in_specs,
        out_specs=[VMEM] * len(out_shape) if several else VMEM,
        scratch_shapes=scratch,
        compiler_params=pltpu.CompilerParams(vmem_limit_bytes=limit * 2**20),
        cost_estimate=pl.CostEstimate(flops=flops, bytes_accessed=moved, transcendentals=0),
        name=name,
    )


def message(rows):
    return jax.ShapeDtypeStruct((GROUPS * rows, 128), bf16)


def stage_of(rows):
    return pltpu.VMEM((GROUPS * rows, 128), f32)


TABLE = pltpu.VMEM((STARTS[-1], LATS), bf16)
TABLE_S = pltpu.VMEM((STEPS[-1], 256), bf16)


def sems(count):
    return pltpu.SemaphoreType.DMA((count,))


def in_hbm(array):
    return pltpu.with_memory_space_constraint(array, pltpu.HBM)


def spread(fields, cotangent, forward):
    cycle = pltpu.VMEM((BAND, LONS, CHANNELS), bf16)
    return call(
        spread_kernel,
        [message(SENT_ROWS), message(SLOT_ROWS), message(SLOT_ROWS)],
        [ANY, ANY, ANY],
        [
            cycle, cycle, pltpu.VMEM((LONS, COEFS), bf16),
            pltpu.VMEM((3, GROUPS * SENT_ROWS, 128), f32), sems(2 * BAND + 1),
        ],
        3 * 10**8, 4 * 10**6, "spread",
    )(in_hbm(fields), in_hbm(cotangent), in_hbm(forward))


def first(received, weighted, degrees, carried):
    return call(
        first_kernel,
        message(SENT_ROWS),
        [VMEM, VMEM, VMEM, VMEM],
        [stage_of(SENT_ROWS), stage_of(SENT_ROWS)],
        10**9, 6 * 10**6, "first",
    )(received, weighted, degrees, carried)


def middle(
    received, one, two, analysis, synthesis, degrees, inverse, inverse_t
):
    return call(
        middle_kernel,
        message(SLOT_ROWS),
        [VMEM, ANY, ANY, ANY, ANY, VMEM, ANY, ANY],
        [
            pltpu.VMEM((LONS, COEFS), bf16), pltpu.VMEM((COEFS, LONS), bf16),
            pltpu.VMEM((GROUPS, 16, 128), bf16), pltpu.VMEM((GROUPS, 32, 128), bf16),
            stage_of(16), stage_of(32), stage_of(SENT_ROWS),
            TABLE, TABLE_S, sems(4), sems(BLOCKS), sems(BLOCKS),
        ],
        3 * 10**9, 12 * 10**6, "middle",
    )(received, one, two, in_hbm(analysis), in_hbm(synthesis), degrees,
      in_hbm(inverse), in_hbm(inverse_t))


def last(received, table, degrees):
    return call(
        last_kernel,
        pltpu.HBM((GROUPS * LAST_ROWS, 128), bf16),
        [VMEM, VMEM, VMEM],
        [stage_of(SLOT_ROWS), stage_of(LAST_ROWS)],
        10**9, 7 * 10**6, "last",
    )(received, table, degrees)


def gather(received, forward, cotangent, weight_grads):
    return call(
        gather_kernel,
        jax.ShapeDtypeStruct((BAND, LONS, CHANNELS), bf16),
        [VMEM, VMEM, VMEM, ANY],
        [stage_of(LAST_ROWS)],
        3 * 10**8, 3 * 10**6, "gather",
    )(received, forward, cotangent, in_hbm(weight_grads))


def mix(adjoint, received, weights, turn, *carried):
    rows = SLOT_ROWS if adjoint else SENT_ROWS
    return call(
        functools.partial(mix_kernel, adjoint),
        [message(rows), jax.ShapeDtypeStruct((SLOTS, CHANNELS, COEFS), bf16)],
        [VMEM, VMEM, VMEM] + [VMEM] * len(carried),
        [stage_of(rows)],
        6 * 10**8, 3 * 10**6, "adjoint_mix" if adjoint else "mix",
    )(received, weights, turn, *carried)


def exchange(rows):
    count = rows.shape[0] // GROUPS
    out = lax.all_to_all(
        rows.reshape(GROUPS, count, 128), "lat", split_axis=0, concat_axis=0, tiled=True,
    )
    return out.reshape(GROUPS * count, 128)


def gradient_kernel(coeffs_source, grads_source, turn, out, coeffs, grads, sems):
    copies = []
    for j in range(SLOTS):
        copies.append(
            [
                pltpu.make_async_copy(source.at[:, j], held.at[:, j], sems.at[2 * j + n])
                for n, (source, held) in enumerate(((coeffs_source, coeffs), (grads_source, grads)))
            ]
        )
    for pair in copies:
        for copy in pair:
            copy.start()
    samples = range(coeffs.shape[0])
    for j in range(SLOTS):
        copies[j][0].wait()
        left = [coeffs[s, j] for s in samples]
        turned = [dot(x, turn[...]).astype(bf16) for x in left]
        copies[j][1].wait()
        right = jnp.concatenate([grads[s, j] for s in samples], axis=1)
        out[j, 0] = dot(jnp.concatenate(left, axis=1), right, NT).astype(bf16)
        out[j, 1] = dot(jnp.concatenate(turned, axis=1), right, NT).astype(bf16)


def weight_gradient(coeffs, grads, turn):
    held = pltpu.VMEM(coeffs.shape, bf16)
    return call(
        gradient_kernel,
        jax.ShapeDtypeStruct((SLOTS, 2, CHANNELS, CHANNELS), bf16),
        [ANY, ANY, VMEM],
        [held, held, sems(2 * SLOTS)],
        5 * 10**9, 8 * 10**6, "weight_gradient",
    )(in_hbm(coeffs), in_hbm(grads), turn)


def local(fields, cotangent, weights, degree_of):
    table = {k: jnp.asarray(v) for k, v in constants().items()}
    degrees = degree_of[None, :]
    sent, cot_two, cot_three = spread(fields[0], cotangent[0], table["forward"])
    one = exchange(sent)
    two = exchange(first(one, table["weighted"], degrees, cot_two))
    filtered, coeffs = mix(False, two, weights, table["turn"], cot_three)
    all_coeffs = lax.all_gather(coeffs, "batch", axis=0)
    three = exchange(filtered)
    as_sent = (GROUPS, SENT_ROWS, 128)
    four = exchange(
        middle(
            three, one.reshape(as_sent), two.reshape(as_sent), table["analysis"],
            table["synthesis"], degrees,
            table["inverse"], table["inverse_t"],
        )
    )
    grad_coeffs, grads = mix(True, four, weights, table["turn"])
    all_grads = lax.all_gather(grads, "batch", axis=0)
    grad_weights = weight_gradient(all_coeffs, all_grads, table["turn"])
    five = exchange(grad_coeffs)
    six = exchange(last(five, table["weighted_synthesis"], degrees))
    grad_fields = gather(six, table["forward"], cotangent[0], grad_weights)[None]
    return grad_fields, grad_weights


def solution(mesh):
    return jax.shard_map(
        local,
        mesh=mesh,
        in_specs=(
            P("batch", "lat", None, None),
            P("batch", "lat", None, None),
            P("lat", None, None, None),
            P(),
        ),
        out_specs=(P("batch", "lat", None, None), P("lat", None, None, None)),
        check_vma=False,
    )
```

```python
import functools

import jax
import jax.numpy as jnp
import numpy as np
from jax import lax
from jax.experimental import pallas as pl
from jax.experimental.pallas import tpu as pltpu
from jax.sharding import PartitionSpec as P

LATS = 192
LONS = 384
ORDERS = 128
DEGREES = 128
CHANNELS = 384

GROUPS = 64
BAND = LATS // GROUPS
PARTS = CHANNELS // GROUPS
SLOTS = DEGREES // GROUPS
COEFS = 2 * ORDERS
BLOCKS = ORDERS // 16
SPEC_ROWS = BAND * PARTS * 2
FIRST_ROWS = 64
SENT_ROWS = 40
CARRIED_ROWS = 16
COT_CUTS = (0, 28, 44, 54)
SLOT_ROWS = SLOTS * PARTS * 2
LAST_ROWS = 40
HALF = GROUPS // 2
LOW = LATS // 2
REACH = [DEGREES // 2 - 8 * t for t in range(BLOCKS)]
STARTS = [16 * sum(REACH[:t]) for t in range(BLOCKS + 1)]
STEPS = [8 * LOW * t for t in range(BLOCKS + 1)]

f32 = jnp.float32
bf16 = jnp.bfloat16
TN = (((0,), (0,)), ((), ()))
NN = (((1,), (0,)), ((), ()))
NT = (((1,), (1,)), ((), ()))


def legendre_table():
    colatitude = np.pi * (np.arange(LATS) + 0.5) / LATS
    cosine, sine = np.cos(colatitude), np.sin(colatitude)
    order = np.arange(ORDERS, dtype=np.float64)[:, None]
    steps = np.arange(1, ORDERS)
    growth = np.concatenate([[0.0], np.cumsum(0.5 * np.log((2.0 * steps + 1.0) / (2.0 * steps)))])
    diagonal = np.exp(0.5 * np.log(1.0 / (4.0 * np.pi)) + growth[:, None] + order * np.log(sine))
    table = np.zeros((ORDERS, DEGREES, LATS))
    for degree in range(DEGREES):
        table[degree, degree] = diagonal[degree]
        if degree >= 1:
            m = degree - 1
            table[m, degree] = np.sqrt(2.0 * m + 3.0) * cosine * table[m, m]
        if degree >= 2:
            m = order[: degree - 1]
            lead = np.sqrt((4.0 * degree**2 - 1.0) / (degree**2 - m**2))
            back = np.sqrt(((degree - 1.0) ** 2 - m**2) / (4.0 * (degree - 1.0) ** 2 - 1.0))
            table[: degree - 1, degree] = lead * (
                cosine * table[: degree - 1, degree - 1] - back * table[: degree - 1, degree - 2]
            )
    return table, 2.0 * np.pi * np.pi / LATS * sine


def fourier_tables():
    lon = np.arange(LONS)[:, None]
    order = np.arange(ORDERS)[None, :]
    phase = 2.0 * np.pi * (lon * order % LONS) / LONS
    forward = np.stack([np.cos(phase), -np.sin(phase)], axis=2).reshape(LONS, COEFS) / LONS
    doubled = np.where(order == 0, 1.0, 2.0)
    inverse = np.stack([doubled * np.cos(phase), -doubled * np.sin(phase)], axis=2)
    return forward.astype(bf16), inverse.reshape(LONS, COEFS).astype(bf16)


@functools.cache
def constants():
    table, quadrature = legendre_table()
    low = (np.arange(HALF)[None, :] * BAND + np.arange(BAND)[:, None]).reshape(-1)

    def for_analysis(values):
        values = values.astype(bf16)
        return np.concatenate(
            [
                np.concatenate([values[16 * t + k + 8 * g, 16 * t + odd :: 2] for g in (0, 1)], axis=1)
                for t in range(BLOCKS)
                for odd in (0, 1)
                for k in range(8)
            ],
            axis=0,
        )

    analysis = for_analysis(table[:, :, low])
    weighted = for_analysis((table * quadrature)[:, :, low])

    def for_synthesis(values):
        values = values.astype(bf16)
        return np.concatenate(
            [
                np.concatenate([values[16 * t + k + 4 * g, odd::2].T for g in range(4)], axis=1)
                for t in range(BLOCKS)
                for odd in (0, 1)
                for k in range(4)
            ],
            axis=0,
        )

    synthesis = for_synthesis(table[:, :, low])
    weighted_synthesis = for_synthesis((table * quadrature)[:, :, low])
    forward, inverse = fourier_tables()
    turn = np.zeros((COEFS, COEFS), np.float32)
    even = np.arange(0, COEFS, 2)
    turn[even + 1, even] = -1.0
    turn[even, even + 1] = 1.0
    return dict(
        analysis=analysis,
        weighted=weighted,
        synthesis=synthesis,
        weighted_synthesis=weighted_synthesis,
        forward=forward,
        inverse=inverse,
        inverse_t=np.ascontiguousarray(inverse.T),
        turn=turn.astype(bf16),
    )


def dot(left, right, dims=NN):
    return lax.dot_general(left, right, dims, preferred_element_type=f32)


def lane_of(shape):
    return lax.broadcasted_iota(jnp.int32, shape, 1)


def join(pieces, lanes):
    rolled = [pltpu.roll(x, s % 128, 1) if s % 128 else x for x, s in pieces]
    left = jnp.where(lanes < 32, rolled[0], rolled[1])
    right = jnp.where(lanes < 96, rolled[2], rolled[3])
    return jnp.where(lanes < 64, left, right)


def join_two(first, shift_first, second, shift_second, lanes):
    a = pltpu.roll(first, shift_first % 128, 1) if shift_first % 128 else first
    b = pltpu.roll(second, shift_second % 128, 1) if shift_second % 128 else second
    return jnp.where(lanes < 64, a, b)


def to_tiles(parts):
    lanes = lane_of(parts[0][0].shape)
    tiles = []
    for pair in range(BLOCKS // 2):
        h, at = pair // 2, 64 * (pair % 2)
        x = [parts[q][h] for q in range(PARTS)]
        a = join([(x[s], 32 * s - at) for s in range(4)], lanes)
        c = join([(x[s], 32 * s - at - 32) for s in range(4)], lanes)
        b = join_two(x[4], -at, x[5], 64 - at, lanes)
        tiles.append((a, b, c))
    return tiles


def from_tiles(tiles):
    lanes = lane_of(tiles[0][0].shape)
    parts = []
    for q in range(4):
        halves = []
        for h in range(2):
            pieces = []
            for k in range(4):
                a, _, c = tiles[2 * h + k // 2]
                pieces.append((c if k % 2 else a, 32 * (k - q)))
            halves.append(join(pieces, lanes))
        parts.append(halves)
    parts.append([join_two(tiles[2 * h][1], 0, tiles[2 * h + 1][1], 64, lanes) for h in range(2)])
    parts.append([join_two(tiles[2 * h][1], 64, tiles[2 * h + 1][1], 0, lanes) for h in range(2)])
    return parts


def as_bf16(tiles):
    return [tuple(x.astype(bf16) for x in tile) for tile in tiles]


def block_operand(tiles, t):
    a, b, c = tiles[t // 2]
    return jnp.concatenate([c if t % 2 else a, b], axis=1)


def merge_blocks(sums):
    tiles = []
    for pair in range(BLOCKS // 2):
        one, two = sums[2 * pair], sums[2 * pair + 1]
        lanes = lane_of((one.shape[0], 128))
        b = jnp.where((lanes // 32) % 2 == 0, one[:, 128:], two[:, 128:])
        tiles.append((one[:, :128], b, two[:, :128]))
    return tiles


def order_sign(lanes):
    return jnp.where((lanes // 2) % 2 == 0, 1.0, -1.0).astype(f32)


def reversal():
    row = lax.broadcasted_iota(jnp.int32, (LOW, LOW), 0)
    return (row + lane_of((LOW, LOW)) == LOW - 1).astype(f32).astype(bf16)


def fold(pair, flip):
    x = jnp.concatenate(pair, axis=1)
    low = jnp.concatenate([x[i * GROUPS : i * GROUPS + HALF] for i in range(BAND)], axis=0)
    high = jnp.concatenate([x[i * GROUPS + HALF : (i + 1) * GROUPS] for i in range(BAND)], axis=0)
    high = dot(flip, high.astype(bf16)) * order_sign(lane_of(high.shape))
    both = (low.astype(bf16).astype(f32) + high, low.astype(bf16).astype(f32) - high)
    return [[x[:, :128], x[:, 128:]] for x in both]


def unfold(even, odd, flip):
    even, odd = jnp.concatenate(even, axis=1), jnp.concatenate(odd, axis=1)
    low = even + odd
    high = (even - odd) * order_sign(lane_of(low.shape))
    high = dot(flip, high.astype(bf16))
    pieces = []
    for i in range(BAND):
        rows = slice(i * HALF, (i + 1) * HALF)
        pieces += [low[rows], high[rows]]
    whole = jnp.concatenate(pieces, axis=0)
    return tuple(whole[:, 128 * n : 128 * (n + 1)] for n in range(3))


def stacked(operand, groups, width):
    order = (lane_of(operand.shape) % 32) // 2
    none = jnp.zeros_like(operand)
    return jnp.concatenate(
        [jnp.where(order // width == g, operand, none) for g in range(groups)], axis=0
    )


def analyse(parts, flip, table, ready):
    folded = [fold(pair, flip) for pair in parts]
    tiles = [as_bf16(to_tiles([x[odd] for x in folded])) for odd in (0, 1)]
    sums = []
    for t in range(BLOCKS):
        ready(t)
        reach = REACH[t]
        order = (lane_of((reach, 256)) % 16) // 2
        pieces = []
        for odd in (0, 1):
            operand = stacked(block_operand(tiles[odd], t), 2, 8)
            rows = pl.ds(STARTS[t] + odd * 8 * reach, 8 * reach)
            part = dot(table[rows, :], operand)
            total = part[:reach]
            for k in range(1, 8):
                total = jnp.where(order == k, part[k * reach : (k + 1) * reach], total)
            if t:
                pieces.append(jnp.zeros((8 * t, 256), f32))
            pieces.append(total)
        sums.append(jnp.concatenate(pieces, axis=0))
    return merge_blocks(sums)


def synthesise(tiles, table, ready):
    sums = ([], [])
    order = (lane_of((LOW, 256)) % 8) // 2
    for t in range(BLOCKS):
        ready(t)
        operand = block_operand(tiles, t)
        for odd in (0, 1):
            rows = operand[odd * GROUPS : (odd + 1) * GROUPS]
            part = dot(table[pl.ds(STEPS[t] + odd * 4 * LOW, 4 * LOW), :], stacked(rows, 4, 4))
            total = part[:LOW]
            for k in range(1, 4):
                total = jnp.where(order == k, part[k * LOW : (k + 1) * LOW], total)
            sums[odd].append(total)
    even, odd = merge_blocks(sums[0]), merge_blocks(sums[1])
    flip = reversal()
    return from_tiles([unfold(e, o, flip) for e, o in zip(even, odd)])


def slot_choice(degrees):
    shape = (DEGREES, DEGREES)
    row, column = lax.broadcasted_iota(jnp.int32, shape, 0), lane_of(shape)
    held = degrees[...] == 2 * (row % GROUPS) + row // GROUPS
    moved = row == SLOTS * (column % GROUPS) + column // GROUPS
    return dot(*[x.astype(f32).astype(bf16) for x in (held, moved)]).astype(bf16)


def permute_rows(matrix, tiles, dims=NN):
    out = []
    for tile in tiles:
        moved = dot(matrix, jnp.concatenate(tile, axis=1), dims)
        out.append(tuple(moved[:, 128 * n : 128 * (n + 1)] for n in range(3)))
    return out


def put_slots(parts, carried, stage, out):
    stride = SLOT_ROWS if carried is None else SENT_ROWS
    for j in range(SLOTS):
        for q in range(PARTS):
            for h in range(2):
                stage[pl.ds((j * PARTS + q) * 2 + h, GROUPS, stride=stride), :] = parts[q][h][
                    j * GROUPS : (j + 1) * GROUPS
                ]
    if carried is None:
        out[...] = stage[pl.ds(0, GROUPS * SLOT_ROWS), :].astype(bf16)
    else:
        rows = stage[...].reshape(GROUPS, SENT_ROWS, 128)[:, :SLOT_ROWS]
        more = carried[...].astype(f32).reshape(GROUPS, CARRIED_ROWS, 128)
        both = jnp.concatenate([rows, more], axis=1)
        out[...] = both.reshape(GROUPS * SENT_ROWS, 128).astype(bf16)


def get_slots(received, stage):
    count = received.shape[0]
    stage[pl.ds(0, count), :] = received[...].astype(f32)
    return [
        [
            jnp.concatenate(
                [
                    stage[pl.ds((j * PARTS + q) * 2 + h, GROUPS, stride=count // GROUPS), :]
                    for j in range(SLOTS)
                ],
                axis=0,
            )
            for h in range(2)
        ]
        for q in range(PARTS)
    ]


def slot_rows_out(tiles, degrees, carried, stage, out):
    moved = permute_rows(slot_choice(degrees), as_bf16(tiles), TN)
    put_slots(from_tiles(moved), carried, stage, out)


def slot_rows_in(received, degrees, stage):
    tiles = as_bf16(to_tiles(get_slots(received, stage)))
    return as_bf16(permute_rows(slot_choice(degrees), tiles))


def table_copies(source, target, sems, bounds):
    copies = []
    for t in range(BLOCKS):
        rows = pl.ds(bounds[t], bounds[t + 1] - bounds[t])
        copies.append(pltpu.make_async_copy(source.at[rows, :], target.at[rows, :], sems.at[t]))
    return copies


def cot_place(i, q, h):
    row = (i * PARTS + q) * 3 + h
    which = sum(row >= cut for cut in COT_CUTS[1:3])
    return which, row - COT_CUTS[which]


def spread_kernel(
    fields, cotangent, forward_source, out, cot_two, cot_three, field, cot, forward, stages, sems
):
    copies = []
    fetch = pltpu.make_async_copy(forward_source, forward, sems.at[2 * BAND])
    fetch.start()
    for i in range(BAND):
        copies.append(
            (
                pltpu.make_async_copy(fields.at[i], field.at[i], sems.at[2 * i]),
                pltpu.make_async_copy(cotangent.at[i], cot.at[i], sems.at[2 * i + 1]),
            )
        )
    for pair in copies:
        for copy in pair:
            copy.start()
    stage, stage_two, stage_three = stages.at[0], stages.at[1], stages.at[2]
    spots = ((stage, SPEC_ROWS, FIRST_ROWS), (stage_two, 0, CARRIED_ROWS), (stage_three, 0, CARRIED_ROWS))
    for i in range(BAND):
        if i == 0:
            fetch.wait()
        copies[i][0].wait()
        spectra = dot(field[i], forward[...], TN)
        for q in range(PARTS):
            rows = slice(q * GROUPS, (q + 1) * GROUPS)
            at = (i * PARTS + q) * 2
            for h in range(2):
                stage[pl.ds(at + h, GROUPS, stride=FIRST_ROWS), :] = spectra[
                    rows, 128 * h : 128 * (h + 1)
                ]
        copies[i][1].wait()
        turned = jnp.transpose(cot[i].astype(f32))
        for q in range(PARTS):
            rows = slice(q * GROUPS, (q + 1) * GROUPS)
            for h in range(3):
                which, at = cot_place(i, q, h)
                place, base, stride = spots[which]
                place[pl.ds(base + at, GROUPS, stride=stride), :] = turned[
                    rows, 128 * h : 128 * (h + 1)
                ]
    for row in range(COT_CUTS[3] - COT_CUTS[2], CARRIED_ROWS):
        stage_three[pl.ds(row, GROUPS, stride=CARRIED_ROWS), :] = jnp.zeros((GROUPS, 128), f32)
    out[...] = stage[...].astype(bf16)
    short = GROUPS * CARRIED_ROWS
    cot_two[...] = stage_two[pl.ds(0, short), :].astype(bf16)
    cot_three[...] = stage_three[pl.ds(0, short), :].astype(bf16)


def first_kernel(
    received, table, degrees, carried, out, stage_in, stage
):
    stage_in[...] = received[...].astype(f32)
    parts = [
        [
            jnp.concatenate(
                [
                    stage_in[pl.ds((i * PARTS + q) * 2 + h, GROUPS, stride=FIRST_ROWS), :]
                    for i in range(BAND)
                ],
                axis=0,
            )
            for h in range(2)
        ]
        for q in range(PARTS)
    ]
    sums = analyse(parts, reversal(), table, lambda t: None)
    slot_rows_out(sums, degrees, carried, stage, out)


def gelu_slope(x):
    c = np.float32(np.sqrt(2.0 / np.pi))
    squared = x * x
    th = jnp.tanh(c * (x + 0.044715 * (x * squared)))
    return 0.5 * (1.0 + th) + (0.5 * c) * x * (1.0 - th * th) * (1.0 + (3 * 0.044715) * squared)


def middle_kernel(
    received, one, two, analysis, synthesis, degrees, inverse_source, turned_source, out,
    inverse, inverse_t, rows_one, rows_two, stage_one, stage_two, stage, table, table_s, row_sems, sems, sems_s,
):
    copies_s = table_copies(synthesis, table_s, sems_s, STEPS)
    copies = table_copies(analysis, table, sems, STARTS)
    fetches = (
        pltpu.make_async_copy(one.at[:, pl.ds(32, 32), :], rows_one, row_sems.at[0]),
        pltpu.make_async_copy(two, rows_two, row_sems.at[1]),
        pltpu.make_async_copy(inverse_source, inverse, row_sems.at[2]),
        pltpu.make_async_copy(turned_source, inverse_t, row_sems.at[3]),
    )
    for copy in (*copies_s, *fetches, *copies):
        copy.start()
    tiles = slot_rows_in(received, degrees, stage)
    synth = synthesise(tiles, table_s, lambda t: copies_s[t].wait())
    for fetch in fetches:
        fetch.wait()
    stage_one[...] = rows_one[...].astype(f32).reshape(GROUPS * 32, 128)
    stage_two[...] = rows_two[...].astype(f32)
    spots = ((stage_one, SPEC_ROWS - 32, 32), (stage_two, SLOT_ROWS, SENT_ROWS), (stage, SLOT_ROWS, SENT_ROWS))

    def cot_rows(i, q, h):
        which, at = cot_place(i, q, h)
        place, base, stride = spots[which]
        return place[pl.ds(base + at, GROUPS, stride=stride), :]

    parts = []
    for q in range(PARTS):
        response = dot(jnp.concatenate(synth[q], axis=1).astype(bf16), inverse_t[...])
        cotangent = jnp.concatenate(
            [
                jnp.concatenate([cot_rows(i, q, h) for h in range(3)], axis=1)
                for i in range(BAND)
            ],
            axis=0,
        )
        upstream = (cotangent * gelu_slope(response)).astype(bf16)
        grad = dot(upstream, inverse[...])
        parts.append([grad[:, :128], grad[:, 128:]])
    sums = analyse(parts, reversal(), table, lambda t: copies[t].wait())
    slot_rows_out(sums, degrees, None, stage, out)


def last_kernel(received, table, degrees, out, stage, stage_out):
    tiles = slot_rows_in(received, degrees, stage)
    synth = synthesise(tiles, table, lambda t: None)
    for q in range(PARTS):
        for h in range(2):
            scaled = synth[q][h]
            for i in range(BAND):
                at = (i * PARTS + q) * 2 + h
                stage_out[pl.ds(at, GROUPS, stride=LAST_ROWS), :] = scaled[
                    i * GROUPS : (i + 1) * GROUPS
                ]
    for row in range(SPEC_ROWS, LAST_ROWS):
        stage_out[pl.ds(row, GROUPS, stride=LAST_ROWS), :] = jnp.zeros((GROUPS, 128), f32)
    out[...] = stage_out[...].astype(bf16)


def gather_kernel(received, forward, cotangent, weight_grads, out, stage):
    stage[...] = received[...].astype(f32)
    for i in range(BAND):
        halves = [
            jnp.concatenate(
                [
                    stage[pl.ds((i * PARTS + q) * 2 + h, GROUPS, stride=LAST_ROWS), :]
                    for q in range(PARTS)
                ],
                axis=0,
            )
            for h in range(2)
        ]
        rows = jnp.concatenate(halves, axis=1).astype(bf16)
        delta = dot(forward[...], rows, NT)
        out[i] = (cotangent[i].astype(f32) + delta).astype(bf16)


def mix_kernel(adjoint, received, weights, turn, *rest):
    carried, out, kept, stage = (None, *rest) if adjoint else rest
    parts = get_slots(received, stage)
    results = []
    for j in range(SLOTS):
        own = slice(j * GROUPS, (j + 1) * GROUPS)
        held = jnp.concatenate(
            [jnp.concatenate([x[own] for x in parts[q]], axis=1) for q in range(PARTS)], axis=0
        ).astype(bf16)
        kept[j] = held
        turned = dot(held, turn[...])
        if adjoint:
            turned = -turned
        turned = turned.astype(bf16)
        dims = NN if adjoint else TN
        results.append(dot(weights[j, 0], held, dims) + dot(weights[j, 1], turned, dims))
    mixed = [
        [
            jnp.concatenate(
                [x[q * GROUPS : (q + 1) * GROUPS, 128 * h : 128 * (h + 1)] for x in results],
                axis=0,
            )
            for h in range(2)
        ]
        for q in range(PARTS)
    ]
    put_slots(mixed, carried, stage, out)


VMEM = pl.BlockSpec(memory_space=pltpu.VMEM)
SMEM = pl.BlockSpec(memory_space=pltpu.SMEM)
ANY = pl.BlockSpec(memory_space=pl.ANY)


def call(kernel, out_shape, in_specs, scratch, flops, moved, name, limit=24):
    several = isinstance(out_shape, list)
    return pl.pallas_call(
        kernel,
        out_shape=out_shape,
        in_specs=in_specs,
        out_specs=[VMEM] * len(out_shape) if several else VMEM,
        scratch_shapes=scratch,
        compiler_params=pltpu.CompilerParams(vmem_limit_bytes=limit * 2**20),
        cost_estimate=pl.CostEstimate(flops=flops, bytes_accessed=moved, transcendentals=0),
        name=name,
    )


def message(rows):
    return jax.ShapeDtypeStruct((GROUPS * rows, 128), bf16)


def stage_of(rows):
    return pltpu.VMEM((GROUPS * rows, 128), f32)


TABLE = pltpu.VMEM((STARTS[-1], LATS), bf16)
TABLE_S = pltpu.VMEM((STEPS[-1], 256), bf16)


def sems(count):
    return pltpu.SemaphoreType.DMA((count,))


def in_hbm(array):
    return pltpu.with_memory_space_constraint(array, pltpu.HBM)


def spread(fields, cotangent, forward):
    cycle = pltpu.VMEM((BAND, LONS, CHANNELS), bf16)
    return call(
        spread_kernel,
        [message(FIRST_ROWS), message(CARRIED_ROWS), message(CARRIED_ROWS)],
        [ANY, ANY, ANY],
        [
            cycle, cycle, pltpu.VMEM((LONS, COEFS), bf16),
            pltpu.VMEM((3, GROUPS * FIRST_ROWS, 128), f32), sems(2 * BAND + 1),
        ],
        3 * 10**8, 4 * 10**6, "spread",
    )(in_hbm(fields), in_hbm(cotangent), in_hbm(forward))


def first(received, weighted, degrees, carried):
    return call(
        first_kernel,
        message(SENT_ROWS),
        [VMEM, VMEM, VMEM, VMEM],
        [stage_of(FIRST_ROWS), stage_of(SENT_ROWS)],
        10**9, 6 * 10**6, "first",
    )(received, weighted, degrees, carried)


def middle(
    received, one, two, analysis, synthesis, degrees, inverse, inverse_t
):
    return call(
        middle_kernel,
        message(SLOT_ROWS),
        [VMEM, ANY, ANY, ANY, ANY, VMEM, ANY, ANY],
        [
            pltpu.VMEM((LONS, COEFS), bf16), pltpu.VMEM((COEFS, LONS), bf16),
            pltpu.VMEM((GROUPS, 32, 128), bf16), pltpu.VMEM((GROUPS * SENT_ROWS, 128), bf16),
            stage_of(32), stage_of(SENT_ROWS), stage_of(SENT_ROWS),
            TABLE, TABLE_S, sems(4), sems(BLOCKS), sems(BLOCKS),
        ],
        3 * 10**9, 12 * 10**6, "middle",
    )(received, one, two, in_hbm(analysis), in_hbm(synthesis), degrees,
      in_hbm(inverse), in_hbm(inverse_t))


def last(received, table, degrees):
    return call(
        last_kernel,
        pltpu.HBM((GROUPS * LAST_ROWS, 128), bf16),
        [VMEM, VMEM, VMEM],
        [stage_of(SLOT_ROWS), stage_of(LAST_ROWS)],
        10**9, 7 * 10**6, "last",
    )(received, table, degrees)


def gather(received, forward, cotangent, weight_grads):
    return call(
        gather_kernel,
        jax.ShapeDtypeStruct((BAND, LONS, CHANNELS), bf16),
        [VMEM, VMEM, VMEM, ANY],
        [stage_of(LAST_ROWS)],
        3 * 10**8, 3 * 10**6, "gather",
    )(received, forward, cotangent, in_hbm(weight_grads))


def mix(adjoint, received, weights, turn, *carried):
    rows = SLOT_ROWS if adjoint else SENT_ROWS
    return call(
        functools.partial(mix_kernel, adjoint),
        [message(rows), jax.ShapeDtypeStruct((SLOTS, CHANNELS, COEFS), bf16)],
        [VMEM, VMEM, VMEM] + [VMEM] * len(carried),
        [stage_of(rows)],
        6 * 10**8, 3 * 10**6, "adjoint_mix" if adjoint else "mix",
    )(received, weights, turn, *carried)


def exchange(rows):
    count = rows.shape[0] // GROUPS
    out = lax.all_to_all(
        rows.reshape(GROUPS, count, 128), "lat", split_axis=0, concat_axis=0, tiled=True,
    )
    return out.reshape(GROUPS * count, 128)


def gradient_kernel(coeffs_source, grads_source, turn, out, coeffs, grads, sems):
    copies = []
    for j in range(SLOTS):
        copies.append(
            [
                pltpu.make_async_copy(source.at[:, j], held.at[:, j], sems.at[2 * j + n])
                for n, (source, held) in enumerate(((coeffs_source, coeffs), (grads_source, grads)))
            ]
        )
    for pair in copies:
        for copy in pair:
            copy.start()
    samples = range(coeffs.shape[0])
    for j in range(SLOTS):
        copies[j][0].wait()
        left = [coeffs[s, j] for s in samples]
        turned = [dot(x, turn[...]).astype(bf16) for x in left]
        copies[j][1].wait()
        right = jnp.concatenate([grads[s, j] for s in samples], axis=1)
        out[j, 0] = dot(jnp.concatenate(left, axis=1), right, NT).astype(bf16)
        out[j, 1] = dot(jnp.concatenate(turned, axis=1), right, NT).astype(bf16)


def weight_gradient(coeffs, grads, turn):
    held = pltpu.VMEM(coeffs.shape, bf16)
    return call(
        gradient_kernel,
        jax.ShapeDtypeStruct((SLOTS, 2, CHANNELS, CHANNELS), bf16),
        [ANY, ANY, VMEM],
        [held, held, sems(2 * SLOTS)],
        5 * 10**9, 8 * 10**6, "weight_gradient",
    )(in_hbm(coeffs), in_hbm(grads), turn)


def local(fields, cotangent, weights, degree_of):
    table = {k: jnp.asarray(v) for k, v in constants().items()}
    degrees = degree_of[None, :]
    sent, cot_two, cot_three = spread(fields[0], cotangent[0], table["forward"])
    one = exchange(sent)
    two = exchange(first(one, table["weighted"], degrees, cot_two))
    filtered, coeffs = mix(False, two, weights, table["turn"], cot_three)
    all_coeffs = lax.all_gather(coeffs, "batch", axis=0)
    three = exchange(filtered)
    four = exchange(
        middle(
            three, one.reshape(GROUPS, FIRST_ROWS, 128), two, table["analysis"],
            table["synthesis"], degrees,
            table["inverse"], table["inverse_t"],
        )
    )
    grad_coeffs, grads = mix(True, four, weights, table["turn"])
    all_grads = lax.all_gather(grads, "batch", axis=0)
    grad_weights = weight_gradient(all_coeffs, all_grads, table["turn"])
    five = exchange(grad_coeffs)
    six = exchange(last(five, table["weighted_synthesis"], degrees))
    grad_fields = gather(six, table["forward"], cotangent[0], grad_weights)[None]
    return grad_fields, grad_weights


def solution(mesh):
    return jax.shard_map(
        local,
        mesh=mesh,
        in_specs=(
            P("batch", "lat", None, None),
            P("batch", "lat", None, None),
            P("lat", None, None, None),
            P(),
        ),
        out_specs=(P("batch", "lat", None, None), P("lat", None, None, None)),
        check_vma=False,
    )
```

```python
import functools

import jax
import jax.numpy as jnp
import numpy as np
from jax import lax
from jax.experimental import pallas as pl
from jax.experimental.pallas import tpu as pltpu
from jax.sharding import PartitionSpec as P

LATS = 192
LONS = 384
ORDERS = 128
DEGREES = 128
CHANNELS = 384

GROUPS = 64
BAND = LATS // GROUPS
PARTS = CHANNELS // GROUPS
SLOTS = DEGREES // GROUPS
COEFS = 2 * ORDERS
BLOCKS = ORDERS // 16
SPEC_ROWS = BAND * PARTS * 2
SENT_ROWS = 48
COT_CUTS = (0, 12, 36, 54)
SLOT_ROWS = SLOTS * PARTS * 2
LAST_ROWS = 40
HALF = GROUPS // 2
LOW = LATS // 2
REACH = [DEGREES // 2 - 8 * t for t in range(BLOCKS)]
STARTS = [16 * sum(REACH[:t]) for t in range(BLOCKS + 1)]
STEPS = [8 * LOW * t for t in range(BLOCKS + 1)]

f32 = jnp.float32
bf16 = jnp.bfloat16
TN = (((0,), (0,)), ((), ()))
NN = (((1,), (0,)), ((), ()))
NT = (((1,), (1,)), ((), ()))


def legendre_table():
    colatitude = np.pi * (np.arange(LATS) + 0.5) / LATS
    cosine, sine = np.cos(colatitude), np.sin(colatitude)
    order = np.arange(ORDERS, dtype=np.float64)[:, None]
    steps = np.arange(1, ORDERS)
    growth = np.concatenate([[0.0], np.cumsum(0.5 * np.log((2.0 * steps + 1.0) / (2.0 * steps)))])
    diagonal = np.exp(0.5 * np.log(1.0 / (4.0 * np.pi)) + growth[:, None] + order * np.log(sine))
    table = np.zeros((ORDERS, DEGREES, LATS))
    for degree in range(DEGREES):
        table[degree, degree] = diagonal[degree]
        if degree >= 1:
            m = degree - 1
            table[m, degree] = np.sqrt(2.0 * m + 3.0) * cosine * table[m, m]
        if degree >= 2:
            m = order[: degree - 1]
            lead = np.sqrt((4.0 * degree**2 - 1.0) / (degree**2 - m**2))
            back = np.sqrt(((degree - 1.0) ** 2 - m**2) / (4.0 * (degree - 1.0) ** 2 - 1.0))
            table[: degree - 1, degree] = lead * (
                cosine * table[: degree - 1, degree - 1] - back * table[: degree - 1, degree - 2]
            )
    return table, 2.0 * np.pi * np.pi / LATS * sine


def fourier_tables():
    lon = np.arange(LONS)[:, None]
    order = np.arange(ORDERS)[None, :]
    phase = 2.0 * np.pi * (lon * order % LONS) / LONS
    forward = np.stack([np.cos(phase), -np.sin(phase)], axis=2).reshape(LONS, COEFS) / LONS
    doubled = np.where(order == 0, 1.0, 2.0)
    inverse = np.stack([doubled * np.cos(phase), -doubled * np.sin(phase)], axis=2)
    return forward.astype(bf16), inverse.reshape(LONS, COEFS).astype(bf16)


@functools.cache
def constants():
    table, quadrature = legendre_table()
    low = (np.arange(HALF)[None, :] * BAND + np.arange(BAND)[:, None]).reshape(-1)

    def for_analysis(values):
        values = values.astype(bf16)
        return np.concatenate(
            [
                np.concatenate([values[16 * t + k + 8 * g, 16 * t + odd :: 2] for g in (0, 1)], axis=1)
                for t in range(BLOCKS)
                for odd in (0, 1)
                for k in range(8)
            ],
            axis=0,
        )

    analysis = for_analysis(table[:, :, low])
    weighted = for_analysis((table * quadrature)[:, :, low])

    def for_synthesis(values):
        values = values.astype(bf16)
        return np.concatenate(
            [
                np.concatenate([values[16 * t + k + 4 * g, odd::2].T for g in range(4)], axis=1)
                for t in range(BLOCKS)
                for odd in (0, 1)
                for k in range(4)
            ],
            axis=0,
        )

    synthesis = for_synthesis(table[:, :, low])
    weighted_synthesis = for_synthesis((table * quadrature)[:, :, low])
    forward, inverse = fourier_tables()
    turn = np.zeros((COEFS, COEFS), np.float32)
    even = np.arange(0, COEFS, 2)
    turn[even + 1, even] = -1.0
    turn[even, even + 1] = 1.0
    return dict(
        analysis=analysis,
        weighted=weighted,
        synthesis=synthesis,
        weighted_synthesis=weighted_synthesis,
        forward=forward,
        inverse=inverse,
        inverse_t=np.ascontiguousarray(inverse.T),
        turn=turn.astype(bf16),
    )


def dot(left, right, dims=NN):
    return lax.dot_general(left, right, dims, preferred_element_type=f32)


def lane_of(shape):
    return lax.broadcasted_iota(jnp.int32, shape, 1)


def join(pieces, lanes):
    rolled = [pltpu.roll(x, s % 128, 1) if s % 128 else x for x, s in pieces]
    left = jnp.where(lanes < 32, rolled[0], rolled[1])
    right = jnp.where(lanes < 96, rolled[2], rolled[3])
    return jnp.where(lanes < 64, left, right)


def join_two(first, shift_first, second, shift_second, lanes):
    a = pltpu.roll(first, shift_first % 128, 1) if shift_first % 128 else first
    b = pltpu.roll(second, shift_second % 128, 1) if shift_second % 128 else second
    return jnp.where(lanes < 64, a, b)


def to_tiles(parts):
    lanes = lane_of(parts[0][0].shape)
    tiles = []
    for pair in range(BLOCKS // 2):
        h, at = pair // 2, 64 * (pair % 2)
        x = [parts[q][h] for q in range(PARTS)]
        a = join([(x[s], 32 * s - at) for s in range(4)], lanes)
        c = join([(x[s], 32 * s - at - 32) for s in range(4)], lanes)
        b = join_two(x[4], -at, x[5], 64 - at, lanes)
        tiles.append((a, b, c))
    return tiles


def from_tiles(tiles):
    lanes = lane_of(tiles[0][0].shape)
    parts = []
    for q in range(4):
        halves = []
        for h in range(2):
            pieces = []
            for k in range(4):
                a, _, c = tiles[2 * h + k // 2]
                pieces.append((c if k % 2 else a, 32 * (k - q)))
            halves.append(join(pieces, lanes))
        parts.append(halves)
    parts.append([join_two(tiles[2 * h][1], 0, tiles[2 * h + 1][1], 64, lanes) for h in range(2)])
    parts.append([join_two(tiles[2 * h][1], 64, tiles[2 * h + 1][1], 0, lanes) for h in range(2)])
    return parts


def as_bf16(tiles):
    return [tuple(x.astype(bf16) for x in tile) for tile in tiles]


def block_operand(tiles, t):
    a, b, c = tiles[t // 2]
    return jnp.concatenate([c if t % 2 else a, b], axis=1)


def merge_blocks(sums):
    tiles = []
    for pair in range(BLOCKS // 2):
        one, two = sums[2 * pair], sums[2 * pair + 1]
        lanes = lane_of((one.shape[0], 128))
        b = jnp.where((lanes // 32) % 2 == 0, one[:, 128:], two[:, 128:])
        tiles.append((one[:, :128], b, two[:, :128]))
    return tiles


def order_sign(lanes):
    return jnp.where((lanes // 2) % 2 == 0, 1.0, -1.0).astype(f32)


def reversal():
    row = lax.broadcasted_iota(jnp.int32, (LOW, LOW), 0)
    return (row + lane_of((LOW, LOW)) == LOW - 1).astype(f32).astype(bf16)


def fold(pair, flip):
    x = jnp.concatenate(pair, axis=1)
    low = jnp.concatenate([x[i * GROUPS : i * GROUPS + HALF] for i in range(BAND)], axis=0)
    high = jnp.concatenate([x[i * GROUPS + HALF : (i + 1) * GROUPS] for i in range(BAND)], axis=0)
    high = dot(flip, high.astype(bf16)) * order_sign(lane_of(high.shape))
    both = (low.astype(bf16).astype(f32) + high, low.astype(bf16).astype(f32) - high)
    return [[x[:, :128], x[:, 128:]] for x in both]


def unfold(even, odd, flip):
    even, odd = jnp.concatenate(even, axis=1), jnp.concatenate(odd, axis=1)
    low = even + odd
    high = (even - odd) * order_sign(lane_of(low.shape))
    high = dot(flip, high.astype(bf16))
    pieces = []
    for i in range(BAND):
        rows = slice(i * HALF, (i + 1) * HALF)
        pieces += [low[rows], high[rows]]
    whole = jnp.concatenate(pieces, axis=0)
    return tuple(whole[:, 128 * n : 128 * (n + 1)] for n in range(3))


def stacked(operand, groups, width):
    order = (lane_of(operand.shape) % 32) // 2
    none = jnp.zeros_like(operand)
    return jnp.concatenate(
        [jnp.where(order // width == g, operand, none) for g in range(groups)], axis=0
    )


def analyse(parts, flip, table, ready):
    folded = [fold(pair, flip) for pair in parts]
    tiles = [as_bf16(to_tiles([x[odd] for x in folded])) for odd in (0, 1)]
    sums = []
    for t in range(BLOCKS):
        ready(t)
        reach = REACH[t]
        order = (lane_of((reach, 256)) % 16) // 2
        pieces = []
        for odd in (0, 1):
            operand = stacked(block_operand(tiles[odd], t), 2, 8)
            rows = pl.ds(STARTS[t] + odd * 8 * reach, 8 * reach)
            part = dot(table[rows, :], operand)
            total = part[:reach]
            for k in range(1, 8):
                total = jnp.where(order == k, part[k * reach : (k + 1) * reach], total)
            if t:
                pieces.append(jnp.zeros((8 * t, 256), f32))
            pieces.append(total)
        sums.append(jnp.concatenate(pieces, axis=0))
    return merge_blocks(sums)


def synthesise(tiles, table, ready):
    sums = ([], [])
    order = (lane_of((LOW, 256)) % 8) // 2
    for t in range(BLOCKS):
        ready(t)
        operand = block_operand(tiles, t)
        for odd in (0, 1):
            rows = operand[odd * GROUPS : (odd + 1) * GROUPS]
            part = dot(table[pl.ds(STEPS[t] + odd * 4 * LOW, 4 * LOW), :], stacked(rows, 4, 4))
            total = part[:LOW]
            for k in range(1, 4):
                total = jnp.where(order == k, part[k * LOW : (k + 1) * LOW], total)
            sums[odd].append(total)
    even, odd = merge_blocks(sums[0]), merge_blocks(sums[1])
    flip = reversal()
    return from_tiles([unfold(e, o, flip) for e, o in zip(even, odd)])


def slot_choice(degrees):
    shape = (DEGREES, DEGREES)
    row, column = lax.broadcasted_iota(jnp.int32, shape, 0), lane_of(shape)
    held = degrees[...] == 2 * (row % GROUPS) + row // GROUPS
    moved = row == SLOTS * (column % GROUPS) + column // GROUPS
    return dot(*[x.astype(f32).astype(bf16) for x in (held, moved)]).astype(bf16)


def permute_rows(matrix, tiles, dims=NN):
    out = []
    for tile in tiles:
        moved = dot(matrix, jnp.concatenate(tile, axis=1), dims)
        out.append(tuple(moved[:, 128 * n : 128 * (n + 1)] for n in range(3)))
    return out


def put_slots(parts, carried, stage, out):
    stride = SLOT_ROWS if carried is None else SENT_ROWS
    for j in range(SLOTS):
        for q in range(PARTS):
            for h in range(2):
                stage[pl.ds((j * PARTS + q) * 2 + h, GROUPS, stride=stride), :] = parts[q][h][
                    j * GROUPS : (j + 1) * GROUPS
                ]
    if carried is None:
        out[...] = stage[pl.ds(0, GROUPS * SLOT_ROWS), :].astype(bf16)
    else:
        rows = stage[...].reshape(GROUPS, SENT_ROWS, 128)[:, :SLOT_ROWS]
        more = carried[...].astype(f32).reshape(GROUPS, SLOT_ROWS, 128)
        both = jnp.concatenate([rows, more], axis=1)
        out[...] = both.reshape(GROUPS * SENT_ROWS, 128).astype(bf16)


def get_slots(received, stage):
    count = received.shape[0]
    stage[pl.ds(0, count), :] = received[...].astype(f32)
    return [
        [
            jnp.concatenate(
                [
                    stage[pl.ds((j * PARTS + q) * 2 + h, GROUPS, stride=count // GROUPS), :]
                    for j in range(SLOTS)
                ],
                axis=0,
            )
            for h in range(2)
        ]
        for q in range(PARTS)
    ]


def slot_rows_out(tiles, degrees, carried, stage, out):
    moved = permute_rows(slot_choice(degrees), as_bf16(tiles), TN)
    put_slots(from_tiles(moved), carried, stage, out)


def slot_rows_in(received, degrees, stage):
    tiles = as_bf16(to_tiles(get_slots(received, stage)))
    return as_bf16(permute_rows(slot_choice(degrees), tiles))


def table_copies(source, target, sems, bounds):
    copies = []
    for t in range(BLOCKS):
        rows = pl.ds(bounds[t], bounds[t + 1] - bounds[t])
        copies.append(pltpu.make_async_copy(source.at[rows, :], target.at[rows, :], sems.at[t]))
    return copies


def cot_place(i, q, h):
    row = (i * PARTS + q) * 3 + h
    which = sum(row >= cut for cut in COT_CUTS[1:3])
    return which, row - COT_CUTS[which]


def put_cotangent(turned, i, parts, wanted, spots):
    for q in parts:
        rows = slice(q * GROUPS, (q + 1) * GROUPS)
        for h in range(3):
            which, at = cot_place(i, q, h)
            if which in wanted:
                place, base, stride = spots[which]
                place[pl.ds(base + at, GROUPS, stride=stride), :] = turned[
                    rows, 128 * h : 128 * (h + 1)
                ]


def spread_kernel(fields, cotangent, forward_source, out, field, cot, forward, stage, sems):
    copies = [
        pltpu.make_async_copy(forward_source, forward, sems.at[BAND]),
        *[pltpu.make_async_copy(fields.at[i], field.at[i], sems.at[i]) for i in range(BAND)],
    ]
    fetch = pltpu.make_async_copy(cotangent.at[0], cot, sems.at[BAND + 1])
    for copy in (*copies, fetch):
        copy.start()
    copies[0].wait()
    for i in range(BAND):
        copies[i + 1].wait()
        spectra = dot(field[i], forward[...], TN)
        for q in range(PARTS):
            rows = slice(q * GROUPS, (q + 1) * GROUPS)
            at = (i * PARTS + q) * 2
            for h in range(2):
                stage[pl.ds(at + h, GROUPS, stride=SENT_ROWS), :] = spectra[
                    rows, 128 * h : 128 * (h + 1)
                ]
    fetch.wait()
    turned = jnp.transpose(cot[:, : 4 * GROUPS].astype(f32))
    put_cotangent(turned, 0, range(4), (0,), ((stage, SPEC_ROWS, SENT_ROWS),))
    out[...] = stage[...].astype(bf16)


def spread_rest_kernel(cotangent, early, cot_two, cot_three, cot, stages, sems):
    copies = [pltpu.make_async_copy(cotangent.at[i], cot.at[i], sems.at[i]) for i in range(BAND)]
    for copy in copies:
        copy.start()
    two, three = stages.at[0], stages.at[1]
    for i in range(BAND):
        copies[i].wait()
        turned = jnp.transpose(cot[i].astype(f32))
        put_cotangent(
            turned, i, range(PARTS), (1, 2), (None, (two, 0, SLOT_ROWS), (three, 0, SLOT_ROWS))
        )
    for row in range(COT_CUTS[3] - COT_CUTS[2], SLOT_ROWS):
        three[pl.ds(row, GROUPS, stride=SLOT_ROWS), :] = jnp.zeros((GROUPS, 128), f32)
    cot_two[...] = two[...].astype(bf16)
    cot_three[...] = three[...].astype(bf16)


def first_kernel(
    received, table, degrees, carried_source, out, stage_in, stage, carried, sem
):
    fetch = pltpu.make_async_copy(carried_source, carried, sem)
    fetch.start()
    stage_in[...] = received[...].astype(f32)
    parts = [
        [
            jnp.concatenate(
                [
                    stage_in[pl.ds((i * PARTS + q) * 2 + h, GROUPS, stride=SENT_ROWS), :]
                    for i in range(BAND)
                ],
                axis=0,
            )
            for h in range(2)
        ]
        for q in range(PARTS)
    ]
    sums = analyse(parts, reversal(), table, lambda t: None)
    fetch.wait()
    slot_rows_out(sums, degrees, carried, stage, out)


def gelu_slope(x):
    c = np.float32(np.sqrt(2.0 / np.pi))
    squared = x * x
    th = jnp.tanh(c * (x + 0.044715 * (x * squared)))
    return 0.5 * (1.0 + th) + (0.5 * c) * x * (1.0 - th * th) * (1.0 + (3 * 0.044715) * squared)


def middle_kernel(
    received, one, two, analysis, synthesis, degrees, inverse_source, turned_source, out,
    inverse, inverse_t, rows_one, rows_two, stage_one, stage_two, stage, table, table_s, row_sems, sems, sems_s,
):
    copies_s = table_copies(synthesis, table_s, sems_s, STEPS)
    copies = table_copies(analysis, table, sems, STARTS)
    fetches = (
        pltpu.make_async_copy(one.at[:, pl.ds(32, 16), :], rows_one, row_sems.at[0]),
        pltpu.make_async_copy(two.at[:, pl.ds(16, 32), :], rows_two, row_sems.at[1]),
        pltpu.make_async_copy(inverse_source, inverse, row_sems.at[2]),
        pltpu.make_async_copy(turned_source, inverse_t, row_sems.at[3]),
    )
    for copy in (*copies_s, *fetches, *copies):
        copy.start()
    tiles = slot_rows_in(received, degrees, stage)
    synth = synthesise(tiles, table_s, lambda t: copies_s[t].wait())
    for fetch in fetches:
        fetch.wait()
    stage_one[...] = rows_one[...].astype(f32).reshape(GROUPS * 16, 128)
    stage_two[...] = rows_two[...].astype(f32).reshape(GROUPS * 32, 128)
    spots = ((stage_one, SPEC_ROWS - 32, 16), (stage_two, 8, 32), (stage, SLOT_ROWS, SENT_ROWS))

    def cot_rows(i, q, h):
        which, at = cot_place(i, q, h)
        place, base, stride = spots[which]
        return place[pl.ds(base + at, GROUPS, stride=stride), :]

    parts = []
    for q in range(PARTS):
        response = dot(jnp.concatenate(synth[q], axis=1).astype(bf16), inverse_t[...])
        cotangent = jnp.concatenate(
            [
                jnp.concatenate([cot_rows(i, q, h) for h in range(3)], axis=1)
                for i in range(BAND)
            ],
            axis=0,
        )
        upstream = (cotangent * gelu_slope(response)).astype(bf16)
        grad = dot(upstream, inverse[...])
        parts.append([grad[:, :128], grad[:, 128:]])
    sums = analyse(parts, reversal(), table, lambda t: copies[t].wait())
    slot_rows_out(sums, degrees, None, stage, out)


def last_kernel(received, table, degrees, out, stage, stage_out):
    tiles = slot_rows_in(received, degrees, stage)
    synth = synthesise(tiles, table, lambda t: None)
    for q in range(PARTS):
        for h in range(2):
            scaled = synth[q][h]
            for i in range(BAND):
                at = (i * PARTS + q) * 2 + h
                stage_out[pl.ds(at, GROUPS, stride=LAST_ROWS), :] = scaled[
                    i * GROUPS : (i + 1) * GROUPS
                ]
    for row in range(SPEC_ROWS, LAST_ROWS):
        stage_out[pl.ds(row, GROUPS, stride=LAST_ROWS), :] = jnp.zeros((GROUPS, 128), f32)
    out[...] = stage_out[...].astype(bf16)


def gather_kernel(received, forward, cotangent, weight_grads, out, stage):
    stage[...] = received[...].astype(f32)
    for i in range(BAND):
        halves = [
            jnp.concatenate(
                [
                    stage[pl.ds((i * PARTS + q) * 2 + h, GROUPS, stride=LAST_ROWS), :]
                    for q in range(PARTS)
                ],
                axis=0,
            )
            for h in range(2)
        ]
        rows = jnp.concatenate(halves, axis=1).astype(bf16)
        delta = dot(forward[...], rows, NT)
        out[i] = (cotangent[i].astype(f32) + delta).astype(bf16)


def mix_kernel(adjoint, received, weights, turn, *rest):
    carried, out, kept, stage = (None, *rest) if adjoint else rest
    parts = get_slots(received, stage)
    results = []
    for j in range(SLOTS):
        own = slice(j * GROUPS, (j + 1) * GROUPS)
        held = jnp.concatenate(
            [jnp.concatenate([x[own] for x in parts[q]], axis=1) for q in range(PARTS)], axis=0
        ).astype(bf16)
        kept[j] = held
        turned = dot(held, turn[...])
        if adjoint:
            turned = -turned
        turned = turned.astype(bf16)
        dims = NN if adjoint else TN
        results.append(dot(weights[j, 0], held, dims) + dot(weights[j, 1], turned, dims))
    mixed = [
        [
            jnp.concatenate(
                [x[q * GROUPS : (q + 1) * GROUPS, 128 * h : 128 * (h + 1)] for x in results],
                axis=0,
            )
            for h in range(2)
        ]
        for q in range(PARTS)
    ]
    put_slots(mixed, carried, stage, out)


VMEM = pl.BlockSpec(memory_space=pltpu.VMEM)
SMEM = pl.BlockSpec(memory_space=pltpu.SMEM)
ANY = pl.BlockSpec(memory_space=pl.ANY)


def call(kernel, out_shape, in_specs, scratch, flops, moved, name, limit=24):
    several = isinstance(out_shape, list)
    return pl.pallas_call(
        kernel,
        out_shape=out_shape,
        in_specs=in_specs,
        out_specs=[VMEM] * len(out_shape) if several else VMEM,
        scratch_shapes=scratch,
        compiler_params=pltpu.CompilerParams(vmem_limit_bytes=limit * 2**20),
        cost_estimate=pl.CostEstimate(flops=flops, bytes_accessed=moved, transcendentals=0),
        name=name,
    )


def message(rows):
    return jax.ShapeDtypeStruct((GROUPS * rows, 128), bf16)


def stage_of(rows):
    return pltpu.VMEM((GROUPS * rows, 128), f32)


TABLE = pltpu.VMEM((STARTS[-1], LATS), bf16)
TABLE_S = pltpu.VMEM((STEPS[-1], 256), bf16)


def sems(count):
    return pltpu.SemaphoreType.DMA((count,))


def in_hbm(array):
    return pltpu.with_memory_space_constraint(array, pltpu.HBM)


def spread(fields, cotangent, forward):
    return call(
        spread_kernel,
        message(SENT_ROWS),
        [ANY, ANY, ANY],
        [
            pltpu.VMEM((BAND, LONS, CHANNELS), bf16), pltpu.VMEM((LONS, CHANNELS), bf16),
            pltpu.VMEM((LONS, COEFS), bf16), stage_of(SENT_ROWS), sems(BAND + 2),
        ],
        3 * 10**8, 3 * 10**6, "spread",
    )(in_hbm(fields), in_hbm(cotangent), in_hbm(forward))


def spread_rest(cotangent, early):
    return call(
        spread_rest_kernel,
        [pltpu.HBM((GROUPS * SLOT_ROWS, 128), bf16)] * 2,
        [ANY, ANY],
        [
            pltpu.VMEM((BAND, LONS, CHANNELS), bf16),
            pltpu.VMEM((2, GROUPS * SLOT_ROWS, 128), f32), sems(BAND),
        ],
        10**7, 3 * 10**6, "spread_rest",
    )(in_hbm(cotangent), early)


def first(received, weighted, degrees, carried):
    return call(
        first_kernel,
        message(SENT_ROWS),
        [VMEM, VMEM, VMEM, ANY],
        [
            stage_of(SENT_ROWS), stage_of(SENT_ROWS),
            pltpu.VMEM((GROUPS * SLOT_ROWS, 128), bf16), pltpu.SemaphoreType.DMA,
        ],
        10**9, 6 * 10**6, "first",
    )(received, weighted, degrees, in_hbm(carried))


def middle(
    received, one, two, analysis, synthesis, degrees, inverse, inverse_t
):
    return call(
        middle_kernel,
        message(SLOT_ROWS),
        [VMEM, ANY, ANY, ANY, ANY, VMEM, ANY, ANY],
        [
            pltpu.VMEM((LONS, COEFS), bf16), pltpu.VMEM((COEFS, LONS), bf16),
            pltpu.VMEM((GROUPS, 16, 128), bf16), pltpu.VMEM((GROUPS, 32, 128), bf16),
            stage_of(16), stage_of(32), stage_of(SENT_ROWS),
            TABLE, TABLE_S, sems(4), sems(BLOCKS), sems(BLOCKS),
        ],
        3 * 10**9, 12 * 10**6, "middle",
    )(received, one, two, in_hbm(analysis), in_hbm(synthesis), degrees,
      in_hbm(inverse), in_hbm(inverse_t))


def last(received, table, degrees):
    return call(
        last_kernel,
        pltpu.HBM((GROUPS * LAST_ROWS, 128), bf16),
        [VMEM, VMEM, VMEM],
        [stage_of(SLOT_ROWS), stage_of(LAST_ROWS)],
        10**9, 7 * 10**6, "last",
    )(received, table, degrees)


def gather(received, forward, cotangent, weight_grads):
    return call(
        gather_kernel,
        jax.ShapeDtypeStruct((BAND, LONS, CHANNELS), bf16),
        [VMEM, VMEM, VMEM, ANY],
        [stage_of(LAST_ROWS)],
        3 * 10**8, 3 * 10**6, "gather",
    )(received, forward, cotangent, in_hbm(weight_grads))


def mix(adjoint, received, weights, turn, *carried):
    rows = SLOT_ROWS if adjoint else SENT_ROWS
    return call(
        functools.partial(mix_kernel, adjoint),
        [message(rows), jax.ShapeDtypeStruct((SLOTS, CHANNELS, COEFS), bf16)],
        [VMEM, VMEM, VMEM] + [VMEM] * len(carried),
        [stage_of(rows)],
        6 * 10**8, 3 * 10**6, "adjoint_mix" if adjoint else "mix",
    )(received, weights, turn, *carried)


def exchange(rows):
    count = rows.shape[0] // GROUPS
    out = lax.all_to_all(
        rows.reshape(GROUPS, count, 128), "lat", split_axis=0, concat_axis=0, tiled=True,
    )
    return out.reshape(GROUPS * count, 128)


def gradient_kernel(coeffs_source, grads_source, turn, out, coeffs, grads, sems):
    copies = []
    for j in range(SLOTS):
        copies.append(
            [
                pltpu.make_async_copy(source.at[:, j], held.at[:, j], sems.at[2 * j + n])
                for n, (source, held) in enumerate(((coeffs_source, coeffs), (grads_source, grads)))
            ]
        )
    for pair in copies:
        for copy in pair:
            copy.start()
    samples = range(coeffs.shape[0])
    for j in range(SLOTS):
        copies[j][0].wait()
        left = [coeffs[s, j] for s in samples]
        turned = [dot(x, turn[...]).astype(bf16) for x in left]
        copies[j][1].wait()
        right = jnp.concatenate([grads[s, j] for s in samples], axis=1)
        out[j, 0] = dot(jnp.concatenate(left, axis=1), right, NT).astype(bf16)
        out[j, 1] = dot(jnp.concatenate(turned, axis=1), right, NT).astype(bf16)


def weight_gradient(coeffs, grads, turn):
    held = pltpu.VMEM(coeffs.shape, bf16)
    return call(
        gradient_kernel,
        jax.ShapeDtypeStruct((SLOTS, 2, CHANNELS, CHANNELS), bf16),
        [ANY, ANY, VMEM],
        [held, held, sems(2 * SLOTS)],
        5 * 10**9, 8 * 10**6, "weight_gradient",
    )(in_hbm(coeffs), in_hbm(grads), turn)


def local(fields, cotangent, weights, degree_of):
    table = {k: jnp.asarray(v) for k, v in constants().items()}
    degrees = degree_of[None, :]
    sent = spread(fields[0], cotangent[0], table["forward"])
    cot_two, cot_three = spread_rest(cotangent[0], sent)
    one = exchange(sent)
    two = exchange(first(one, table["weighted"], degrees, cot_two))
    filtered, coeffs = mix(False, two, weights, table["turn"], cot_three)
    all_coeffs = lax.all_gather(coeffs, "batch", axis=0)
    three = exchange(filtered)
    as_sent = (GROUPS, SENT_ROWS, 128)
    four = exchange(
        middle(
            three, one.reshape(as_sent), two.reshape(as_sent), table["analysis"],
            table["synthesis"], degrees,
            table["inverse"], table["inverse_t"],
        )
    )
    grad_coeffs, grads = mix(True, four, weights, table["turn"])
    all_grads = lax.all_gather(grads, "batch", axis=0)
    grad_weights = weight_gradient(all_coeffs, all_grads, table["turn"])
    five = exchange(grad_coeffs)
    six = exchange(last(five, table["weighted_synthesis"], degrees))
    grad_fields = gather(six, table["forward"], cotangent[0], grad_weights)[None]
    return grad_fields, grad_weights


def solution(mesh):
    return jax.shard_map(
        local,
        mesh=mesh,
        in_specs=(
            P("batch", "lat", None, None),
            P("batch", "lat", None, None),
            P("lat", None, None, None),
            P(),
        ),
        out_specs=(P("batch", "lat", None, None), P("lat", None, None, None)),
        check_vma=False,
    )
```

```python
import functools

import jax
import jax.numpy as jnp
import numpy as np
from jax import lax
from jax.experimental import pallas as pl
from jax.experimental.pallas import tpu as pltpu
from jax.sharding import PartitionSpec as P

LATS = 192
LONS = 384
ORDERS = 128
DEGREES = 128
CHANNELS = 384

GROUPS = 64
BAND = LATS // GROUPS
PARTS = CHANNELS // GROUPS
SLOTS = DEGREES // GROUPS
COEFS = 2 * ORDERS
BLOCKS = ORDERS // 16
SPEC_ROWS = BAND * PARTS * 2
SENT_ROWS = 48
COT_CUTS = (0, 12, 36, 54)
SLOT_ROWS = SLOTS * PARTS * 2
LAST_ROWS = 40
HALF = GROUPS // 2
LOW = LATS // 2
REACH = [DEGREES // 2 - 8 * t for t in range(BLOCKS)]
STARTS = [16 * sum(REACH[:t]) for t in range(BLOCKS + 1)]
STEPS = [8 * LOW * t for t in range(BLOCKS + 1)]

f32 = jnp.float32
bf16 = jnp.bfloat16
TN = (((0,), (0,)), ((), ()))
NN = (((1,), (0,)), ((), ()))
NT = (((1,), (1,)), ((), ()))


def legendre_table():
    colatitude = np.pi * (np.arange(LATS) + 0.5) / LATS
    cosine, sine = np.cos(colatitude), np.sin(colatitude)
    order = np.arange(ORDERS, dtype=np.float64)[:, None]
    steps = np.arange(1, ORDERS)
    growth = np.concatenate([[0.0], np.cumsum(0.5 * np.log((2.0 * steps + 1.0) / (2.0 * steps)))])
    diagonal = np.exp(0.5 * np.log(1.0 / (4.0 * np.pi)) + growth[:, None] + order * np.log(sine))
    table = np.zeros((ORDERS, DEGREES, LATS))
    for degree in range(DEGREES):
        table[degree, degree] = diagonal[degree]
        if degree >= 1:
            m = degree - 1
            table[m, degree] = np.sqrt(2.0 * m + 3.0) * cosine * table[m, m]
        if degree >= 2:
            m = order[: degree - 1]
            lead = np.sqrt((4.0 * degree**2 - 1.0) / (degree**2 - m**2))
            back = np.sqrt(((degree - 1.0) ** 2 - m**2) / (4.0 * (degree - 1.0) ** 2 - 1.0))
            table[: degree - 1, degree] = lead * (
                cosine * table[: degree - 1, degree - 1] - back * table[: degree - 1, degree - 2]
            )
    return table, 2.0 * np.pi * np.pi / LATS * sine


def fourier_tables():
    lon = np.arange(LONS)[:, None]
    order = np.arange(ORDERS)[None, :]
    phase = 2.0 * np.pi * (lon * order % LONS) / LONS
    forward = np.stack([np.cos(phase), -np.sin(phase)], axis=2).reshape(LONS, COEFS) / LONS
    doubled = np.where(order == 0, 1.0, 2.0)
    inverse = np.stack([doubled * np.cos(phase), -doubled * np.sin(phase)], axis=2)
    return forward.astype(bf16), inverse.reshape(LONS, COEFS).astype(bf16)


@functools.cache
def constants():
    table, quadrature = legendre_table()
    low = (np.arange(HALF)[None, :] * BAND + np.arange(BAND)[:, None]).reshape(-1)

    def for_analysis(values):
        values = values.astype(bf16)
        return np.concatenate(
            [
                np.concatenate([values[16 * t + k + 8 * g, 16 * t + odd :: 2] for g in (0, 1)], axis=1)
                for t in range(BLOCKS)
                for odd in (0, 1)
                for k in range(8)
            ],
            axis=0,
        )

    analysis = for_analysis(table[:, :, low])
    weighted = for_analysis((table * quadrature)[:, :, low])

    def for_synthesis(values):
        values = values.astype(bf16)
        return np.concatenate(
            [
                np.concatenate([values[16 * t + k + 4 * g, odd::2].T for g in range(4)], axis=1)
                for t in range(BLOCKS)
                for odd in (0, 1)
                for k in range(4)
            ],
            axis=0,
        )

    synthesis = for_synthesis(table[:, :, low])
    half = 8 * LOW * (BLOCKS // 2)
    upper = synthesis[half:].reshape(BLOCKS // 4, 2, 8 * LOW, 4, 2, HALF)[:, :, :, :, 1]
    upper = upper.reshape(BLOCKS // 4, 2, 8 * LOW, 128).transpose(0, 2, 1, 3).reshape(-1, 256)
    synthesis = np.concatenate([synthesis[:half], upper], axis=0)
    weighted_synthesis = for_synthesis((table * quadrature)[:, :, low])
    forward, inverse = fourier_tables()
    turn = np.zeros((COEFS, COEFS), np.float32)
    even = np.arange(0, COEFS, 2)
    turn[even + 1, even] = -1.0
    turn[even, even + 1] = 1.0
    return dict(
        analysis=analysis,
        weighted=weighted,
        synthesis=synthesis,
        weighted_synthesis=weighted_synthesis,
        forward=forward,
        inverse=inverse,
        inverse_t=np.ascontiguousarray(inverse.T),
        turn=turn.astype(bf16),
    )


def dot(left, right, dims=NN):
    return lax.dot_general(left, right, dims, preferred_element_type=f32)


def lane_of(shape):
    return lax.broadcasted_iota(jnp.int32, shape, 1)


def join(pieces, lanes):
    rolled = [pltpu.roll(x, s % 128, 1) if s % 128 else x for x, s in pieces]
    left = jnp.where(lanes < 32, rolled[0], rolled[1])
    right = jnp.where(lanes < 96, rolled[2], rolled[3])
    return jnp.where(lanes < 64, left, right)


def join_two(first, shift_first, second, shift_second, lanes):
    a = pltpu.roll(first, shift_first % 128, 1) if shift_first % 128 else first
    b = pltpu.roll(second, shift_second % 128, 1) if shift_second % 128 else second
    return jnp.where(lanes < 64, a, b)


def to_tiles(parts):
    lanes = lane_of(parts[0][0].shape)
    tiles = []
    for pair in range(BLOCKS // 2):
        h, at = pair // 2, 64 * (pair % 2)
        x = [parts[q][h] for q in range(PARTS)]
        a = join([(x[s], 32 * s - at) for s in range(4)], lanes)
        c = join([(x[s], 32 * s - at - 32) for s in range(4)], lanes)
        b = join_two(x[4], -at, x[5], 64 - at, lanes)
        tiles.append((a, b, c))
    return tiles


def from_tiles(tiles):
    lanes = lane_of(tiles[0][0].shape)
    parts = []
    for q in range(4):
        halves = []
        for h in range(2):
            pieces = []
            for k in range(4):
                a, _, c = tiles[2 * h + k // 2]
                pieces.append((c if k % 2 else a, 32 * (k - q)))
            halves.append(join(pieces, lanes))
        parts.append(halves)
    parts.append([join_two(tiles[2 * h][1], 0, tiles[2 * h + 1][1], 64, lanes) for h in range(2)])
    parts.append([join_two(tiles[2 * h][1], 64, tiles[2 * h + 1][1], 0, lanes) for h in range(2)])
    return parts


def as_bf16(tiles):
    return [tuple(x.astype(bf16) for x in tile) for tile in tiles]


def block_operand(tiles, t):
    a, b, c = tiles[t // 2]
    return jnp.concatenate([c if t % 2 else a, b], axis=1)


def merge_blocks(sums):
    tiles = []
    for pair in range(BLOCKS // 2):
        one, two = sums[2 * pair], sums[2 * pair + 1]
        lanes = lane_of((one.shape[0], 128))
        b = jnp.where((lanes // 32) % 2 == 0, one[:, 128:], two[:, 128:])
        tiles.append((one[:, :128], b, two[:, :128]))
    return tiles


def order_sign(lanes):
    return jnp.where((lanes // 2) % 2 == 0, 1.0, -1.0).astype(f32)


def reversal():
    row = lax.broadcasted_iota(jnp.int32, (LOW, LOW), 0)
    return (row + lane_of((LOW, LOW)) == LOW - 1).astype(f32).astype(bf16)


def fold(pair, flip):
    x = jnp.concatenate(pair, axis=1)
    low = jnp.concatenate([x[i * GROUPS : i * GROUPS + HALF] for i in range(BAND)], axis=0)
    high = jnp.concatenate([x[i * GROUPS + HALF : (i + 1) * GROUPS] for i in range(BAND)], axis=0)
    high = dot(flip, high.astype(bf16)) * order_sign(lane_of(high.shape))
    both = (low.astype(bf16).astype(f32) + high, low.astype(bf16).astype(f32) - high)
    return [[x[:, :128], x[:, 128:]] for x in both]


def unfold(even, odd, flip):
    even, odd = jnp.concatenate(even, axis=1), jnp.concatenate(odd, axis=1)
    low = even + odd
    high = (even - odd) * order_sign(lane_of(low.shape))
    high = dot(flip, high.astype(bf16))
    pieces = []
    for i in range(BAND):
        rows = slice(i * HALF, (i + 1) * HALF)
        pieces += [low[rows], high[rows]]
    whole = jnp.concatenate(pieces, axis=0)
    return tuple(whole[:, 128 * n : 128 * (n + 1)] for n in range(3))


def stacked(operand, groups, width):
    order = (lane_of(operand.shape) % 32) // 2
    none = jnp.zeros_like(operand)
    return jnp.concatenate(
        [jnp.where(order // width == g, operand, none) for g in range(groups)], axis=0
    )


def analyse(parts, flip, table, ready):
    folded = [fold(pair, flip) for pair in parts]
    tiles = [as_bf16(to_tiles([x[odd] for x in folded])) for odd in (0, 1)]
    sums = []
    for t in range(BLOCKS):
        ready(t)
        reach = REACH[t]
        order = (lane_of((reach, 256)) % 16) // 2
        pieces = []
        for odd in (0, 1):
            operand = stacked(block_operand(tiles[odd], t), 2, 8)
            rows = pl.ds(STARTS[t] + odd * 8 * reach, 8 * reach)
            part = dot(table[rows, :], operand)
            total = part[:reach]
            for k in range(1, 8):
                total = jnp.where(order == k, part[k * reach : (k + 1) * reach], total)
            if t:
                pieces.append(jnp.zeros((8 * t, 256), f32))
            pieces.append(total)
        sums.append(jnp.concatenate(pieces, axis=0))
    return merge_blocks(sums)


def synthesise(tiles, table, ready, packed=False):
    sums = ([], [])
    order = (lane_of((LOW, 256)) % 8) // 2
    for t in range(BLOCKS):
        ready(t)
        operand = block_operand(tiles, t)
        for odd in (0, 1):
            least, start, lanes = 0, STEPS[t], pl.ds(0, 256)
            if packed and t >= BLOCKS // 2:
                least, start, lanes = HALF, STEPS[(t + BLOCKS // 2) // 2], pl.ds(t % 2 * 128, 128)
            rows = operand[odd * GROUPS + least : (odd + 1) * GROUPS]
            part = dot(table[pl.ds(start + odd * 4 * LOW, 4 * LOW), lanes], stacked(rows, 4, 4))
            total = part[:LOW]
            for k in range(1, 4):
                total = jnp.where(order == k, part[k * LOW : (k + 1) * LOW], total)
            sums[odd].append(total)
    even, odd = merge_blocks(sums[0]), merge_blocks(sums[1])
    flip = reversal()
    return from_tiles([unfold(e, o, flip) for e, o in zip(even, odd)])


def slot_choice(degrees):
    shape = (DEGREES, DEGREES)
    row, column = lax.broadcasted_iota(jnp.int32, shape, 0), lane_of(shape)
    held = degrees[...] == 2 * (row % GROUPS) + row // GROUPS
    moved = row == SLOTS * (column % GROUPS) + column // GROUPS
    return dot(*[x.astype(f32).astype(bf16) for x in (held, moved)]).astype(bf16)


def permute_rows(matrix, tiles, dims=NN):
    out = []
    for tile in tiles:
        moved = dot(matrix, jnp.concatenate(tile, axis=1), dims)
        out.append(tuple(moved[:, 128 * n : 128 * (n + 1)] for n in range(3)))
    return out


def put_slots(parts, carried, stage, out):
    stride = SLOT_ROWS if carried is None else SENT_ROWS
    for j in range(SLOTS):
        for q in range(PARTS):
            for h in range(2):
                stage[pl.ds((j * PARTS + q) * 2 + h, GROUPS, stride=stride), :] = parts[q][h][
                    j * GROUPS : (j + 1) * GROUPS
                ]
    if carried is None:
        out[...] = stage[pl.ds(0, GROUPS * SLOT_ROWS), :].astype(bf16)
    else:
        rows = stage[...].reshape(GROUPS, SENT_ROWS, 128)[:, :SLOT_ROWS]
        more = carried[...].astype(f32).reshape(GROUPS, SLOT_ROWS, 128)
        both = jnp.concatenate([rows, more], axis=1)
        out[...] = both.reshape(GROUPS * SENT_ROWS, 128).astype(bf16)


def get_slots(received, stage):
    count = received.shape[0]
    stage[pl.ds(0, count), :] = received[...].astype(f32)
    return [
        [
            jnp.concatenate(
                [
                    stage[pl.ds((j * PARTS + q) * 2 + h, GROUPS, stride=count // GROUPS), :]
                    for j in range(SLOTS)
                ],
                axis=0,
            )
            for h in range(2)
        ]
        for q in range(PARTS)
    ]


def slot_rows_out(tiles, degrees, carried, stage, out):
    moved = permute_rows(slot_choice(degrees), as_bf16(tiles), TN)
    put_slots(from_tiles(moved), carried, stage, out)


def slot_rows_in(received, degrees, stage):
    tiles = as_bf16(to_tiles(get_slots(received, stage)))
    return as_bf16(permute_rows(slot_choice(degrees), tiles))


def table_copies(source, target, sems, bounds):
    copies = []
    for t in range(len(bounds) - 1):
        rows = pl.ds(bounds[t], bounds[t + 1] - bounds[t])
        copies.append(pltpu.make_async_copy(source.at[rows, :], target.at[rows, :], sems.at[t]))
    return copies


def cot_place(i, q, h):
    row = (i * PARTS + q) * 3 + h
    which = sum(row >= cut for cut in COT_CUTS[1:3])
    return which, row - COT_CUTS[which]


def spread_kernel(
    fields, cotangent, forward_source, out, cot_two, cot_three, field, cot, forward, stages, sems
):
    copies = []
    fetch = pltpu.make_async_copy(forward_source, forward, sems.at[2 * BAND])
    fetch.start()
    for i in range(BAND):
        copies.append(
            (
                pltpu.make_async_copy(fields.at[i], field.at[i], sems.at[2 * i]),
                pltpu.make_async_copy(cotangent.at[i], cot.at[i], sems.at[2 * i + 1]),
            )
        )
    for pair in copies:
        for copy in pair:
            copy.start()
    stage, stage_two, stage_three = stages.at[0], stages.at[1], stages.at[2]
    spots = ((stage, SPEC_ROWS, SENT_ROWS), (stage_two, 0, SLOT_ROWS), (stage_three, 0, SLOT_ROWS))
    for i in range(BAND):
        if i == 0:
            fetch.wait()
        copies[i][0].wait()
        spectra = dot(field[i], forward[...], TN)
        for q in range(PARTS):
            rows = slice(q * GROUPS, (q + 1) * GROUPS)
            at = (i * PARTS + q) * 2
            for h in range(2):
                stage[pl.ds(at + h, GROUPS, stride=SENT_ROWS), :] = spectra[
                    rows, 128 * h : 128 * (h + 1)
                ]
        copies[i][1].wait()
        turned = jnp.transpose(cot[i].astype(f32))
        for q in range(PARTS):
            rows = slice(q * GROUPS, (q + 1) * GROUPS)
            for h in range(3):
                which, at = cot_place(i, q, h)
                place, base, stride = spots[which]
                place[pl.ds(base + at, GROUPS, stride=stride), :] = turned[
                    rows, 128 * h : 128 * (h + 1)
                ]
    for row in range(COT_CUTS[3] - COT_CUTS[2], SLOT_ROWS):
        stage_three[pl.ds(row, GROUPS, stride=SLOT_ROWS), :] = jnp.zeros((GROUPS, 128), f32)
    out[...] = stage[...].astype(bf16)
    short = GROUPS * SLOT_ROWS
    cot_two[...] = stage_two[pl.ds(0, short), :].astype(bf16)
    cot_three[...] = stage_three[pl.ds(0, short), :].astype(bf16)


def first_kernel(
    received, table, degrees, carried, out, stage_in, stage
):
    stage_in[...] = received[...].astype(f32)
    parts = [
        [
            jnp.concatenate(
                [
                    stage_in[pl.ds((i * PARTS + q) * 2 + h, GROUPS, stride=SENT_ROWS), :]
                    for i in range(BAND)
                ],
                axis=0,
            )
            for h in range(2)
        ]
        for q in range(PARTS)
    ]
    sums = analyse(parts, reversal(), table, lambda t: None)
    slot_rows_out(sums, degrees, carried, stage, out)


def gelu_slope(x):
    c = np.float32(np.sqrt(2.0 / np.pi))
    squared = x * x
    th = jnp.tanh(c * (x + 0.044715 * (x * squared)))
    return 0.5 * (1.0 + th) + (0.5 * c) * x * (1.0 - th * th) * (1.0 + (3 * 0.044715) * squared)


def middle_kernel(
    received, one, two, analysis, synthesis, degrees, inverse_source, turned_source, out,
    inverse, inverse_t, rows_one, rows_two, stage_one, stage_two, stage, table, table_s, row_sems, sems, sems_s,
):
    copies_s = table_copies(synthesis, table_s, sems_s, STEPS[:7])
    copies = table_copies(analysis, table, sems, STARTS)
    fetches = (
        pltpu.make_async_copy(one.at[:, pl.ds(32, 16), :], rows_one, row_sems.at[0]),
        pltpu.make_async_copy(two.at[:, pl.ds(16, 32), :], rows_two, row_sems.at[1]),
        pltpu.make_async_copy(inverse_source, inverse, row_sems.at[2]),
        pltpu.make_async_copy(turned_source, inverse_t, row_sems.at[3]),
    )
    for copy in (*copies_s, *fetches, *copies):
        copy.start()
    tiles = slot_rows_in(received, degrees, stage)

    def ready(t):
        if t < BLOCKS // 2:
            copies_s[t].wait()
        elif t % 2 == 0:
            copies_s[(t + BLOCKS // 2) // 2].wait()

    synth = synthesise(tiles, table_s, ready, True)
    for fetch in fetches:
        fetch.wait()
    stage_one[...] = rows_one[...].astype(f32).reshape(GROUPS * 16, 128)
    stage_two[...] = rows_two[...].astype(f32).reshape(GROUPS * 32, 128)
    spots = ((stage_one, SPEC_ROWS - 32, 16), (stage_two, 8, 32), (stage, SLOT_ROWS, SENT_ROWS))

    def cot_rows(i, q, h):
        which, at = cot_place(i, q, h)
        place, base, stride = spots[which]
        return place[pl.ds(base + at, GROUPS, stride=stride), :]

    parts = []
    for q in range(PARTS):
        response = dot(jnp.concatenate(synth[q], axis=1).astype(bf16), inverse_t[...])
        cotangent = jnp.concatenate(
            [
                jnp.concatenate([cot_rows(i, q, h) for h in range(3)], axis=1)
                for i in range(BAND)
            ],
            axis=0,
        )
        upstream = (cotangent * gelu_slope(response)).astype(bf16)
        grad = dot(upstream, inverse[...])
        parts.append([grad[:, :128], grad[:, 128:]])
    sums = analyse(parts, reversal(), table, lambda t: copies[t].wait())
    slot_rows_out(sums, degrees, None, stage, out)


def last_kernel(received, table, degrees, out, stage, stage_out):
    tiles = slot_rows_in(received, degrees, stage)
    synth = synthesise(tiles, table, lambda t: None)
    for q in range(PARTS):
        for h in range(2):
            scaled = synth[q][h]
            for i in range(BAND):
                at = (i * PARTS + q) * 2 + h
                stage_out[pl.ds(at, GROUPS, stride=LAST_ROWS), :] = scaled[
                    i * GROUPS : (i + 1) * GROUPS
                ]
    for row in range(SPEC_ROWS, LAST_ROWS):
        stage_out[pl.ds(row, GROUPS, stride=LAST_ROWS), :] = jnp.zeros((GROUPS, 128), f32)
    out[...] = stage_out[...].astype(bf16)


def gather_kernel(received, forward, cotangent, weight_grads, out, stage):
    stage[...] = received[...].astype(f32)
    for i in range(BAND):
        halves = [
            jnp.concatenate(
                [
                    stage[pl.ds((i * PARTS + q) * 2 + h, GROUPS, stride=LAST_ROWS), :]
                    for q in range(PARTS)
                ],
                axis=0,
            )
            for h in range(2)
        ]
        rows = jnp.concatenate(halves, axis=1).astype(bf16)
        delta = dot(forward[...], rows, NT)
        out[i] = (cotangent[i].astype(f32) + delta).astype(bf16)


def mix_kernel(adjoint, received, weights, turn, *rest):
    carried, out, kept, stage = (None, *rest) if adjoint else rest
    parts = get_slots(received, stage)
    results = []
    for j in range(SLOTS):
        own = slice(j * GROUPS, (j + 1) * GROUPS)
        held = jnp.concatenate(
            [jnp.concatenate([x[own] for x in parts[q]], axis=1) for q in range(PARTS)], axis=0
        ).astype(bf16)
        kept[j] = held
        turned = dot(held, turn[...])
        if adjoint:
            turned = -turned
        turned = turned.astype(bf16)
        dims = NN if adjoint else TN
        results.append(dot(weights[j, 0], held, dims) + dot(weights[j, 1], turned, dims))
    mixed = [
        [
            jnp.concatenate(
                [x[q * GROUPS : (q + 1) * GROUPS, 128 * h : 128 * (h + 1)] for x in results],
                axis=0,
            )
            for h in range(2)
        ]
        for q in range(PARTS)
    ]
    put_slots(mixed, carried, stage, out)


VMEM = pl.BlockSpec(memory_space=pltpu.VMEM)
SMEM = pl.BlockSpec(memory_space=pltpu.SMEM)
ANY = pl.BlockSpec(memory_space=pl.ANY)


def call(kernel, out_shape, in_specs, scratch, flops, moved, name, limit=24):
    several = isinstance(out_shape, list)
    return pl.pallas_call(
        kernel,
        out_shape=out_shape,
        in_specs=in_specs,
        out_specs=[VMEM] * len(out_shape) if several else VMEM,
        scratch_shapes=scratch,
        compiler_params=pltpu.CompilerParams(vmem_limit_bytes=limit * 2**20),
        cost_estimate=pl.CostEstimate(flops=flops, bytes_accessed=moved, transcendentals=0),
        name=name,
    )


def message(rows):
    return jax.ShapeDtypeStruct((GROUPS * rows, 128), bf16)


def stage_of(rows):
    return pltpu.VMEM((GROUPS * rows, 128), f32)


TABLE = pltpu.VMEM((STARTS[-1], LATS), bf16)
TABLE_S = pltpu.VMEM((STEPS[6], 256), bf16)


def sems(count):
    return pltpu.SemaphoreType.DMA((count,))


def in_hbm(array):
    return pltpu.with_memory_space_constraint(array, pltpu.HBM)


def spread(fields, cotangent, forward):
    cycle = pltpu.VMEM((BAND, LONS, CHANNELS), bf16)
    return call(
        spread_kernel,
        [message(SENT_ROWS), message(SLOT_ROWS), message(SLOT_ROWS)],
        [ANY, ANY, ANY],
        [
            cycle, cycle, pltpu.VMEM((LONS, COEFS), bf16),
            pltpu.VMEM((3, GROUPS * SENT_ROWS, 128), f32), sems(2 * BAND + 1),
        ],
        3 * 10**8, 4 * 10**6, "spread",
    )(in_hbm(fields), in_hbm(cotangent), in_hbm(forward))


def first(received, weighted, degrees, carried):
    return call(
        first_kernel,
        message(SENT_ROWS),
        [VMEM, VMEM, VMEM, VMEM],
        [stage_of(SENT_ROWS), stage_of(SENT_ROWS)],
        10**9, 6 * 10**6, "first",
    )(received, weighted, degrees, carried)


def middle(
    received, one, two, analysis, synthesis, degrees, inverse, inverse_t
):
    return call(
        middle_kernel,
        message(SLOT_ROWS),
        [VMEM, ANY, ANY, ANY, ANY, VMEM, ANY, ANY],
        [
            pltpu.VMEM((LONS, COEFS), bf16), pltpu.VMEM((COEFS, LONS), bf16),
            pltpu.VMEM((GROUPS, 16, 128), bf16), pltpu.VMEM((GROUPS, 32, 128), bf16),
            stage_of(16), stage_of(32), stage_of(SENT_ROWS),
            TABLE, TABLE_S, sems(4), sems(BLOCKS), sems(BLOCKS),
        ],
        3 * 10**9, 12 * 10**6, "middle",
    )(received, one, two, in_hbm(analysis), in_hbm(synthesis), degrees,
      in_hbm(inverse), in_hbm(inverse_t))


def last(received, table, degrees):
    return call(
        last_kernel,
        pltpu.HBM((GROUPS * LAST_ROWS, 128), bf16),
        [VMEM, VMEM, VMEM],
        [stage_of(SLOT_ROWS), stage_of(LAST_ROWS)],
        10**9, 7 * 10**6, "last",
    )(received, table, degrees)


def gather(received, forward, cotangent, weight_grads):
    return call(
        gather_kernel,
        jax.ShapeDtypeStruct((BAND, LONS, CHANNELS), bf16),
        [VMEM, VMEM, VMEM, ANY],
        [stage_of(LAST_ROWS)],
        3 * 10**8, 3 * 10**6, "gather",
    )(received, forward, cotangent, in_hbm(weight_grads))


def mix(adjoint, received, weights, turn, *carried):
    rows = SLOT_ROWS if adjoint else SENT_ROWS
    return call(
        functools.partial(mix_kernel, adjoint),
        [message(rows), jax.ShapeDtypeStruct((SLOTS, CHANNELS, COEFS), bf16)],
        [VMEM, VMEM, VMEM] + [VMEM] * len(carried),
        [stage_of(rows)],
        6 * 10**8, 3 * 10**6, "adjoint_mix" if adjoint else "mix",
    )(received, weights, turn, *carried)


def exchange(rows):
    count = rows.shape[0] // GROUPS
    out = lax.all_to_all(
        rows.reshape(GROUPS, count, 128), "lat", split_axis=0, concat_axis=0, tiled=True,
    )
    return out.reshape(GROUPS * count, 128)


def gradient_kernel(coeffs_source, grads_source, turn, out, coeffs, grads, sems):
    copies = []
    for j in range(SLOTS):
        copies.append(
            [
                pltpu.make_async_copy(source.at[:, j], held.at[:, j], sems.at[2 * j + n])
                for n, (source, held) in enumerate(((coeffs_source, coeffs), (grads_source, grads)))
            ]
        )
    for pair in copies:
        for copy in pair:
            copy.start()
    samples = range(coeffs.shape[0])
    for j in range(SLOTS):
        copies[j][0].wait()
        left = [coeffs[s, j] for s in samples]
        turned = [dot(x, turn[...]).astype(bf16) for x in left]
        copies[j][1].wait()
        right = jnp.concatenate([grads[s, j] for s in samples], axis=1)
        out[j, 0] = dot(jnp.concatenate(left, axis=1), right, NT).astype(bf16)
        out[j, 1] = dot(jnp.concatenate(turned, axis=1), right, NT).astype(bf16)


def weight_gradient(coeffs, grads, turn):
    held = pltpu.VMEM(coeffs.shape, bf16)
    return call(
        gradient_kernel,
        jax.ShapeDtypeStruct((SLOTS, 2, CHANNELS, CHANNELS), bf16),
        [ANY, ANY, VMEM],
        [held, held, sems(2 * SLOTS)],
        5 * 10**9, 8 * 10**6, "weight_gradient",
    )(in_hbm(coeffs), in_hbm(grads), turn)


def local(fields, cotangent, weights, degree_of):
    table = {k: jnp.asarray(v) for k, v in constants().items()}
    degrees = degree_of[None, :]
    sent, cot_two, cot_three = spread(fields[0], cotangent[0], table["forward"])
    one = exchange(sent)
    two = exchange(first(one, table["weighted"], degrees, cot_two))
    filtered, coeffs = mix(False, two, weights, table["turn"], cot_three)
    all_coeffs = lax.all_gather(coeffs, "batch", axis=0)
    three = exchange(filtered)
    as_sent = (GROUPS, SENT_ROWS, 128)
    four = exchange(
        middle(
            three, one.reshape(as_sent), two.reshape(as_sent), table["analysis"],
            table["synthesis"], degrees,
            table["inverse"], table["inverse_t"],
        )
    )
    grad_coeffs, grads = mix(True, four, weights, table["turn"])
    all_grads = lax.all_gather(grads, "batch", axis=0)
    grad_weights = weight_gradient(all_coeffs, all_grads, table["turn"])
    five = exchange(grad_coeffs)
    six = exchange(last(five, table["weighted_synthesis"], degrees))
    grad_fields = gather(six, table["forward"], cotangent[0], grad_weights)[None]
    return grad_fields, grad_weights


def solution(mesh):
    return jax.shard_map(
        local,
        mesh=mesh,
        in_specs=(
            P("batch", "lat", None, None),
            P("batch", "lat", None, None),
            P("lat", None, None, None),
            P(),
        ),
        out_specs=(P("batch", "lat", None, None), P("lat", None, None, None)),
        check_vma=False,
    )
```
